32 devices in a mesh: dp: 8 (over z, y), mp: 4 (over x, core).
Axes of the slice: x: 2, y: 2, z: 4, core: 2. Of those that a mesh axis runs over, the one named last changes fastest.
Arguments:
- image_tokens: bfloat16 [64, 128, 768], P('dp'), may hold values from -6 to 6
- image_norms: float32 [4, 768], replicated, may hold values from -1.2 to 1.6, as said below
- image_inward: bfloat16 [3, 768, 768], P(None, None, 'mp'), may hold values from -0.21875 to 0.21875
- image_biases: float32 [2, 768], P(None, 'mp'), may hold values from -1.5 to 1.5
- image_outward: bfloat16 [768, 768], P('mp'), may hold values from -0.625 to 0.625
- image_shifts: float32 [2, 768], replicated, may hold values from -1.5 to 1.5
- image_expand: bfloat16 [768, 3072], P(None, 'mp'), may hold values from -0.21875 to 0.21875
- image_offsets: float32 [3072], P('mp'), may hold values from -1.5 to 1.5
- image_contract: bfloat16 [3072, 768], P('mp'), may hold values from -0.15625 to 0.15625
- image_embed: bfloat16 [768, 512], replicated, may hold values from -0.21875 to 0.21875
- text_tokens: bfloat16 [64, 77, 512], P('dp'), may hold values from -6 to 6
- text_norms: float32 [4, 512], replicated, may hold values from -1.2 to 1.6, as said below
- text_inward: bfloat16 [3, 512, 512], P(None, None, 'mp'), may hold values from -0.25 to 0.25
- text_biases: float32 [2, 512], P(None, 'mp'), may hold values from -1.5 to 1.5
- text_outward: bfloat16 [512, 512], P('mp'), may hold values from -0.625 to 0.625
- text_shifts: float32 [2, 512], replicated, may hold values from -1.5 to 1.5
- text_expand: bfloat16 [512, 2048], P(None, 'mp'), may hold values from -0.25 to 0.25
- text_offsets: float32 [2048], P('mp'), may hold values from -1.5 to 1.5
- text_contract: bfloat16 [2048, 512], P('mp'), may hold values from -0.1875 to 0.1875
- text_embed: bfloat16 [512, 512], replicated, may hold values from -0.25 to 0.25
- post_norms: float32 [2, 1280], replicated, may hold values from -1.2 to 1.6, as said below
- logit_scale: float32 [1], replicated, may hold values from 3.2 to 4
- image_cotangent: bfloat16 [64, 128, 768], P('dp'), may hold values from -6 to 6
- text_cotangent: bfloat16 [64, 77, 512], P('dp'), may hold values from -6 to 6
- resolution: int32 [64], P('dp'), may hold values from 0 to 1, as said below
- validity: int32 [64], P('dp'), may hold values from 0 to 1, as said below
- text_ends: int32 [64], P('dp'), may hold values from 19 to 76
Outputs:
- image_result: bfloat16 [64, 128, 768], P('dp')
- text_result: bfloat16 [64, 77, 512], P('dp')
- loss_value: float32 [1], replicated
- soft_hits: float32 [1], replicated
- grad_image_tokens: float32 [64, 128, 768], P('dp')
- grad_text_tokens: float32 [64, 77, 512], P('dp')
- grad_image_norms: float32 [4, 768], replicated
- grad_image_inward: float32 [3, 768, 768], P(None, None, 'mp')
- grad_image_biases: float32 [2, 768], P(None, 'mp')
- grad_image_outward: float32 [768, 768], P('mp')
- grad_image_shifts: float32 [2, 768], replicated
- grad_image_expand: float32 [768, 3072], P(None, 'mp')
- grad_image_offsets: float32 [3072], P('mp')
- grad_image_contract: float32 [3072, 768], P('mp')
- grad_image_embed: float32 [768, 512], replicated
- grad_text_norms: float32 [4, 512], replicated
- grad_text_inward: float32 [3, 512, 512], P(None, None, 'mp')
- grad_text_biases: float32 [2, 512], P(None, 'mp')
- grad_text_outward: float32 [512, 512], P('mp')
- grad_text_shifts: float32 [2, 512], replicated
- grad_text_expand: float32 [512, 2048], P(None, 'mp')
- grad_text_offsets: float32 [2048], P('mp')
- grad_text_contract: float32 [2048, 512], P('mp')
- grad_text_embed: float32 [512, 512], replicated
- grad_post_norms: float32 [2, 1280], replicated
- grad_logit_scale: float32 [1], replicated
The draws below stay inside these ranges and needn't reach their ends.
Inputs may be any that keep to these rules, and one draw needn't show every extreme that they name: `resolution`: 1 marks a 336px image with 101 live rows, 0 a 224px image with 50; the first 8 examples are all 1, the last 8 all 0, the others drawn independently. `validity`: 1 marks an example that enters the loss and the counts; the first example is 0 and the last is 1. `image_norms`: rows 0 and 2 are gains and rows 1 and 3 shifts. `text_norms`: rows 0 and 2 are gains and rows 1 and 3 shifts. `post_norms`: row 0 holds gains and row 1 shifts; the first 768 columns belong to the image tower, the last 512 to the text tower.
All inputs are finite; a program needn't handle non-finite values.
Results may differ from the reference program's by a relative error of at most 0.015.
Values sent between devices are 32-bit elements; how exact they have to be, the bound alone decides.
A program may use at most 128 MiB of HBM per device.

```python
import jax
import jax.numpy as jnp
from jax import lax

HEAD = 64
F_IMG = 3072
F_TXT = 2048
EMBED = 512
CTX = 77
LOW_LEN = 50
HIGH_LEN = 101
PATCH = 128
EX_DEV = 8
D_IMG = 768
D_TXT = 512
EXAMPLES = 64


def norm_rows(base_key, count, width):
    noise = jnp.clip(jax.random.normal(base_key, (count, width), jnp.float32), -4.0, 4.0)
    even_rows = (jnp.arange(count) % 2 == 0)[:, None]
    return jnp.where(even_rows, 1.0 + 0.15 * noise, 0.3 * noise)


def draw_image_norms(key, part):
    key = jax.random.fold_in(key, 1)
    return norm_rows(key, 4, D_IMG)


def draw_text_norms(key, part):
    key = jax.random.fold_in(key, 2)
    return norm_rows(key, 4, D_TXT)


def draw_post_norms(key, part):
    key = jax.random.fold_in(key, 5)
    return norm_rows(key, 2, D_IMG + D_TXT)


def draw_resolution(key, part):
    key = jax.random.fold_in(key, 3)
    positions = jnp.arange(EXAMPLES, dtype=jnp.int32)
    coins = jax.random.randint(jax.random.fold_in(key, 11), (EXAMPLES,), 0, 2, dtype=jnp.int32)
    coins = jnp.where(positions < EX_DEV, 1, coins)
    coins = jnp.where(positions >= EXAMPLES - EX_DEV, 0, coins)
    return coins.astype(jnp.int32)


def draw_validity(key, part):
    key = jax.random.fold_in(key, 4)
    positions = jnp.arange(EXAMPLES, dtype=jnp.int32)
    numbers = jax.random.randint(key, (EXAMPLES,), 0, 3 * EXAMPLES - 1)
    valid_marks = (numbers < EXAMPLES + 2 * positions + 1).astype(jnp.int32)
    return valid_marks.at[0].set(0)


def with_ends(entries, own_key, low, largest):
    longest = entries.shape.index(max(entries.shape))
    spots = []
    for shift in (0, 1):
        where = [jax.random.randint(jax.random.fold_in(own_key, axis), (), 0, length) for axis, length in enumerate(entries.shape)]
        where[longest] = (where[longest] + shift) % entries.shape[longest]
        spots.append(tuple(where))
    return entries.at[spots[0]].set(low).at[spots[1]].set(largest)


def levels(stream_key, shape, split, smallest, largest):
    gain, own = 1.0, jax.random.fold_in(stream_key, 6)
    for dim, parts in split:
        heights = jnp.exp(jax.random.uniform(jax.random.fold_in(own, dim), (parts,), jnp.float32, smallest / len(split), largest / len(split)))
        gain = gain * jnp.repeat(heights, shape[dim] // parts).reshape([-1 if axis == dim else 1 for axis in range(len(shape))])
    return gain


def bell_draw(key, extent, scale, most, pieces=(), kind=jnp.bfloat16):
    values = scale * jax.random.normal(key, extent, jnp.float32)
    if pieces:
        values = values * levels(key, extent, pieces, -0.22, 0.18)
    return jnp.clip(values, -most, most).astype(kind)


def setup_inputs(seed: int = 0) -> dict:
    seeds = jax.random.split(jax.random.key(seed), 28)
    return {
        "image_tokens": bell_draw(seeds[0], (EXAMPLES, PATCH, D_IMG), 1.0, 6.0, ((0, 8),)),
        "image_norms": draw_image_norms(jax.random.fold_in(seeds[27], 71), 0),
        "image_inward": bell_draw(seeds[2], (3, D_IMG, D_IMG), D_IMG ** -0.5, 0.21875, ((2, 4),)),
        "image_biases": bell_draw(seeds[3], (2, D_IMG), 0.3, 1.5, ((1, 4),), jnp.float32),
        "image_outward": bell_draw(seeds[4], (D_IMG, D_IMG), (D_IMG // 8) ** -0.5, 0.625, ((0, 4),)),
        "image_shifts": bell_draw(seeds[5], (2, D_IMG), 0.3, 1.5, (), jnp.float32),
        "image_expand": bell_draw(seeds[6], (D_IMG, F_IMG), D_IMG ** -0.5, 0.21875, ((1, 4),)),
        "image_offsets": bell_draw(seeds[7], (F_IMG,), 0.3, 1.5, ((0, 4),), jnp.float32),
        "image_contract": bell_draw(seeds[8], (F_IMG, D_IMG), (F_IMG // 2) ** -0.5, 0.15625, ((0, 4),)),
        "image_embed": bell_draw(seeds[9], (D_IMG, EMBED), D_IMG ** -0.5, 0.21875),
        "text_tokens": bell_draw(seeds[10], (EXAMPLES, CTX, D_TXT), 1.0, 6.0, ((0, 8),)),
        "text_norms": draw_text_norms(jax.random.fold_in(seeds[27], 71), 0),
        "text_inward": bell_draw(seeds[12], (3, D_TXT, D_TXT), D_TXT ** -0.5, 0.25, ((2, 4),)),
        "text_biases": bell_draw(seeds[13], (2, D_TXT), 0.3, 1.5, ((1, 4),), jnp.float32),
        "text_outward": bell_draw(seeds[14], (D_TXT, D_TXT), (D_TXT // 6) ** -0.5, 0.625, ((0, 4),)),
        "text_shifts": bell_draw(seeds[15], (2, D_TXT), 0.3, 1.5, (), jnp.float32),
        "text_expand": bell_draw(seeds[16], (D_TXT, F_TXT), D_TXT ** -0.5, 0.25, ((1, 4),)),
        "text_offsets": bell_draw(seeds[17], (F_TXT,), 0.3, 1.5, ((0, 4),), jnp.float32),
        "text_contract": bell_draw(seeds[18], (F_TXT, D_TXT), (F_TXT // 2) ** -0.5, 0.1875, ((0, 4),)),
        "text_embed": bell_draw(seeds[19], (D_TXT, EMBED), D_TXT ** -0.5, 0.25),
        "post_norms": draw_post_norms(jax.random.fold_in(seeds[27], 71), 0),
        "logit_scale": jnp.clip(jax.random.uniform(seeds[21], (1,), jnp.float32, 3.2, 4.0), 3.2, 4.0),
        "image_cotangent": bell_draw(seeds[22], (EXAMPLES, PATCH, D_IMG), 1.0, 6.0, ((0, 8),)),
        "text_cotangent": bell_draw(seeds[23], (EXAMPLES, CTX, D_TXT), 1.0, 6.0, ((0, 8),)),
        "resolution": draw_resolution(jax.random.fold_in(seeds[27], 71), 0),
        "validity": draw_validity(jax.random.fold_in(seeds[27], 71), 0),
        "text_ends": with_ends(jax.random.randint(seeds[26], (EXAMPLES,), CTX // 4, CTX), jax.random.fold_in(seeds[26], 1), CTX // 4, CTX - 1).astype(jnp.int32),
    }


@jax.custom_vjp
def low(v):
    return lax.optimization_barrier(v.astype(jnp.bfloat16)).astype(jnp.float32)

@jax.custom_vjp
def low_back(v):
    return v

def low_keep(v):
    return (low(v), None)

def low_pass(kept, grad):
    return (grad,)

def back_keep(v):
    return (v, None)

def back_low(kept, grad):
    return (low(grad),)
low.defvjp(low_keep, low_pass)
low_back.defvjp(back_keep, back_low)
EPSILON = 1e-05
MASKED = -1000000000.0
HIGHEST = lax.Precision.HIGHEST

def layer_norm(values, gain_vec, shift_vec):
    centre = lax.optimization_barrier(jnp.mean(values, axis=-1, keepdims=True))
    centred = values - centre
    spread = lax.optimization_barrier(jnp.mean(centred * centred, axis=-1, keepdims=True))
    return centred * lax.rsqrt(spread + EPSILON) * gain_vec + shift_vec

def quick_gelu(values):
    return values * jax.nn.sigmoid(1.702 * values)

def unit_rows(values):
    return values * lax.rsqrt(lax.optimization_barrier(jnp.sum(values * values, axis=-1, keepdims=True)) + 1e-06)

def project(left_side, right_side):
    return jnp.einsum('btd,de->bte', left_side, right_side, precision=HIGHEST)

def by_heads(values):
    return values.reshape(values.shape[0], values.shape[1], values.shape[2] // HEAD, HEAD)

def tower(tokens, norms, inward, biases, outward, shifts, expand, offsets, contract, mask):
    factor = HEAD ** (-0.5)
    normed = low(layer_norm(tokens, norms[0], norms[1]))
    query_heads = by_heads(low(low_back(project(normed, inward[0])) + biases[0]))
    key_heads = by_heads(low(low_back(project(normed, inward[1]))))
    value_heads = by_heads(low(low_back(project(normed, inward[2])) + biases[1]))
    scores = low_back(jnp.einsum('bqhd,bkhd->bhqk', query_heads, key_heads, precision=HIGHEST) * factor)
    scores = jnp.where(mask[:, None], scores, MASKED)
    weights = jax.nn.softmax(scores, axis=-1)
    mixed_heads = low(low_back(jnp.einsum('bhqk,bkhd->bqhd', low(weights), value_heads, precision=HIGHEST)))
    merged = mixed_heads.reshape(tokens.shape[0], tokens.shape[1], -1)
    resid_sum = tokens + low_back(project(merged, outward)) + shifts[0]
    normed_two = low(layer_norm(resid_sum, norms[2], norms[3]))
    hidden = low_back(project(normed_two, expand)) + offsets
    active = low(low_back(quick_gelu(hidden)))
    return resid_sum + low_back(project(active, contract)) + shifts[1]

def embed_of(final, pick_rows, gain_vec, shift_vec, embed):
    chosen = lax.optimization_barrier(jnp.sum(final * pick_rows[..., None], axis=1))
    normed = low(layer_norm(chosen, gain_vec, shift_vec))
    return unit_rows(low_back(jnp.dot(normed, embed, precision=HIGHEST)))

def contrastive(image_rows, text_rows, valid_rows, logit_scale):
    factor = jnp.exp(logit_scale[0])
    logits = factor * jnp.dot(image_rows, text_rows.T, precision=HIGHEST)
    usable = valid_rows > 0.5
    row_lse = jax.nn.logsumexp(jnp.where(usable[None, :], logits, MASKED), axis=1)
    col_lse = jax.nn.logsumexp(jnp.where(usable[:, None], logits, MASKED), axis=0)
    diagonal = factor * lax.optimization_barrier(jnp.sum(image_rows * text_rows, axis=1))
    total = jnp.sum(valid_rows)
    loss_value = jnp.sum(valid_rows * (row_lse + col_lse - 2.0 * diagonal)) / (2.0 * total)
    soft_hits = jnp.sum(valid_rows * jnp.exp(diagonal - row_lse))
    return (loss_value.reshape(1), soft_hits.reshape(1))

def reference(image_tokens, image_norms, image_inward, image_biases, image_outward, image_shifts, image_expand, image_offsets, image_contract, image_embed, text_tokens, text_norms, text_inward, text_biases, text_outward, text_shifts, text_expand, text_offsets, text_contract, text_embed, post_norms, logit_scale, image_cotangent, text_cotangent, resolution, validity, text_ends):
    length = jnp.where(resolution == 1, HIGH_LEN, LOW_LEN).astype(jnp.int32)
    places = jnp.arange(PATCH, dtype=jnp.int32)
    live_rows = (places[None, :] < length[:, None]).astype(jnp.float32)
    image_mask = places[None, None, :] < length[:, None, None]
    positions = jnp.arange(CTX, dtype=jnp.int32)
    text_mask = (positions[None, :] <= positions[:, None])[None]
    image_pick = jnp.broadcast_to((places == 0).astype(jnp.float32)[None, :], live_rows.shape)
    text_pick = (positions[None, :] == text_ends.astype(jnp.int32)[:, None]).astype(jnp.float32)
    valid_rows = validity.astype(jnp.float32)
    inputs = tuple((member.astype(jnp.float32) for member in (image_tokens, image_norms, image_inward, image_biases, image_outward, image_shifts, image_expand, image_offsets, image_contract, image_embed, text_tokens, text_norms, text_inward, text_biases, text_outward, text_shifts, text_expand, text_offsets, text_contract, text_embed, post_norms, logit_scale)))

    def forward(*params):
        image_final = tower(params[0], params[1], params[2], params[3], params[4], params[5], params[6], params[7], params[8], image_mask)
        text_final = tower(params[10], params[11], params[12], params[13], params[14], params[15], params[16], params[17], params[18], text_mask)
        finals = params[20]
        image_rows = embed_of(image_final, image_pick, finals[0, :D_IMG], finals[1, :D_IMG], params[9])
        text_rows = embed_of(text_final, text_pick, finals[0, D_IMG:], finals[1, D_IMG:], params[19])
        loss_value, soft_hits = contrastive(image_rows, text_rows, valid_rows, params[21])
        return (image_final * live_rows[..., None], text_final, loss_value, soft_hits)
    outputs, pull_back = jax.vjp(forward, *inputs)
    gradients = pull_back((image_cotangent.astype(jnp.float32), text_cotangent.astype(jnp.float32), jnp.ones((1,), jnp.float32), jnp.zeros((1,), jnp.float32)))
    return (outputs[0].astype(jnp.bfloat16), outputs[1].astype(jnp.bfloat16), outputs[2], outputs[3], gradients[0], gradients[10], gradients[1], gradients[2], gradients[3], gradients[4], gradients[5], gradients[6], gradients[7], gradients[8], gradients[9], gradients[11], gradients[12], gradients[13], gradients[14], gradients[15], gradients[16], gradients[17], gradients[18], gradients[19], gradients[20], gradients[21])
```

```python
import functools

import jax
import jax.numpy as jnp
from jax import lax
from jax.experimental import pallas as pl
from jax.experimental.pallas import tpu as pltpu
from jax.sharding import PartitionSpec as P

MESH = pl.DeviceIdType.MESH
HEAD = 64
LOW_LEN = 50
HIGH_LEN = 101
IMG_ROWS = 104
TXT_ROWS = 80
SPAN = 256
SLOTS = 4
LANES = 256

EPSILON = 1e-05
MASKED = -1000000000.0
HIGHEST = lax.Precision.HIGHEST


def layer_norm(values, gain_vec, shift_vec):
    centre = jnp.mean(values, axis=-1, keepdims=True)
    centred = values - centre
    spread = jnp.mean(centred * centred, axis=-1, keepdims=True)
    return centred * lax.rsqrt(spread + EPSILON) * gain_vec + shift_vec


def quick_gelu(values):
    return values * jax.nn.sigmoid(1.702 * values)


def unit_rows(values):
    return values * lax.rsqrt(jnp.sum(values * values, axis=-1, keepdims=True) + 1e-06)


def to_low(values):
    return values.astype(jnp.bfloat16)


def norm_back(values, gain_vec, shift_vec, gradient):
    _, pull_back = jax.vjp(layer_norm, values, gain_vec, shift_vec)
    return pull_back(gradient)


def project(left_side, right_side):
    return jnp.einsum("btd,de->bte", left_side, right_side, preferred_element_type=jnp.float32)


def project_back(left_side, right_side):
    return jnp.einsum("bte,de->btd", left_side, right_side, preferred_element_type=jnp.float32)


def outer_rows(left_side, right_side):
    return jnp.einsum("btd,bte->de", left_side, right_side, preferred_element_type=jnp.float32)


def by_heads(values):
    return values.reshape(values.shape[0], values.shape[1], values.shape[2] // HEAD, HEAD)


def merge_heads(values):
    return values.reshape(values.shape[0], values.shape[1], values.shape[2] * values.shape[3])


def greet(peers):
    barrier = pltpu.get_barrier_semaphore()
    for peer in peers:
        pl.semaphore_signal(barrier, inc=1, device_id=peer, device_id_type=MESH)
    pl.semaphore_wait(barrier, len(peers))


def mp_peers(dp, mp):
    core = mp + 1 - 2 * lax.rem(mp, 2)
    across = lax.rem(mp + 2, 4)
    return (dp, core), (dp, across)


def mp_sum_kernel(sizes, *refs):
    k = len(sizes)
    parts, outs = refs[:k], refs[k : 2 * k]
    core_bufs, across_bufs = refs[2 * k : 3 * k], refs[3 * k : 4 * k]
    sends, recvs = refs[4 * k :]
    dp, mp = lax.axis_index("dp"), lax.axis_index("mp")
    core, across = mp_peers(dp, mp)
    diag = lax.rem(core[1] + 2, 4)
    greet((core, across))

    def copy(src, dst, sem, peer):
        return pltpu.make_async_remote_copy(
            src_ref=src,
            dst_ref=dst,
            send_sem=sends.at[sem],
            recv_sem=recvs.at[sem],
            device_id=peer,
            device_id_type=MESH,
        )

    def rows(ref, owner, size):
        return ref.at[pl.ds(pl.multiple_of(owner * size, size), size)]

    first = []
    for i, size in enumerate(sizes):
        far = copy(rows(parts[i], diag, size), core_bufs[i].at[0], 6 * i, core)
        near = copy(rows(parts[i], core[1], size), core_bufs[i].at[1], 6 * i + 1, core)
        far.start()
        near.start()
        first.append((far, near))
    second = []
    for i, size in enumerate(sizes):
        far, near = first[i]
        far.wait()
        mine = rows(parts[i], across[1], size)
        core_bufs[i][0] = core_bufs[i][0] + mine[...]
        over = copy(core_bufs[i].at[0], across_bufs[i], 6 * i + 2, across)
        over.start()
        second.append(over)
    third = []
    for i, size in enumerate(sizes):
        far, near = first[i]
        near.wait()
        core_bufs[i][1] = core_bufs[i][1] + rows(parts[i], mp, size)[...]
        second[i].wait()
        home = rows(outs[i], mp, size)
        home[...] = core_bufs[i][1] + across_bufs[i][...]
        one = copy(home, home, 6 * i + 3, across)
        two = copy(home, home, 6 * i + 4, core)
        one.start()
        two.start()
        third.append((one, two))
    last = []
    for i, size in enumerate(sizes):
        one, two = third[i]
        one.wait_recv()
        got = rows(outs[i], across[1], size)
        on = copy(got, got, 6 * i + 5, core)
        on.start()
        last.append(on)
    for i, size in enumerate(sizes):
        one, two = third[i]
        one.wait_send()
        two.wait()
        last[i].wait()


def mp_sum(parts, collective_id):
    sizes = [part.shape[0] // 4 for part in parts]
    scratch = [pltpu.VMEM((2, s, p.shape[1]), jnp.float32) for s, p in zip(sizes, parts)]
    scratch += [pltpu.VMEM((s, p.shape[1]), jnp.float32) for s, p in zip(sizes, parts)]
    scratch += [pltpu.SemaphoreType.DMA((6 * len(parts),))] * 2
    return pl.pallas_call(
        functools.partial(mp_sum_kernel, sizes),
        out_shape=[jax.ShapeDtypeStruct(p.shape, jnp.float32) for p in parts],
        in_specs=[pl.BlockSpec(memory_space=pltpu.VMEM)] * len(parts),
        out_specs=[pl.BlockSpec(memory_space=pltpu.VMEM)] * len(parts),
        scratch_shapes=scratch,
        compiler_params=pltpu.CompilerParams(
            collective_id=collective_id, has_side_effects=True, vmem_limit_bytes=40 << 20
        ),
        name="mp_sum",
    )(*parts)


def dp_sum_machine(count, blocks, total, rings, sends, recvs, credits):
    places = count // 2
    deep = places // 2
    dp, mp = lax.axis_index("dp"), lax.axis_index("mp")
    side, place = lax.rem(dp, 2), dp // 2
    low = place < deep
    depth = jnp.where(low, place, places - 1 - place)
    inner = jnp.where(low, place + 1, place - 1)
    outer = jnp.clip(jnp.where(low, place - 1, place + 1), 0, places - 1)
    half = jnp.where(low, 0, 1)
    pair_id = (place * 2 + 1 - side, mp)
    inner_id = (inner * 2 + side, mp)
    outer_id = (outer * 2 + side, mp)
    quarter = SPAN // 4

    def part(offset, size):
        def at(block):
            start = pl.multiple_of(block * SPAN + offset, quarter)
            return total.at[pl.ds(start, size)]

        return at

    kept = part(side * quarter, quarter)
    given = part((1 - side) * quarter, quarter)
    whole = part(2 * quarter, 2 * quarter)
    mid_kept = part((2 + half) * quarter, quarter)
    mid_given = part((3 - half) * quarter, quarter)
    middle = depth == deep - 1
    not_middle = depth < deep - 1
    not_end = depth > 0
    yes = depth >= 0

    kinds = [
        (yes, 0, given, pair_id, yes, 0, pair_id, rings[0], kept),
        (not_middle, depth, whole, inner_id, not_end, depth - 1, outer_id, rings[1], whole),
        (not_middle, depth + 1, kept, inner_id, not_end, depth, outer_id, rings[2], kept),
        (middle, deep - 1, mid_given, inner_id, middle, deep - 1, inner_id, rings[3], mid_kept),
        (middle, deep, mid_kept, pair_id, middle, deep, pair_id, rings[4], mid_kept),
        (middle, deep, kept, inner_id, middle, deep, inner_id, rings[5], kept),
        (middle, deep + 1, mid_kept, inner_id, middle, deep + 1, inner_id, None, mid_given),
        (not_end, 2 * deep - depth, kept, outer_id, not_middle, 2 * deep - depth - 1, inner_id, None, kept),
        (not_end, 2 * deep + 1 - depth, whole, outer_id, not_middle, 2 * deep - depth, inner_id, None, whole),
        (yes, 2 * deep, kept, pair_id, yes, 2 * deep, pair_id, None, given),
    ]

    def copy(k, kind, block):
        _, _, src, target, _, _, _, ring, land = kind
        slot = lax.rem(block, SLOTS)
        dst = src(block) if ring is None else ring.at[slot]
        return pltpu.make_async_remote_copy(
            src_ref=src(block),
            dst_ref=dst,
            send_sem=sends.at[k, slot],
            recv_sem=recvs.at[k, slot],
            device_id=target,
            device_id_type=MESH,
        )

    def valid(block):
        return jnp.logical_and(block >= 0, block < blocks)

    def start(t):
        for k, kind in enumerate(kinds):
            block = t - 2 * kind[1]

            @pl.when(jnp.logical_and(kind[0], valid(block)))
            def _():
                @pl.when(block >= SLOTS)
                def _():
                    pl.semaphore_wait(credits.at[k], 1)

                copy(k, kind, block).start()

    def finish(t):
        for k, kind in enumerate(kinds):
            sends_it, sent_stage, _, _, takes_it, got_stage, source, ring, land = kind
            sent = t - 2 * sent_stage
            got = t - 2 * got_stage

            @pl.when(jnp.logical_and(sends_it, valid(sent)))
            def _():
                copy(k, kind, sent).wait_send()

            @pl.when(jnp.logical_and(takes_it, valid(got)))
            def _():
                copy(k, kind, got).wait_recv()
                if ring is not None:
                    here = land(got)
                    here[...] = here[...] + ring[lax.rem(got, SLOTS)]

                @pl.when(got < blocks - SLOTS)
                def _():
                    pl.semaphore_signal(credits.at[k], inc=1, device_id=source, device_id_type=MESH)

    def tick(t):
        start(t)

        @pl.when(t > 0)
        def _():
            finish(t - 1)

    return tick, blocks + 4 * deep + 1


def dp_peers(count):
    places = count // 2
    deep = places // 2
    dp, mp = lax.axis_index("dp"), lax.axis_index("mp")
    side, place = lax.rem(dp, 2), dp // 2
    low = place < deep
    inner = jnp.where(low, place + 1, place - 1)
    outer = jnp.clip(jnp.where(low, place - 1, place + 1), 0, places - 1)
    at_end = jnp.logical_or(place == 0, place == places - 1)
    return (place * 2 + 1 - side, mp), (inner * 2 + side, mp), (outer * 2 + side, mp), at_end


def dp_rings():
    quarter = SPAN // 4
    sizes = [quarter, 2 * quarter, quarter, quarter, quarter, quarter]
    return [pltpu.VMEM((SLOTS, size, LANES), jnp.float32) for size in sizes] + [
        pltpu.SemaphoreType.DMA((10, SLOTS)),
        pltpu.SemaphoreType.DMA((10, SLOTS)),
        pltpu.SemaphoreType.REGULAR((10,)),
    ]


def dp_sum_kernel(count, blocks, given, total, *scratch):
    rings, (sends, recvs, credits, sem) = scratch[:6], scratch[6:]
    load = pltpu.make_async_copy(given, total, sem)
    load.start()
    pair_id, inner_id, outer_id, at_end = dp_peers(count)
    barrier = pltpu.get_barrier_semaphore()
    for peer in (pair_id, inner_id):
        pl.semaphore_signal(barrier, inc=1, device_id=peer, device_id_type=MESH)

    @pl.when(jnp.logical_not(at_end))
    def _():
        pl.semaphore_signal(barrier, inc=1, device_id=outer_id, device_id_type=MESH)
        pl.semaphore_wait(barrier, 3)

    @pl.when(at_end)
    def _():
        pl.semaphore_wait(barrier, 2)

    load.wait()
    tick, ticks = dp_sum_machine(count, blocks, total, rings, sends, recvs, credits)

    def step(t, carry):
        tick(t)
        return carry

    lax.fori_loop(0, ticks, step, 0)


def dp_sum(count, total, collective_id):
    blocks = total.shape[0] // SPAN
    return pl.pallas_call(
        functools.partial(dp_sum_kernel, count, blocks),
        out_shape=jax.ShapeDtypeStruct(total.shape, jnp.float32),
        in_specs=[pl.BlockSpec(memory_space=pl.ANY)],
        out_specs=pl.BlockSpec(memory_space=pltpu.VMEM),
        scratch_shapes=dp_rings() + [pltpu.SemaphoreType.DMA],
        compiler_params=pltpu.CompilerParams(
            collective_id=collective_id, has_side_effects=True, vmem_limit_bytes=40 << 20
        ),
        name="dp_sum",
    )(total)


def attention_scores(query_heads, key_heads, mask):
    factor = HEAD ** (-0.5)
    scores = (
        jnp.einsum("bqhd,bkhd->bhqk", query_heads, key_heads, preferred_element_type=jnp.float32)
        * factor
    )
    return jnp.where(mask[:, None], scores, MASKED)


def attention_front(tokens, norms, inward, biases, outward, mask):
    values = tokens.astype(jnp.float32)
    normed = to_low(layer_norm(values, norms[0], norms[1]))
    query_heads = by_heads(to_low(project(normed, inward[0]) + biases[0]))
    key_heads = by_heads(to_low(project(normed, inward[1])))
    value_heads = by_heads(to_low(project(normed, inward[2]) + biases[1]))
    scores = attention_scores(query_heads, key_heads, mask)
    totals = jax.nn.logsumexp(scores, axis=-1, keepdims=True)
    weights = jnp.exp(scores - totals)
    mixed = merge_heads(
        to_low(
            jnp.einsum(
                "bhqk,bkhd->bqhd", to_low(weights), value_heads, preferred_element_type=jnp.float32
            )
        )
    )
    stored = {
        "values": values,
        "normed": normed,
        "query": query_heads,
        "keys": key_heads,
        "vals": value_heads,
        "totals": totals,
        "mixed": mixed,
    }
    return (project(mixed, outward), stored)


def feed_front(stored, attended, norms, shifts, expand, offsets, contract):
    resid_sum = stored["values"] + attended + shifts[0]
    normed = to_low(layer_norm(resid_sum, norms[2], norms[3]))
    hidden = project(normed, expand) + offsets
    active = to_low(quick_gelu(hidden))
    return (
        project(active, contract),
        {"resid": resid_sum, "normed": normed, "hidden": hidden, "active": active},
    )


def head_front(chosen, gain_vec, shift_vec, embed):
    normed = to_low(layer_norm(chosen, gain_vec, shift_vec))
    raw_rows = jnp.dot(normed, embed, preferred_element_type=jnp.float32)
    return (unit_rows(raw_rows), (chosen, normed, raw_rows))


def head_back(retained, gain_vec, shift_vec, embed, gradient):
    chosen, normed, raw_rows = retained
    _, pull_back = jax.vjp(unit_rows, raw_rows)
    raw_grad = to_low(pull_back(gradient)[0])
    embed_grad = jnp.einsum("bd,be->de", normed, raw_grad, preferred_element_type=jnp.float32)
    normed_grad = jnp.einsum("be,de->bd", raw_grad, embed, preferred_element_type=jnp.float32)
    chosen_grad, gain_grad, shift_grad = norm_back(chosen, gain_vec, shift_vec, normed_grad)
    return (chosen_grad, embed_grad, gain_grad, shift_grad)


def feed_back(gradient, retained, expand, contract):
    grad_low = to_low(gradient)
    shift_grad = jnp.sum(gradient, axis=(0, 1))
    contract_grad = outer_rows(retained["active"], grad_low)
    active_grad = to_low(project_back(grad_low, contract)).astype(jnp.float32)
    _, pull_back = jax.vjp(quick_gelu, retained["hidden"])
    hidden_grad = pull_back(active_grad)[0]
    offset_grad = jnp.sum(hidden_grad, axis=(0, 1))
    hidden_low = to_low(hidden_grad)
    expand_grad = outer_rows(retained["normed"], hidden_low)
    normed_grad = project_back(hidden_low, expand)
    return (normed_grad, expand_grad, offset_grad, contract_grad, shift_grad)


def attention_back(gradient, stored, mask, inward, outward):
    factor = HEAD ** (-0.5)
    grad_low = to_low(gradient)
    shift_grad = jnp.sum(gradient, axis=(0, 1))
    outward_grad = outer_rows(stored["mixed"], grad_low)
    mixed_grad = by_heads(to_low(project_back(grad_low, outward)))
    weights = jnp.exp(attention_scores(stored["query"], stored["keys"], mask) - stored["totals"])
    weight_grad = jnp.einsum(
        "bqhd,bkhd->bhqk", mixed_grad, stored["vals"], preferred_element_type=jnp.float32
    )
    value_grad = merge_heads(
        jnp.einsum(
            "bhqk,bqhd->bkhd", to_low(weights), mixed_grad, preferred_element_type=jnp.float32
        )
    )
    score_grad = to_low(
        weights * (weight_grad - jnp.sum(weight_grad * weights, axis=-1, keepdims=True))
    )
    query_grad = merge_heads(
        jnp.einsum(
            "bhqk,bkhd->bqhd", score_grad, stored["keys"], preferred_element_type=jnp.float32
        )
        * factor
    )
    key_grad = merge_heads(
        jnp.einsum(
            "bhqk,bqhd->bkhd", score_grad, stored["query"], preferred_element_type=jnp.float32
        )
        * factor
    )
    bias_grad = jnp.stack([jnp.sum(query_grad, axis=(0, 1)), jnp.sum(value_grad, axis=(0, 1))])
    query_low = to_low(query_grad)
    key_low = to_low(key_grad)
    value_low = to_low(value_grad)
    inward_grad = jnp.concatenate(
        [
            outer_rows(query_low, stored["normed"]),
            outer_rows(key_low, stored["normed"]),
            outer_rows(value_low, stored["normed"]),
        ],
        axis=0,
    )
    normed_grad = (
        project_back(query_low, inward[0])
        + project_back(key_low, inward[1])
        + project_back(value_low, inward[2])
    )
    return (normed_grad, inward_grad, bias_grad, outward_grad, shift_grad)


def contrastive(every_image, every_text, every_valid, logit_scale):
    factor = jnp.exp(logit_scale[0])
    total = jnp.sum(every_valid)
    weight = 1.0 / (2.0 * total)
    usable = every_valid > 0.5
    all_logits = factor * jnp.dot(every_image, every_text.T, precision=HIGHEST)
    row_masked = jnp.where(usable[None, :], all_logits, MASKED)
    col_masked = jnp.where(usable[:, None], all_logits, MASKED)
    row_lse = jax.nn.logsumexp(row_masked, axis=1)
    col_lse = jax.nn.logsumexp(col_masked, axis=0)
    diagonal = factor * jnp.sum(every_image * every_text, axis=1)
    loss_value = jnp.sum(every_valid * (row_lse + col_lse - 2.0 * diagonal)) / (2.0 * total)
    hit_sum = jnp.sum(every_valid * jnp.exp(diagonal - row_lse))
    identity = (
        jnp.arange(every_valid.shape[0])[None, :] == jnp.arange(every_valid.shape[0])[:, None]
    ).astype(jnp.float32)
    pair_grad = weight * (
        every_valid[:, None] * (jnp.exp(row_masked - row_lse[:, None]) - identity)
        + every_valid[None, :] * (jnp.exp(col_masked - col_lse[None, :]) - identity)
    )
    scale_grad = jnp.sum(pair_grad * all_logits)
    image_grad = factor * jnp.dot(pair_grad, every_text, precision=HIGHEST)
    text_grad = factor * jnp.dot(pair_grad.T, every_image, precision=HIGHEST)
    return (loss_value, hit_sum, image_grad, text_grad, scale_grad)


def panels(values):
    rows, columns = values.shape
    return jnp.swapaxes(values.reshape(rows, columns // LANES, LANES), 0, 1).reshape(-1, LANES)


def unpanel(values, columns):
    count = columns // LANES
    return jnp.swapaxes(values.reshape(count, -1, LANES), 0, 1).reshape(-1, columns)


def shards(
    count,
    image_tokens,
    image_norms,
    image_inward,
    image_biases,
    image_outward,
    image_shifts,
    image_expand,
    image_offsets,
    image_contract,
    image_embed,
    text_tokens,
    text_norms,
    text_inward,
    text_biases,
    text_outward,
    text_shifts,
    text_expand,
    text_offsets,
    text_contract,
    text_embed,
    post_norms,
    logit_scale,
    image_cotangent,
    text_cotangent,
    resolution,
    validity,
    text_ends,
):
    examples, patch, image_width = image_tokens.shape
    context, text_width = text_tokens.shape[1:]
    image_tokens = image_tokens[:, :IMG_ROWS]
    image_cotangent = image_cotangent[:, :IMG_ROWS]
    grow = ((0, 0), (0, TXT_ROWS - context), (0, 0))
    text_tokens = jnp.pad(text_tokens, grow)
    text_cotangent = jnp.pad(text_cotangent, grow)

    length = jnp.where(resolution == 1, HIGH_LEN, LOW_LEN).astype(jnp.int32)
    places = jnp.arange(IMG_ROWS, dtype=jnp.int32)
    live_rows = (places[None, :] < length[:, None]).astype(jnp.float32)
    image_mask = places[None, None, :] < length[:, None, None]
    image_pick = jnp.broadcast_to((places == 0).astype(jnp.float32)[None, :], live_rows.shape)
    positions = jnp.arange(TXT_ROWS, dtype=jnp.int32)
    text_mask = (positions[None, :] <= positions[:, None])[None]
    text_pick = (positions[None, :] == text_ends[:, None]).astype(jnp.float32)
    image_post = post_norms[:, :image_width]
    text_post = post_norms[:, image_width:]

    def over_mp(image_part, text_part, collective_id):
        image_sum, text_sum = mp_sum(
            [image_part.reshape(-1, image_width), text_part.reshape(-1, text_width)], collective_id
        )
        return image_sum.reshape(image_part.shape), text_sum.reshape(text_part.shape)

    image_part, image_stored = attention_front(
        image_tokens, image_norms, image_inward, image_biases, image_outward, image_mask
    )
    text_part, text_stored = attention_front(
        text_tokens, text_norms, text_inward, text_biases, text_outward, text_mask
    )
    image_attn, text_attn = over_mp(image_part, text_part, 0)
    image_fpart, image_kept = feed_front(
        image_stored,
        image_attn,
        image_norms,
        image_shifts,
        image_expand,
        image_offsets,
        image_contract,
    )
    text_fpart, text_kept = feed_front(
        text_stored, text_attn, text_norms, text_shifts, text_expand, text_offsets, text_contract
    )
    image_feed, text_feed = over_mp(image_fpart, text_fpart, 0)
    image_final = image_kept["resid"] + image_feed + image_shifts[1]
    text_final = text_kept["resid"] + text_feed + text_shifts[1]

    image_chosen = image_final[:, 0]
    text_chosen = jnp.sum(text_final * text_pick[..., None], axis=1)
    valid_rows = validity.astype(jnp.float32)
    mine = jnp.concatenate(
        [image_chosen, text_chosen, jnp.broadcast_to(valid_rows[:, None], (examples, 128))], axis=1
    )
    every = lax.all_gather(mine, "dp", axis=0, tiled=True)
    every_image = every[:, :image_width]
    every_text = every[:, image_width : image_width + text_width]
    every_valid = every[:, -1]
    image_rows, image_head = head_front(every_image, image_post[0], image_post[1], image_embed)
    text_rows, text_head = head_front(every_text, text_post[0], text_post[1], text_embed)
    loss_value, hit_sum, image_row_grad, text_row_grad, scale_grad = contrastive(
        image_rows, text_rows, every_valid, logit_scale
    )
    image_top, image_embed_grad, image_post_gain, image_post_shift = head_back(
        image_head, image_post[0], image_post[1], image_embed, image_row_grad
    )
    text_top, text_embed_grad, text_post_gain, text_post_shift = head_back(
        text_head, text_post[0], text_post[1], text_embed, text_row_grad
    )
    offset = lax.axis_index("dp") * examples
    image_top = lax.dynamic_slice_in_dim(image_top, offset, examples, 0)
    text_top = lax.dynamic_slice_in_dim(text_top, offset, examples, 0)
    image_top = image_pick[..., None] * image_top[:, None, :]
    text_top = text_pick[..., None] * text_top[:, None, :]
    image_grad = image_cotangent.astype(jnp.float32) * live_rows[..., None] + image_top
    text_grad = text_cotangent.astype(jnp.float32) + text_top
    image_ngrad, image_expand_grad, image_offset_grad, image_contract_grad, image_feed_shift = (
        feed_back(image_grad, image_kept, image_expand, image_contract)
    )
    text_ngrad, text_expand_grad, text_offset_grad, text_contract_grad, text_feed_shift = feed_back(
        text_grad, text_kept, text_expand, text_contract
    )
    image_nsum, text_nsum = over_mp(image_ngrad, text_ngrad, 0)
    image_rgrad, image_gain_two, image_shift_two = norm_back(
        image_kept["resid"], image_norms[2], image_norms[3], image_nsum
    )
    text_rgrad, text_gain_two, text_shift_two = norm_back(
        text_kept["resid"], text_norms[2], text_norms[3], text_nsum
    )
    image_resid_grad = image_grad + image_rgrad
    text_resid_grad = text_grad + text_rgrad
    image_agrad, image_inward_grad, image_bias_grad, image_outward_grad, image_attn_shift = (
        attention_back(image_resid_grad, image_stored, image_mask, image_inward, image_outward)
    )
    text_agrad, text_inward_grad, text_bias_grad, text_outward_grad, text_attn_shift = (
        attention_back(text_resid_grad, text_stored, text_mask, text_inward, text_outward)
    )
    image_asum, text_asum = over_mp(image_agrad, text_agrad, 0)
    image_xgrad, image_gain_one, image_shift_one = norm_back(
        image_stored["values"], image_norms[0], image_norms[1], image_asum
    )
    text_xgrad, text_gain_one, text_shift_one = norm_back(
        text_stored["values"], text_norms[0], text_norms[1], text_asum
    )
    image_token_grad = image_resid_grad + image_xgrad
    text_token_grad = text_resid_grad + text_xgrad

    def vectors(gain_one, shift_one, gain_two, shift_two, attn, feed, offsets, biases):
        joined = biases.reshape(-1)
        joined = jnp.pad(joined, (0, gain_one.shape[0] - joined.shape[0]))
        return jnp.stack([gain_one, shift_one, gain_two, shift_two, attn, feed, offsets, joined])

    image_vectors = vectors(
        image_gain_one,
        image_shift_one,
        image_gain_two,
        image_shift_two,
        image_attn_shift,
        image_feed_shift,
        image_offset_grad,
        image_bias_grad,
    )
    text_vectors = vectors(
        text_gain_one,
        text_shift_one,
        text_gain_two,
        text_shift_two,
        text_attn_shift,
        text_feed_shift,
        text_offset_grad,
        text_bias_grad,
    )
    pieces = [
        image_expand_grad,
        image_contract_grad,
        text_expand_grad,
        text_contract_grad,
        image_outward_grad,
        image_inward_grad,
        text_outward_grad,
        text_inward_grad,
        image_vectors,
        text_vectors,
    ]
    flat = jnp.concatenate([panels(piece) for piece in pieces], axis=0)
    held = flat.shape[0]
    flat = jnp.pad(flat, ((0, -held % SPAN), (0, 0)))
    flat = dp_sum(count, flat, 1)
    summed, start = [], 0
    for piece in pieces:
        rows = piece.size // LANES
        summed.append(unpanel(flat[start : start + rows], piece.shape[1]))
        start += rows
    (
        image_expand_grad,
        image_contract_grad,
        text_expand_grad,
        text_contract_grad,
        image_outward_grad,
        image_inward_grad,
        text_outward_grad,
        text_inward_grad,
        image_vectors,
        text_vectors,
    ) = summed

    def inward_of(values):
        return jnp.swapaxes(values.reshape(3, -1, values.shape[1]), 1, 2)

    image_bias = image_vectors[7, : image_biases.size].reshape(image_biases.shape)
    text_bias = text_vectors[7, : text_biases.size].reshape(text_biases.shape)
    post_grad = jnp.concatenate(
        [
            jnp.stack([image_post_gain, image_post_shift]),
            jnp.stack([text_post_gain, text_post_shift]),
        ],
        axis=1,
    )
    image_result = to_low(image_final * live_rows[..., None])
    spare = ((0, 0), (0, patch - IMG_ROWS), (0, 0))
    return (
        jnp.pad(image_result, spare),
        to_low(text_final)[:, :context],
        jnp.reshape(loss_value, (1,)),
        jnp.reshape(hit_sum, (1,)),
        jnp.pad(image_token_grad, spare),
        text_token_grad[:, :context],
        image_vectors[:4],
        inward_of(image_inward_grad),
        image_bias,
        image_outward_grad,
        image_vectors[4:6],
        image_expand_grad,
        image_vectors[6],
        image_contract_grad,
        image_embed_grad,
        text_vectors[:4],
        inward_of(text_inward_grad),
        text_bias,
        text_outward_grad,
        text_vectors[4:6],
        text_expand_grad,
        text_vectors[6],
        text_contract_grad,
        text_embed_grad,
        post_grad,
        jnp.reshape(scale_grad, (1,)),
    )


def solution(mesh):
    placed = (
        P("dp", None, None),
        P(),
        P(None, None, "mp"),
        P(None, "mp"),
        P("mp", None),
        P(),
        P(None, "mp"),
        P("mp"),
        P("mp", None),
        P(),
        P("dp", None, None),
        P(),
        P(None, None, "mp"),
        P(None, "mp"),
        P("mp", None),
        P(),
        P(None, "mp"),
        P("mp"),
        P("mp", None),
        P(),
        P(),
        P(),
        P("dp", None, None),
        P("dp", None, None),
        P("dp"),
        P("dp"),
        P("dp"),
    )
    return jax.shard_map(
        functools.partial(shards, mesh.shape["dp"]),
        mesh=mesh,
        in_specs=placed,
        out_specs=(
            P("dp", None, None),
            P("dp", None, None),
            P(),
            P(),
            P("dp", None, None),
            P("dp", None, None),
            P(),
            P(None, None, "mp"),
            P(None, "mp"),
            P("mp", None),
            P(),
            P(None, "mp"),
            P("mp"),
            P("mp", None),
            P(),
            P(),
            P(None, None, "mp"),
            P(None, "mp"),
            P("mp", None),
            P(),
            P(None, "mp"),
            P("mp"),
            P("mp", None),
            P(),
            P(),
            P(),
        ),
        check_vma=False,
    )
```

```python
import functools

import jax
import jax.numpy as jnp
from jax import lax
from jax.experimental import pallas as pl
from jax.experimental.pallas import tpu as pltpu
from jax.sharding import PartitionSpec as P

MESH = pl.DeviceIdType.MESH
HEAD = 64
LOW_LEN = 50
HIGH_LEN = 101
IMG_ROWS = 104
TXT_ROWS = 80
SPAN = 256
SLOTS = 4
LANES = 256

EPSILON = 1e-05
MASKED = -1000000000.0
HIGHEST = lax.Precision.HIGHEST


def dp_sum_machine(count, blocks, total, rings, sends, recvs, credits):
    places = count // 2
    deep = places // 2
    dp, mp = lax.axis_index("dp"), lax.axis_index("mp")
    side, place = lax.rem(dp, 2), dp // 2
    low = place < deep
    depth = jnp.where(low, place, places - 1 - place)
    inner = jnp.where(low, place + 1, place - 1)
    outer = jnp.clip(jnp.where(low, place - 1, place + 1), 0, places - 1)
    half = jnp.where(low, 0, 1)
    pair_id = (place * 2 + 1 - side, mp)
    inner_id = (inner * 2 + side, mp)
    outer_id = (outer * 2 + side, mp)
    quarter = SPAN // 4

    def part(offset, size):
        def at(block):
            start = pl.multiple_of(block * SPAN + offset, quarter)
            return total.at[pl.ds(start, size)]

        return at

    kept = part(side * quarter, quarter)
    given = part((1 - side) * quarter, quarter)
    whole = part(2 * quarter, 2 * quarter)
    mid_kept = part((2 + half) * quarter, quarter)
    mid_given = part((3 - half) * quarter, quarter)
    middle = depth == deep - 1
    not_middle = depth < deep - 1
    not_end = depth > 0
    yes = depth >= 0

    kinds = [
        (yes, 0, given, pair_id, yes, 0, pair_id, rings[0], kept),
        (not_middle, depth, whole, inner_id, not_end, depth - 1, outer_id, rings[1], whole),
        (not_middle, depth + 1, kept, inner_id, not_end, depth, outer_id, rings[2], kept),
        (middle, deep - 1, mid_given, inner_id, middle, deep - 1, inner_id, rings[3], mid_kept),
        (middle, deep, mid_kept, pair_id, middle, deep, pair_id, rings[4], mid_kept),
        (middle, deep, kept, inner_id, middle, deep, inner_id, rings[5], kept),
        (middle, deep + 1, mid_kept, inner_id, middle, deep + 1, inner_id, None, mid_given),
        (not_end, 2 * deep - depth, kept, outer_id, not_middle, 2 * deep - depth - 1, inner_id, None, kept),
        (not_end, 2 * deep + 1 - depth, whole, outer_id, not_middle, 2 * deep - depth, inner_id, None, whole),
        (yes, 2 * deep, kept, pair_id, yes, 2 * deep, pair_id, None, given),
    ]

    def copy(k, kind, block):
        _, _, src, target, _, _, _, ring, land = kind
        slot = lax.rem(block, SLOTS)
        dst = src(block) if ring is None else ring.at[slot]
        return pltpu.make_async_remote_copy(
            src_ref=src(block),
            dst_ref=dst,
            send_sem=sends.at[k, slot],
            recv_sem=recvs.at[k, slot],
            device_id=target,
            device_id_type=MESH,
        )

    def valid(block):
        return jnp.logical_and(block >= 0, block < blocks)

    def start(t):
        for k, kind in enumerate(kinds):
            block = t - 2 * kind[1]

            @pl.when(jnp.logical_and(kind[0], valid(block)))
            def _():
                @pl.when(block >= SLOTS)
                def _():
                    pl.semaphore_wait(credits.at[k], 1)

                copy(k, kind, block).start()

    def finish(t):
        for k, kind in enumerate(kinds):
            sends_it, sent_stage, _, _, takes_it, got_stage, source, ring, land = kind
            sent = t - 2 * sent_stage
            got = t - 2 * got_stage

            @pl.when(jnp.logical_and(sends_it, valid(sent)))
            def _():
                copy(k, kind, sent).wait_send()

            @pl.when(jnp.logical_and(takes_it, valid(got)))
            def _():
                copy(k, kind, got).wait_recv()
                if ring is not None:
                    here = land(got)
                    here[...] = here[...] + ring[lax.rem(got, SLOTS)]

                @pl.when(got < blocks - SLOTS)
                def _():
                    pl.semaphore_signal(credits.at[k], inc=1, device_id=source, device_id_type=MESH)

    def tick(t):
        start(t)

        @pl.when(t > 0)
        def _():
            finish(t - 1)

    return tick, blocks + 4 * deep + 1


def dp_rings():
    quarter = SPAN // 4
    sizes = [quarter, 2 * quarter, quarter, quarter, quarter, quarter]
    return [pltpu.VMEM((SLOTS, size, LANES), jnp.float32) for size in sizes] + [
        pltpu.SemaphoreType.DMA((10, SLOTS)),
        pltpu.SemaphoreType.DMA((10, SLOTS)),
        pltpu.SemaphoreType.REGULAR((10,)),
    ]


LOW, FULL = jnp.bfloat16, jnp.float32


def mm(left, right):
    return jnp.dot(left, right, preferred_element_type=FULL)


def mm_nt(left, right, precision=None):
    dims = (((1,), (1,)), ((), ()))
    return lax.dot_general(left, right, dims, precision=precision, preferred_element_type=FULL)


def mm_tn(left, right, precision=None):
    dims = (((0,), (0,)), ((), ()))
    return lax.dot_general(left, right, dims, precision=precision, preferred_element_type=FULL)


def row_sum(values):
    return jnp.sum(values, axis=1, keepdims=True)


def col_sum(values):
    return jnp.sum(values, axis=0, keepdims=True)


def whitened(values):
    width = values.shape[1]
    centred = values - row_sum(values) * (1.0 / width)
    scale = lax.rsqrt(row_sum(centred * centred) * (1.0 / width) + EPSILON)
    return centred * scale, scale


def whitened_back(white, scale, gain, gradient):
    width = white.shape[1]
    inner = gradient * gain
    mean = row_sum(inner) * (1.0 / width)
    slope = row_sum(inner * white) * (1.0 / width)
    return scale * (inner - mean - white * slope)


class Fields:
    pass


class Tower:
    def __init__(self, index, rows, per, fields):
        self.__dict__.update(fields.__dict__)
        self.index, self.rows, self.per = index, rows, per
        self.wide = self.shifts.shape[1]
        self.across_heads = self.biases.shape[1]
        self.hidden = self.offsets.shape[1]
        self.panels = self.wide // LANES

    def at(self, owner):
        return pl.ds(pl.multiple_of(owner * self.rows, self.rows), self.rows)

    def token_place(self, owner):
        return self.token_grad.at[pl.ds(2 * owner, 2), pl.ds(0, self.per)]


def gradient_rows(towers):
    image, text = towers
    where, start = {}, 0
    for tower, name, rows in (
        (text, "contract", text.hidden),
        (text, "expand", text.wide),
        (image, "contract", image.hidden),
        (image, "expand", image.wide),
        (text, "outward", text.across_heads),
        (text, "inward", 3 * text.across_heads),
        (image, "outward", image.across_heads),
        (image, "inward", 3 * image.across_heads),
        (image, "vectors", 8),
        (text, "vectors", 8),
    ):
        width = tower.hidden if name == "expand" else tower.wide
        where[tower.index, name] = (start, rows, width)
        start += rows * (width // LANES)
    return where, start


def block_kernel(count, names, *refs):
    fields = [Fields(), Fields(), Fields()]
    for (index, name), ref in zip(names, refs):
        setattr(fields[index], name, ref)
    image = Tower(0, 2 * IMG_ROWS, IMG_ROWS, fields[0])
    text = Tower(1, 2 * TXT_ROWS, TXT_ROWS, fields[1])
    r = fields[2]
    places, _ = gradient_rows((image, text))
    deep = count // 4
    dp, mp = lax.axis_index("dp"), lax.axis_index("mp")
    flip, core_bit = mp // 2, lax.rem(mp, 2)
    core_mp = flip * 2 + 1 - core_bit
    across_mp = (1 - flip) * 2 + core_bit
    diag_mp = (1 - flip) * 2 + 1 - core_bit
    core, across, diag = (dp, core_mp), (dp, across_mp), (dp, diag_mp)
    own_mp = mp

    for tower in (text, image):
        tower.loads = {}
    for k, name in enumerate(LOADED):
        for tower in (text, image):
            source, target = getattr(tower, name + FAR), getattr(tower, name)
            copy = pltpu.make_async_copy(source, target, r.load_sems.at[2 * k + tower.index])
            copy.start()
            tower.loads[name] = copy
    r.blank[...] = jnp.zeros(r.blank.shape, FULL)
    blank_store = pltpu.make_async_copy(
        r.blank,
        image.token_grad.at[:, pl.ds(image.per, image.token_grad.shape[1] - image.per)],
        r.store_sems.at[7],
    )
    blank_store.start()
    barrier = pltpu.get_barrier_semaphore()
    friends = [core, across, diag] + [(lax.rem(dp + k, count), mp) for k in range(1, count)]
    for friend in friends:
        pl.semaphore_signal(barrier, inc=1, device_id=friend, device_id_type=MESH)
    pl.semaphore_wait(barrier, len(friends))

    scatter_sems = r.scatter_send, r.scatter_recv
    gather_sems = r.gather_send, r.gather_recv
    swap_sems = r.swap_send, r.swap_recv
    spread_sems = r.spread_send, r.spread_recv
    trade_sems = r.trade_send, r.trade_recv

    def remote(src, dst, group, k, peer):
        return pltpu.make_async_remote_copy(
            src_ref=src,
            dst_ref=dst,
            send_sem=group[0].at[k],
            recv_sem=group[1].at[k],
            device_id=peer,
            device_id_type=MESH,
        )

    class Scatter:
        def __init__(self, tower, phase, bank):
            self.tower = tower
            self.parts, self.near_buf, self.over_buf = (
                (tower.parts1, tower.near1, tower.over1)
                if bank
                else (tower.parts0, tower.near0, tower.over0)
            )
            k = (phase * 2 + tower.index) * 3
            self.far = remote(self.parts.at[tower.at(diag_mp)], self.near_buf.at[0], scatter_sems, k, core)
            self.near = remote(self.parts.at[tower.at(core_mp)], self.near_buf.at[1], scatter_sems, k + 1, core)
            self.over = remote(self.near_buf.at[0], self.over_buf, scatter_sems, k + 2, across)

        def send_over(self):
            self.far.wait()
            self.near_buf[0] = self.near_buf[0] + self.parts[self.tower.at(across_mp), :]
            self.over.start()

        def result(self):
            self.near.wait()
            self.over.wait()
            return self.parts[self.tower.at(own_mp), :] + self.near_buf[1] + self.over_buf[...]

    class Gather:
        def __init__(self, tower, phase):
            k = (phase * 2 + tower.index) * 3
            if phase == 2:
                source, mine, passed = (
                    tower.back,
                    tower.token_place(own_mp),
                    tower.token_place(across_mp),
                )
            else:
                mine = source = tower.carried.at[tower.at(own_mp)]
                passed = tower.carried.at[tower.at(across_mp)]
            self.one = remote(source, mine, gather_sems, k, across)
            self.two = remote(source, mine, gather_sems, k + 1, core)
            self.on = remote(passed, passed, gather_sems, k + 2, core)

        def start(self):
            self.one.start()
            self.two.start()

        def got_core(self):
            self.two.wait_recv()

        def got_across(self):
            self.one.wait_recv()
            self.on.start()

        def got_diag(self):
            self.on.wait_recv()

        def sent(self):
            self.one.wait_send()
            self.two.wait_send()
            self.on.wait_send()

    def length(example):
        return jnp.where(r.resolution[example] == 1, HIGH_LEN, LOW_LEN)

    def live(tower, owner, places_):
        if tower is text:
            return None
        first, second = length(2 * owner), length(2 * owner + 1) + tower.per
        return places_ < jnp.where(places_ < tower.per, first, second)

    def allowed(tower, owner):
        shape = (tower.rows, tower.rows)
        query = lax.broadcasted_iota(jnp.int32, shape, 0)
        key = lax.broadcasted_iota(jnp.int32, shape, 1)
        key_start = jnp.where(query < tower.per, 0, tower.per)
        if tower is text:
            end = query + 1
        else:
            first, second = length(2 * owner), length(2 * owner + 1) + tower.per
            end = jnp.where(query < tower.per, first, second)
        return jnp.logical_and(key >= key_start, key < end)

    def chosen_places(tower, owner):
        if tower is text:
            return r.ends[2 * owner], r.ends[2 * owner + 1] + tower.per
        return 0, tower.per

    def pick(tower, owner, values):
        if tower is image:
            return [values[0:1], values[tower.per : tower.per + 1]]
        place = lax.broadcasted_iota(jnp.int32, (tower.rows, 1), 0)
        return [
            col_sum(jnp.where(place == at, values, 0.0)) for at in chosen_places(tower, owner)
        ]

    def softmax(tower, scores, mask):
        scores = jnp.where(mask, scores * HEAD ** (-0.5), MASKED)
        top = jnp.max(scores, axis=1, keepdims=True)
        weights = jnp.exp(scores - top)
        return weights * (1.0 / row_sum(weights))

    def owner_of(j):
        return lax.rem(flip + 1 - j // 2, 2) * 2 + lax.rem(core_bit + 1 - lax.rem(j, 2), 2)

    def prepare(tower):
        for name in ("tokens", "inward", "outward"):
            tower.loads[name].wait()
        heads = tower.across_heads
        if tower is text:
            for k in range(3):
                tower.joined[:, k * heads : (k + 1) * heads] = tower.inward[k]
        tower.bias_row[:, 0:heads] = tower.biases[0:1, :]
        tower.bias_row[:, heads : 2 * heads] = jnp.zeros((1, heads), FULL)
        tower.bias_row[:, 2 * heads : 3 * heads] = tower.biases[1:2, :]

    def rows_of(tower, owner):
        if tower is text:
            return tower.tokens[tower.at(owner), :].astype(FULL)
        pair = [tower.tokens[2 * owner + k].astype(FULL)[0 : tower.per] for k in range(2)]
        return jnp.concatenate(pair, axis=0)

    def into_heads(tower, normed):
        if tower is text:
            return mm(normed, tower.joined[...])
        return mm_nt(normed, tower.inward[...].reshape(3 * tower.across_heads, tower.wide))

    def out_of_heads(tower, grads):
        if tower is text:
            return mm_nt(grads, tower.joined[...])
        return mm(grads, tower.inward[...].reshape(3 * tower.across_heads, tower.wide))

    def attend(tower, owner):
        at, heads = tower.at(owner), tower.across_heads
        white, _ = whitened(rows_of(tower, owner))
        normed = (white * tower.norms[0:1, :] + tower.norms[1:2, :]).astype(LOW)
        tower.normed[at, :] = normed
        qkv = (into_heads(tower, normed) + tower.bias_row[...]).astype(LOW)
        tower.qkv[at, :] = qkv
        mask = allowed(tower, owner)
        mixed = []
        for h in range(heads // HEAD):
            query, key, value = (
                qkv[:, k * heads + h * HEAD : k * heads + (h + 1) * HEAD] for k in range(3)
            )
            weights = softmax(tower, mm_nt(query, key), mask)
            mixed.append(mm(weights.astype(LOW), value).astype(LOW))
        mixed = jnp.concatenate(mixed, axis=1)
        tower.mixed[at, :] = mixed
        tower.parts0[at, :] = mm(mixed, tower.outward[...])

    def attend_all(tower, scatter, first, last):
        def body(j, carry):
            attend(tower, owner_of(j))

            @pl.when(j == 0)
            def _():
                scatter.far.start()

            @pl.when(j == 1)
            def _():
                scatter.send_over()

            @pl.when(j == 2)
            def _():
                scatter.near.start()

            return carry

        lax.fori_loop(first, last, body, 0)

    def second_norm(tower, scatter, gather):
        at = tower.at(own_mp)
        mine = rows_of(tower, own_mp)
        tower.own_tokens[...] = mine.astype(LOW)
        resid = mine + scatter.result() + tower.shifts[0:1, :]
        tower.resid[...] = resid
        white, _ = whitened(resid)
        normed = (white * tower.norms[2:3, :] + tower.norms[3:4, :]).astype(LOW)
        tower.carried[at, :] = normed.astype(FULL)
        gather.start()

    def feed(tower, owner):
        at = tower.at(owner)
        normed = tower.carried[at, :].astype(LOW)
        tower.normed_two[at, :] = normed
        hidden = mm(normed, tower.expand[...]) + tower.offsets[...]
        gate = 1.0 / (1.0 + jnp.exp(-1.702 * hidden))
        active = (hidden * gate).astype(LOW)
        tower.active[at, :] = active
        tower.slope[at, :] = (gate * (1.0 + 1.702 * hidden * (1.0 - gate))).astype(LOW)
        part = mm(active, tower.contract[...])
        tower.parts1[at, :] = part
        for k, row in enumerate(pick(tower, owner, part)):
            spot = 2 * tower.index + k
            r.chosen[owner, spot : spot + 1, 0 : tower.wide] = row

    scatters = [[Scatter(t, phase, phase == 1) for t in (image, text)] for phase in range(4)]
    gathers = [[Gather(t, phase) for t in (image, text)] for phase in range(4)]

    prepare(text)
    attend_all(text, scatters[0][1], 0, 4)
    prepare(image)
    attend_all(image, scatters[0][0], 0, 2)
    second_norm(text, scatters[0][1], gathers[0][1])
    attend_all(image, scatters[0][0], 2, 4)
    for tower in (text, image):
        reload = pltpu.make_async_copy(
            tower.cotangent_far, tower.tokens, r.load_sems.at[2 * len(LOADED) + tower.index]
        )
        tower.loads["cotangent"] = reload
        tower.loads["expand"].wait()
        tower.loads["contract"].wait()
    r.chosen[...] = jnp.zeros(r.chosen.shape, FULL)
    feed(text, own_mp)
    gathers[0][1].got_core()
    feed(text, core_mp)
    second_norm(image, scatters[0][0], gathers[0][0])
    for tower in (text, image):
        tower.loads["cotangent"].start()
    feed(image, own_mp)
    gathers[0][0].got_core()
    feed(image, core_mp)
    gathers[0][1].got_across()
    feed(text, across_mp)
    gathers[0][1].got_diag()
    feed(text, diag_mp)
    gathers[0][0].got_across()
    feed(image, across_mp)
    gathers[0][0].got_diag()
    feed(image, diag_mp)

    for gather in gathers[0]:
        gather.sent()

    chosen, chosen_got = r.chosen, r.chosen_got
    swaps = [
        remote(chosen.at[peer[1]], chosen_got.at[k], swap_sems, k, peer)
        for k, peer in enumerate((core, across, diag))
    ]
    for swap in swaps:
        swap.start()
    for swap in swaps:
        swap.wait()
    total = chosen[own_mp] + chosen_got[0] + chosen_got[1] + chosen_got[2]
    every = r.every
    for tower in (image, text):
        wide = tower.wide
        for k, row in enumerate(pick(tower, own_mp, tower.resid[...])):
            spot = 2 * tower.index + k
            every[own_mp, dp, spot : spot + 1, 0:wide] = (
                total[spot : spot + 1, 0:wide] + row + tower.shifts[1:2, :]
            )
    for k in range(2):
        mark = r.validity[2 * own_mp + k].astype(FULL)
        every[own_mp, dp, 2 + k : 3 + k, text.wide : text.wide + 128] = jnp.full((1, 128), mark, FULL)
    mine = every.at[own_mp, dp]
    spread = [
        remote(mine, mine, spread_sems, k, (lax.rem(dp + k, count), mp)) for k in range(1, count)
    ]
    for copy in spread:
        copy.start()
    for scatter in scatters[1]:
        scatter.far.start()
        scatter.near.start()
    for copy in spread:
        copy.wait()
    one = remote(every.at[own_mp], every.at[own_mp], swap_sems, 3, across)
    two = remote(every.at[own_mp], every.at[own_mp], swap_sems, 4, core)
    on = remote(every.at[across_mp], every.at[across_mp], swap_sems, 5, core)
    one.start()
    two.start()
    one.wait_recv()
    on.start()
    scatters[1][1].send_over()
    scatters[1][0].send_over()
    two.wait_recv()
    on.wait_recv()
    for copy in (one, two, on):
        copy.wait_send()

    for place in range(count):
        for quarter in range(4):
            spot = (place * 4 + quarter) * 2
            block = every[quarter, place]
            image.carried[spot : spot + 2, :] = block[0:2, :]
            text.carried[spot : spot + 2, :] = block[2:4, 0 : text.wide]
            r.marks[spot : spot + 2, :] = block[2:4, text.wide : text.wide + 128]
    for tower in (text, image):
        tower.loads["embed"].wait()
    post = r.post_norms

    def head(tower, rows):
        lanes = slice(0, image.wide) if tower is image else slice(image.wide, image.wide + text.wide)
        white, scale = whitened(rows)
        low = (white * post[0:1, lanes] + post[1:2, lanes]).astype(LOW)
        raw = mm(low, tower.embed[...])
        inverse = lax.rsqrt(row_sum(raw * raw) + 1e-06)
        return lanes, white, scale, low, raw * inverse, inverse

    heads = [head(image, image.carried[0 : 8 * count, :]), head(text, text.carried[0 : 8 * count, :])]
    unit_i, unit_t = heads[0][4], heads[1][4]
    marks = r.marks[...]
    examples = marks.shape[0]
    valid_col = marks[:, 0:1]
    valid_row = jnp.transpose(marks)[0:1, :]
    number = col_sum(valid_col)
    factor = jnp.exp(r.logit_scale[...])
    logits = factor * mm_nt(unit_i, unit_t, HIGHEST)
    by_row = jnp.where(valid_row > 0.5, logits, MASKED)
    by_col = jnp.where(valid_col > 0.5, logits, MASKED)
    row_top = jnp.max(by_row, axis=1, keepdims=True)
    row_lse = row_top + jnp.log(row_sum(jnp.exp(by_row - row_top)))
    col_top = jnp.max(by_col, axis=0, keepdims=True)
    col_lse = col_top + jnp.log(col_sum(jnp.exp(by_col - col_top)))
    diagonal = factor * row_sum(unit_i * unit_t)
    loss = col_sum(valid_col * (row_lse - 2.0 * diagonal)) + row_sum(valid_row * col_lse)
    r.loss[...] = loss / (2.0 * number)
    r.hits[...] = col_sum(valid_col * jnp.exp(diagonal - row_lse))
    row_id = lax.broadcasted_iota(jnp.int32, (examples, examples), 0)
    col_id = lax.broadcasted_iota(jnp.int32, (examples, examples), 1)
    same = jnp.where(row_id == col_id, 1.0, 0.0)
    pairs = (
        valid_col * (jnp.exp(by_row - row_lse) - same)
        + valid_row * (jnp.exp(by_col - col_lse) - same)
    ) / (2.0 * number)
    r.scale_grad[...] = col_sum(row_sum(pairs * logits))
    unit_grads = [
        factor * lax.dot(pairs, unit_t, precision=HIGHEST, preferred_element_type=FULL),
        factor * mm_tn(pairs, unit_i, HIGHEST),
    ]
    stores = []
    for tower, (lanes, white, scale, low, unit, inverse), grad in zip((image, text), heads, unit_grads):
        raw_grad = (inverse * (grad - unit * row_sum(unit * grad))).astype(LOW)
        home = tower.parts0.at[0 : tower.wide, 0 : tower.embed.shape[1]]
        home[...] = mm_tn(low, raw_grad)
        stores.append(pltpu.make_async_copy(home, tower.embed_grad, r.store_sems.at[tower.index]))
        stores[-1].start()
        low_grad = mm_nt(raw_grad, tower.embed[...])
        r.post_grad[0:1, lanes] = col_sum(low_grad * white)
        r.post_grad[1:2, lanes] = col_sum(low_grad)
        tower.carried[0 : 8 * count, :] = whitened_back(white, scale, post[0:1, lanes], low_grad)
        own = tower.carried[pl.ds(pl.multiple_of(dp * 8, 8), 8), :]
        for k in range(8):
            tower.top[k] = own[k : k + 1, :]

    def grad_rows(tower, owner):
        place = lax.broadcasted_iota(jnp.int32, (tower.rows, 1), 0)
        values = rows_of(tower, owner)
        alive = live(tower, owner, place)
        if alive is not None:
            values = jnp.where(alive, values, 0.0)
        for k, at in enumerate(chosen_places(tower, owner)):
            values = values + jnp.where(place == at, tower.top[2 * owner + k], 0.0)
        return values

    def feed_back(tower, j, scatter):
        owner = owner_of(j)
        at = tower.at(owner)
        low = grad_rows(tower, owner).astype(LOW)
        tower.low_grad[at, :] = low
        active_grad = mm_nt(low, tower.contract[...]).astype(LOW).astype(FULL)
        hidden_grad = active_grad * tower.slope[at, :].astype(FULL)
        tower.offset_grad[...] = tower.offset_grad[...] + col_sum(hidden_grad)
        hidden_low = hidden_grad.astype(LOW)
        tower.slope[at, :] = hidden_low
        tower.parts0[at, :] = mm_nt(hidden_low, tower.expand[...])

        @pl.when(j == 0)
        def _():
            scatter.far.start()

        @pl.when(j == 2)
        def _():
            scatter.near.start()

    def put_back(tower, values):
        tower.back[...] = values.reshape(2, tower.per, tower.wide)

    def get_back(tower):
        return tower.back[...].reshape(tower.rows, tower.wide)

    summed = r.summed

    def put(tower, name, values, first=0):
        start, rows, width = places[tower.index, name]
        for k in range(width // LANES):
            to = pl.ds(pl.multiple_of(start + k * rows + first, 8), values.shape[0])
            summed[to, :] = values[:, k * LANES : (k + 1) * LANES]

    def outer(tower, name, left, right):
        def body(j, carry):
            cut = pl.ds(pl.multiple_of(j * LANES, LANES), LANES)
            put(tower, name, mm_tn(left[:, cut], right[...]), j * LANES)
            return carry

        lax.fori_loop(0, left.shape[1] // LANES, body, 0)

    rings = [r.ring0, r.ring1, r.ring2, r.ring3, r.ring4, r.ring5]
    tick, ticks = dp_sum_machine(
        count, summed.shape[0] // SPAN, summed, rings, r.dp_send, r.dp_recv, r.dp_credit
    )
    out_copy = pltpu.make_async_copy(summed, r.summed_far, r.store_sems.at[4])
    clock = [0]

    def go(number):
        def body(t, carry):
            tick(t)
            done = t - 1 - 4 * deep

            @pl.when(done >= 0)
            def _():
                at = pl.ds(pl.multiple_of(done * SPAN, SPAN), SPAN)
                pltpu.make_async_copy(
                    summed.at[at], r.summed_far.at[at], r.store_sems.at[4]
                ).start()

            return carry

        lax.fori_loop(clock[0], clock[0] + number, body, 0)
        clock[0] += number

    for copy in stores:
        copy.wait()
    for tower in (image, text):
        tower.loads["cotangent"].wait()
        tower.offset_grad[...] = jnp.zeros(tower.offset_grad.shape, FULL)
        tower.bias_grad[...] = jnp.zeros(tower.bias_grad.shape, FULL)
        grads = grad_rows(tower, own_mp)
        put_back(tower, grads)
        tower.mixed_vectors[own_mp] = jnp.zeros((8, tower.wide), FULL)
        tower.mixed_vectors[own_mp, 5:6, :] = col_sum(grads)

    def feed_back_loop(tower, first, last, scatter):
        def body(j, carry):
            feed_back(tower, j, scatter)
            return carry

        lax.fori_loop(first, last, body, 0)

    feed_back_loop(text, 0, 4, scatters[2][1])
    outer(text, "contract", text.active, text.low_grad)
    outer(text, "expand", text.normed_two, text.slope)
    go(1)
    scatters[2][1].send_over()
    feed_back_loop(image, 0, 1, scatters[2][0])
    go(1)
    feed_back_loop(image, 1, 2, scatters[2][0])
    scatters[2][0].send_over()
    go(1)
    feed_back_loop(image, 2, 4, scatters[2][0])
    go(1)
    outer(image, "contract", image.active, image.low_grad)
    go(1)
    outer(image, "expand", image.normed_two, image.slope)
    go(1)

    def second_norm_back(tower, scatter, gather):
        normed_grad = scatter.result()
        white, scale = whitened(tower.resid[...])
        vectors = tower.mixed_vectors
        vectors[own_mp, 2:3, :] = col_sum(normed_grad * white)
        vectors[own_mp, 3:4, :] = col_sum(normed_grad)
        grads = get_back(tower) + whitened_back(white, scale, tower.norms[2:3, :], normed_grad)
        vectors[own_mp, 4:5, :] = col_sum(grads)
        put_back(tower, grads)
        tower.carried[tower.at(own_mp), :] = grads.astype(LOW).astype(FULL)
        gather.start()

    def attend_back(tower, owner):
        at, heads = tower.at(owner), tower.across_heads
        low = tower.carried[at, :].astype(LOW)
        tower.low_grad[at, :] = low
        mixed_grad = mm_nt(low, tower.outward[...]).astype(LOW)
        qkv = tower.qkv[at, :]
        mask = allowed(tower, owner)
        grads = [[], [], []]
        for h in range(heads // HEAD):
            query, key, value = (
                qkv[:, k * heads + h * HEAD : k * heads + (h + 1) * HEAD] for k in range(3)
            )
            weights = softmax(tower, mm_nt(query, key), mask)
            grad = mixed_grad[:, h * HEAD : (h + 1) * HEAD]
            weight_grad = mm_nt(grad, value)
            grads[2].append(mm_tn(weights.astype(LOW), grad))
            score_grad = weights * (weight_grad - row_sum(weight_grad * weights))
            score_grad = score_grad.astype(LOW)
            grads[0].append(mm(score_grad, key) * HEAD ** (-0.5))
            grads[1].append(mm_tn(score_grad, query) * HEAD ** (-0.5))
        joined = jnp.concatenate([part for kind in grads for part in kind], axis=1)
        tower.bias_grad[...] = tower.bias_grad[...] + col_sum(joined)
        low = joined.astype(LOW)
        tower.qkv[at, :] = low
        tower.parts0[at, :] = out_of_heads(tower, low)

    def outer_attention(tower):
        heads = tower.across_heads
        put(tower, "outward", mm_tn(tower.mixed[...], tower.low_grad[...]))
        for k in range(3):
            grads = tower.qkv[:, k * heads : (k + 1) * heads]
            if tower is image:
                put(tower, "inward", mm_tn(grads, tower.normed[...]), k * heads)
            else:
                part = mm_tn(tower.normed[...], grads)
                start, rows, _ = places[tower.index, "inward"]
                high = tower.wide // 2
                for side in range(2):
                    summed[start + k * high : start + (k + 1) * high, side * heads : (side + 1) * heads] = (
                        part[side * high : (side + 1) * high]
                    )

    second_norm_back(text, scatters[2][1], gathers[1][1])
    attend_back(text, own_mp)
    go(1)
    gathers[1][1].got_core()
    attend_back(text, core_mp)
    scatters[3][1].near.start()
    go(1)
    second_norm_back(image, scatters[2][0], gathers[1][0])
    gathers[1][1].got_across()
    attend_back(text, across_mp)
    go(1)
    gathers[1][1].got_diag()
    attend_back(text, diag_mp)
    scatters[3][1].far.start()
    attend_back(image, own_mp)
    go(1)
    scatters[3][1].send_over()
    gathers[1][0].got_core()
    attend_back(image, core_mp)
    scatters[3][0].near.start()
    go(1)
    outer_attention(text)
    go(1)
    gathers[1][0].got_across()
    attend_back(image, across_mp)
    go(1)
    gathers[1][0].got_diag()
    attend_back(image, diag_mp)
    scatters[3][0].far.start()
    go(1)
    scatters[3][0].send_over()
    outer_attention(image)
    go(1)

    def first_norm_back(tower, scatter, gather):
        normed_grad = scatter.result()
        white, scale = whitened(tower.own_tokens[...].astype(FULL))
        vectors = tower.mixed_vectors
        vectors[own_mp, 0:1, :] = col_sum(normed_grad * white)
        vectors[own_mp, 1:2, :] = col_sum(normed_grad)
        more = whitened_back(white, scale, tower.norms[0:1, :], normed_grad)
        put_back(tower, get_back(tower) + more)
        gather.start()
        store = pltpu.make_async_copy(
            tower.back, tower.token_place(own_mp), r.store_sems.at[2 + tower.index]
        )
        store.start()
        return store

    for gather in gathers[1]:
        gather.sent()
    go(1)
    token_stores = [first_norm_back(text, scatters[3][1], gathers[2][1])]
    go(3)
    token_stores.append(first_norm_back(image, scatters[3][0], gathers[2][0]))
    trades = []
    for tower in (image, text):
        vectors = tower.mixed_vectors
        for k, peer in enumerate((core, across, diag)):
            mine = vectors.at[own_mp]
            trades.append(remote(mine, mine, trade_sems, 3 * tower.index + k, peer))
            trades[-1].start()
    go(1)
    for trade in trades:
        trade.wait()
    vec_start = places[0, "vectors"][0]
    left = summed.shape[0] - vec_start
    summed[vec_start:, :] = jnp.zeros((left, LANES), FULL)
    for tower in (image, text):
        vectors = tower.mixed_vectors
        sums = vectors[0] + vectors[1] + vectors[2] + vectors[3]
        vectors[own_mp] = sums
        heads = tower.across_heads
        vectors[own_mp, 6:7, :] = tower.offset_grad[...]
        vectors[own_mp, 7:8, 0:heads] = tower.bias_grad[:, 0:heads]
        vectors[own_mp, 7:8, heads : 2 * heads] = tower.bias_grad[:, 2 * heads : 3 * heads]
        put(tower, "vectors", vectors[own_mp])
    gathers[2][1].got_core()
    gathers[2][1].got_across()
    go(2)

    def result_rows(tower, scatter, gather):
        values = tower.resid[...] + scatter.result() + tower.shifts[1:2, :]
        place = lax.broadcasted_iota(jnp.int32, (tower.rows, 1), 0)
        alive = live(tower, own_mp, place)
        if alive is not None:
            values = jnp.where(alive, values, 0.0)
        tower.carried[tower.at(own_mp), :] = values.astype(LOW).astype(FULL)
        gather.start()

    result_rows(text, scatters[1][1], gathers[3][1])
    result_rows(image, scatters[1][0], gathers[3][0])
    go(1)
    gathers[2][0].got_core()
    gathers[2][0].got_across()
    go(3)
    gathers[3][1].got_core()
    gathers[3][1].got_across()
    gathers[3][0].got_core()
    go(4)
    gathers[3][0].got_across()
    go(1)
    result_stores = []
    for tower in (text, image):
        gathers[3][tower.index].got_diag()
        for owner in range(4):
            at = tower.at(owner)
            values = tower.carried[at, :]
            if tower is text:
                tower.tokens[at, :] = values.astype(LOW)
            else:
                for k in range(2):
                    part = values[k * tower.per : (k + 1) * tower.per]
                    blank = jnp.zeros((tower.tokens.shape[1] - tower.per, tower.wide), FULL)
                    tower.tokens[2 * owner + k] = jnp.concatenate([part, blank], axis=0).astype(LOW)
        result_stores.append(
            pltpu.make_async_copy(tower.tokens, tower.result, r.store_sems.at[5 + tower.index])
        )
        result_stores[-1].start()
    go(ticks - clock[0])
    for gather in gathers[2]:
        gather.got_diag()
    for gather in gathers[2] + gathers[3]:
        gather.sent()
    for copy in token_stores + result_stores + [blank_store]:
        copy.wait()
    out_copy.wait()


LOADED = ("tokens", "inward", "outward", "expand", "contract", "embed")
FAR = "_far"


def block_call(count, towers, post_norms, logit_scale, scalars, collective_id):
    names, args, in_specs = [], [], []
    outs, out_names, out_specs = [], [], []
    scratch, scratch_names = [], []
    vmem, smem, anywhere = pltpu.VMEM, pltpu.SMEM, pl.ANY

    def give(index, space, **named):
        for name, value in named.items():
            names.append((index, name))
            args.append(value)
            in_specs.append(pl.BlockSpec(memory_space=space))

    def take(index, space, kind=FULL, **named):
        for name, shape in named.items():
            out_names.append((index, name))
            outs.append(jax.ShapeDtypeStruct(shape, kind))
            out_specs.append(pl.BlockSpec(memory_space=space))

    def hold(index, **named):
        for name, what in named.items():
            scratch_names.append((index, name))
            scratch.append(what)

    examples = 8 * count
    sizes = []
    for index, tower in enumerate(towers):
        give(index, anywhere, cotangent_far=tower["cotangent"])
        for name in LOADED:
            give(index, anywhere, **{name + FAR: tower[name]})
            hold(index, **{name: vmem(tower[name].shape, LOW)})
        for name in ("norms", "biases", "shifts", "offsets"):
            give(index, vmem, **{name: tower[name]})
        rows, wide, spaces = 8 * IMG_ROWS, tower["tokens"].shape[-1], tower["tokens"].shape
        if index:
            rows, spaces = 8 * TXT_ROWS, (8, TXT_ROWS, wide)
        heads, hidden, quarter = tower["biases"].shape[1], tower["offsets"].shape[1], rows // 4
        size = Fields()
        size.index, size.wide, size.across_heads, size.hidden = index, wide, heads, hidden
        sizes.append(size)
        take(index, anywhere, token_grad=spaces, embed_grad=tower["embed"].shape)
        take(index, anywhere, LOW, result=tower["tokens"].shape)
        hold(
            index,
            joined=vmem((wide, 3 * heads), LOW),
            normed=vmem((rows, wide), LOW),
            qkv=vmem((rows, 3 * heads), LOW),
            mixed=vmem((rows, heads), LOW),
            normed_two=vmem((rows, wide), LOW),
            active=vmem((rows, hidden), LOW),
            slope=vmem((rows, hidden), LOW),
            bias_row=vmem((1, 3 * heads), FULL),
            resid=vmem((quarter, wide), FULL),
            carried=vmem((rows, wide), FULL),
            back=vmem((2, quarter // 2, wide), FULL),
            own_tokens=vmem((quarter, wide), LOW),
            low_grad=vmem((rows, wide), LOW),
            parts0=vmem((rows, wide), FULL),
            near0=vmem((2, quarter, wide), FULL),
            over0=vmem((quarter, wide), FULL),
            parts1=vmem((rows, wide), FULL),
            near1=vmem((2, quarter, wide), FULL),
            over1=vmem((quarter, wide), FULL),
            top=vmem((8, 1, wide), FULL),
            offset_grad=vmem((1, hidden), FULL),
            bias_grad=vmem((1, 3 * heads), FULL),
            mixed_vectors=vmem((4, 8, wide), FULL),
        )
    _, held = gradient_rows(sizes)
    held += -held % SPAN
    give(2, vmem, post_norms=post_norms, logit_scale=logit_scale)
    give(2, smem, **scalars)
    take(2, anywhere, summed_far=(held, LANES))
    take(2, vmem, loss=(1, 1), hits=(1, 1), scale_grad=(1, 1), post_grad=post_norms.shape)
    wide = sizes[0].wide
    dma = pltpu.SemaphoreType.DMA
    rings = dp_rings()
    hold(
        2,
        summed=vmem((held, LANES), FULL),
        marks=vmem((examples, 128), FULL),
        chosen=vmem((4, 4, wide), FULL),
        chosen_got=vmem((3, 4, wide), FULL),
        every=vmem((4, count, 4, wide), FULL),
        load_sems=dma((2 * len(LOADED) + 2,)),
        store_sems=dma((8,)),
        blank=vmem((8, towers[0]["tokens"].shape[1] - IMG_ROWS, wide), FULL),
        scatter_send=dma((24,)),
        scatter_recv=dma((24,)),
        gather_send=dma((24,)),
        gather_recv=dma((24,)),
        swap_send=dma((6,)),
        swap_recv=dma((6,)),
        spread_send=dma((count,)),
        spread_recv=dma((count,)),
        trade_send=dma((6,)),
        trade_recv=dma((6,)),
        ring0=rings[0],
        ring1=rings[1],
        ring2=rings[2],
        ring3=rings[3],
        ring4=rings[4],
        ring5=rings[5],
        dp_send=rings[6],
        dp_recv=rings[7],
        dp_credit=rings[8],
    )
    results = pl.pallas_call(
        functools.partial(block_kernel, count, names + out_names + scratch_names),
        out_shape=outs,
        in_specs=in_specs,
        out_specs=out_specs,
        scratch_shapes=scratch,
        compiler_params=pltpu.CompilerParams(
            collective_id=collective_id, has_side_effects=True, vmem_limit_bytes=64 << 20
        ),
        name="block",
    )(*args)
    out = [Fields(), Fields(), Fields()]
    for (index, name), value in zip(out_names, results):
        setattr(out[index], name, value)
    return out, sizes


def finish_kernel(where, names, *refs):
    r = Fields()
    for name, ref in zip(names, refs):
        setattr(r, name, ref)
    copies = []

    def move(source, target):
        copies.append(pltpu.make_async_copy(source, target, r.sems.at[len(copies)]))
        copies[-1].start()

    start, _, _ = where[0, "vectors"]
    move(r.summed.at[start : start + 40], r.vectors)
    move(r.token_grad_t, r.text_rows)
    move(r.result_t, r.text_low)
    first = len(copies)

    def weight(index, name, target):
        start, rows, width = where[index, name]
        for k in range(width // LANES):
            source = r.summed.at[start + k * rows : start + (k + 1) * rows]
            move(source, target.at[:, k * LANES : (k + 1) * LANES])

    weight(0, "contract", r.contract_i)
    weight(0, "expand", r.expand_i)
    move(r.token_grad_i, r.tokens_i)
    weight(0, "inward", r.inward_i)
    weight(0, "outward", r.outward_i)
    move(r.embed_grad_i, r.embed_i)
    move(r.result_i, r.image_result)
    weight(1, "contract", r.contract_t)
    weight(1, "expand", r.expand_t)
    weight(1, "outward", r.outward_t)
    move(r.embed_grad_t, r.embed_t)
    start, _, _ = where[1, "inward"]
    kinds, wide, heads = r.inward_t.shape
    high = wide // 2
    for k in range(kinds):
        for side in range(2):
            move(
                r.summed.at[start + k * high : start + (k + 1) * high, side * heads : (side + 1) * heads],
                r.inward_t.at[k, side * high : (side + 1) * high],
            )
    for copy in copies[:first]:
        copy.wait()
    context, examples, _ = r.tokens_t.shape
    for e in range(examples):
        r.tokens_t[:, e, :] = r.text_rows[e][0:context]
        r.text_turned[:, e, :] = r.text_low[e * TXT_ROWS : (e + 1) * TXT_ROWS].astype(FULL)[0:context]
    r.text_result[...] = r.text_turned[...].astype(LOW)
    at = 0
    for norms, shifts, offsets, biases in (
        (r.norms_i, r.shifts_i, r.offsets_i, r.biases_i),
        (r.norms_t, r.shifts_t, r.offsets_t, r.biases_t),
    ):
        count = norms.shape[1] // LANES
        rows = jnp.concatenate([r.vectors[at + 8 * k : at + 8 * k + 8, :] for k in range(count)], axis=1)
        at += 8 * count
        norms[...] = rows[0:4]
        shifts[...] = rows[4:6]
        offsets[...] = rows[6:7]
        heads = biases.shape[1]
        biases[...] = jnp.concatenate([rows[7:8, 0:heads], rows[7:8, heads : 2 * heads]], axis=0)
    for copy in copies[first:]:
        copy.wait()


def finish_call(out, where, shapes, context, biases_i, biases_t):
    names, outs, out_specs = [], [], []
    given = dict(
        summed=out[2].summed_far,
        token_grad_i=out[0].token_grad,
        token_grad_t=out[1].token_grad,
        result_i=out[0].result,
        result_t=out[1].result,
        embed_grad_i=out[0].embed_grad,
        embed_grad_t=out[1].embed_grad,
    )

    def take(space, kind=FULL, **named):
        for name, shape in named.items():
            names.append(name)
            outs.append(jax.ShapeDtypeStruct(shape, kind))
            out_specs.append(pl.BlockSpec(memory_space=space))

    for name, shape in shapes.items():
        take(pl.ANY, **{name: shape})
    examples, patch, wide_i = out[0].token_grad.shape
    wide_t = out[1].token_grad.shape[2]
    take(pl.ANY, LOW, image_result=(examples, patch, wide_i))
    take(pltpu.VMEM, LOW, text_result=(context, examples, wide_t))
    take(pltpu.VMEM, tokens_t=(context, examples, wide_t))
    for name, shape in dict(norms=4, shifts=2, offsets=1).items():
        take(pltpu.VMEM, **{name + "_i": (shape, wide_i), name + "_t": (shape, wide_t)})
    take(pltpu.VMEM, biases_i=biases_i, biases_t=biases_t)
    scratch = dict(
        vectors=pltpu.VMEM((40, LANES), FULL),
        text_rows=pltpu.VMEM(out[1].token_grad.shape, FULL),
        text_low=pltpu.VMEM(out[1].result.shape, LOW),
        text_turned=pltpu.VMEM((context, examples, wide_t), FULL),
        sems=pltpu.SemaphoreType.DMA((48,)),
    )
    results = pl.pallas_call(
        functools.partial(finish_kernel, where, list(given) + names + list(scratch)),
        out_shape=outs,
        in_specs=[pl.BlockSpec(memory_space=pl.ANY)] * len(given),
        out_specs=out_specs,
        scratch_shapes=list(scratch.values()),
        compiler_params=pltpu.CompilerParams(vmem_limit_bytes=62 << 20),
        name="finish",
    )(*given.values())
    fields = Fields()
    for name, value in zip(names, results):
        setattr(fields, name, value)
    return fields


def shards(
    count,
    image_tokens,
    image_norms,
    image_inward,
    image_biases,
    image_outward,
    image_shifts,
    image_expand,
    image_offsets,
    image_contract,
    image_embed,
    text_tokens,
    text_norms,
    text_inward,
    text_biases,
    text_outward,
    text_shifts,
    text_expand,
    text_offsets,
    text_contract,
    text_embed,
    post_norms,
    logit_scale,
    image_cotangent,
    text_cotangent,
    resolution,
    validity,
    text_ends,
):
    examples, patch, image_width = image_tokens.shape
    context, text_width = text_tokens.shape[1:]

    def fit(values):
        grow = ((0, 0), (0, TXT_ROWS - context), (0, 0))
        return jnp.pad(values, grow).reshape(-1, values.shape[2])

    image = dict(
        tokens=image_tokens,
        inward=jnp.swapaxes(image_inward, 1, 2),
        outward=image_outward,
        expand=image_expand,
        contract=image_contract,
        embed=image_embed,
        cotangent=image_cotangent,
        norms=image_norms,
        biases=image_biases,
        shifts=image_shifts,
        offsets=image_offsets.reshape(1, -1),
    )
    text = dict(
        tokens=fit(text_tokens),
        inward=text_inward,
        outward=text_outward,
        expand=text_expand,
        contract=text_contract,
        embed=text_embed,
        cotangent=fit(text_cotangent),
        norms=text_norms,
        biases=text_biases,
        shifts=text_shifts,
        offsets=text_offsets.reshape(1, -1),
    )
    scalars = dict(resolution=resolution, validity=validity, ends=text_ends)
    out, sizes = block_call(
        count, (image, text), post_norms, logit_scale.reshape(1, 1), scalars, 0
    )
    where, _ = gradient_rows(sizes)
    shapes = dict(
        contract_i=image_contract.shape,
        expand_i=image_expand.shape,
        outward_i=image_outward.shape,
        inward_i=(image_inward.shape[0] * image_inward.shape[2], image_width),
        embed_i=image_embed.shape,
        tokens_i=image_tokens.shape,
        contract_t=text_contract.shape,
        expand_t=text_expand.shape,
        outward_t=text_outward.shape,
        inward_t=text_inward.shape,
        embed_t=text_embed.shape,
    )
    end = finish_call(out, where, shapes, context, image_biases.shape, text_biases.shape)
    inward_i = end.inward_i.reshape(image_inward.shape[0], -1, image_width)
    return (
        end.image_result,
        jnp.swapaxes(end.text_result, 0, 1),
        out[2].loss.reshape(1),
        out[2].hits.reshape(1),
        end.tokens_i,
        jnp.swapaxes(end.tokens_t, 0, 1),
        end.norms_i,
        jnp.swapaxes(inward_i, 1, 2),
        end.biases_i,
        end.outward_i,
        end.shifts_i,
        end.expand_i,
        end.offsets_i.reshape(-1),
        end.contract_i,
        end.embed_i,
        end.norms_t,
        end.inward_t,
        end.biases_t,
        end.outward_t,
        end.shifts_t,
        end.expand_t,
        end.offsets_t.reshape(-1),
        end.contract_t,
        end.embed_t,
        out[2].post_grad,
        out[2].scale_grad.reshape(1),
    )


def solution(mesh):
    placed = (
        P("dp", None, None),
        P(),
        P(None, None, "mp"),
        P(None, "mp"),
        P("mp", None),
        P(),
        P(None, "mp"),
        P("mp"),
        P("mp", None),
        P(),
        P("dp", None, None),
        P(),
        P(None, None, "mp"),
        P(None, "mp"),
        P("mp", None),
        P(),
        P(None, "mp"),
        P("mp"),
        P("mp", None),
        P(),
        P(),
        P(),
        P("dp", None, None),
        P("dp", None, None),
        P("dp"),
        P("dp"),
        P("dp"),
    )
    return jax.shard_map(
        functools.partial(shards, mesh.shape["dp"]),
        mesh=mesh,
        in_specs=placed,
        out_specs=(
            P("dp", None, None),
            P("dp", None, None),
            P(),
            P(),
            P("dp", None, None),
            P("dp", None, None),
            P(),
            P(None, None, "mp"),
            P(None, "mp"),
            P("mp", None),
            P(),
            P(None, "mp"),
            P("mp"),
            P("mp", None),
            P(),
            P(),
            P(None, None, "mp"),
            P(None, "mp"),
            P("mp", None),
            P(),
            P(None, "mp"),
            P("mp"),
            P("mp", None),
            P(),
            P(),
            P(),
        ),
        check_vma=False,
    )
```

```python
import functools

import jax
import jax.numpy as jnp
from jax import lax
from jax.experimental import pallas as pl
from jax.experimental.pallas import tpu as pltpu
from jax.sharding import PartitionSpec as P

MESH = pl.DeviceIdType.MESH
HEAD = 64
LOW_LEN = 50
HIGH_LEN = 101
IMG_ROWS = 104
TXT_ROWS = 80
SPAN = 256
SLOTS = 4
LANES = 256

EPSILON = 1e-05
MASKED = -1000000000.0
HIGHEST = lax.Precision.HIGHEST


def dp_sum_machine(count, blocks, total, rings, sends, recvs, credits):
    places = count // 2
    deep = places // 2
    dp, mp = lax.axis_index("dp"), lax.axis_index("mp")
    side, place = lax.rem(dp, 2), dp // 2
    low = place < deep
    depth = jnp.where(low, place, places - 1 - place)
    inner = jnp.where(low, place + 1, place - 1)
    outer = jnp.clip(jnp.where(low, place - 1, place + 1), 0, places - 1)
    half = jnp.where(low, 0, 1)
    pair_id = (place * 2 + 1 - side, mp)
    inner_id = (inner * 2 + side, mp)
    outer_id = (outer * 2 + side, mp)
    quarter = SPAN // 4

    def part(offset, size):
        def at(block):
            start = pl.multiple_of(block * SPAN + offset, quarter)
            return total.at[pl.ds(start, size)]

        return at

    kept = part(side * quarter, quarter)
    given = part((1 - side) * quarter, quarter)
    whole = part(2 * quarter, 2 * quarter)
    mid_kept = part((2 + half) * quarter, quarter)
    mid_given = part((3 - half) * quarter, quarter)
    middle = depth == deep - 1
    not_middle = depth < deep - 1
    not_end = depth > 0
    yes = depth >= 0

    kinds = [
        (yes, 0, given, pair_id, yes, 0, pair_id, rings[0], kept),
        (not_middle, depth, whole, inner_id, not_end, depth - 1, outer_id, rings[1], whole),
        (not_middle, depth + 1, kept, inner_id, not_end, depth, outer_id, rings[2], kept),
        (middle, deep - 1, mid_given, inner_id, middle, deep - 1, inner_id, rings[3], mid_kept),
        (middle, deep, mid_kept, pair_id, middle, deep, pair_id, rings[4], mid_kept),
        (middle, deep, kept, inner_id, middle, deep, inner_id, rings[5], kept),
        (middle, deep + 1, mid_kept, inner_id, middle, deep + 1, inner_id, None, mid_given),
        (not_end, 2 * deep - depth, kept, outer_id, not_middle, 2 * deep - depth - 1, inner_id, None, kept),
        (not_end, 2 * deep + 1 - depth, whole, outer_id, not_middle, 2 * deep - depth, inner_id, None, whole),
        (yes, 2 * deep, kept, pair_id, yes, 2 * deep, pair_id, None, given),
    ]

    def copy(k, kind, block):
        _, _, src, target, _, _, _, ring, land = kind
        slot = lax.rem(block, SLOTS)
        dst = src(block) if ring is None else ring.at[slot]
        return pltpu.make_async_remote_copy(
            src_ref=src(block),
            dst_ref=dst,
            send_sem=sends.at[k, slot],
            recv_sem=recvs.at[k, slot],
            device_id=target,
            device_id_type=MESH,
        )

    def valid(block):
        return jnp.logical_and(block >= 0, block < blocks)

    def start(t):
        for k, kind in enumerate(kinds):
            block = t - 2 * kind[1]

            @pl.when(jnp.logical_and(kind[0], valid(block)))
            def _():
                @pl.when(block >= SLOTS)
                def _():
                    pl.semaphore_wait(credits.at[k], 1)

                copy(k, kind, block).start()

    def finish(t):
        for k, kind in enumerate(kinds):
            sends_it, sent_stage, _, _, takes_it, got_stage, source, ring, land = kind
            sent = t - 2 * sent_stage
            got = t - 2 * got_stage

            @pl.when(jnp.logical_and(sends_it, valid(sent)))
            def _():
                copy(k, kind, sent).wait_send()

            @pl.when(jnp.logical_and(takes_it, valid(got)))
            def _():
                copy(k, kind, got).wait_recv()
                if ring is not None:
                    here = land(got)
                    here[...] = here[...] + ring[lax.rem(got, SLOTS)]

                @pl.when(got < blocks - SLOTS)
                def _():
                    pl.semaphore_signal(credits.at[k], inc=1, device_id=source, device_id_type=MESH)

    def tick(t):
        start(t)

        @pl.when(t > 0)
        def _():
            finish(t - 1)

    return tick, blocks + 4 * deep + 1


def dp_rings():
    quarter = SPAN // 4
    sizes = [quarter, 2 * quarter, quarter, quarter, quarter, quarter]
    return [pltpu.VMEM((SLOTS, size, LANES), jnp.float32) for size in sizes] + [
        pltpu.SemaphoreType.DMA((10, SLOTS)),
        pltpu.SemaphoreType.DMA((10, SLOTS)),
        pltpu.SemaphoreType.REGULAR((10,)),
    ]


LOW, FULL = jnp.bfloat16, jnp.float32


def mm(left, right):
    return jnp.dot(left, right, preferred_element_type=FULL)


def mm_nt(left, right, precision=None):
    dims = (((1,), (1,)), ((), ()))
    return lax.dot_general(left, right, dims, precision=precision, preferred_element_type=FULL)


def mm_tn(left, right, precision=None):
    dims = (((0,), (0,)), ((), ()))
    return lax.dot_general(left, right, dims, precision=precision, preferred_element_type=FULL)


def row_sum(values):
    return jnp.sum(values, axis=1, keepdims=True)


def col_sum(values):
    return jnp.sum(values, axis=0, keepdims=True)


def whitened(values):
    width = values.shape[1]
    centred = values - row_sum(values) * (1.0 / width)
    scale = lax.rsqrt(row_sum(centred * centred) * (1.0 / width) + EPSILON)
    return centred * scale, scale


def whitened_back(white, scale, gain, gradient):
    width = white.shape[1]
    inner = gradient * gain
    mean = row_sum(inner) * (1.0 / width)
    slope = row_sum(inner * white) * (1.0 / width)
    return scale * (inner - mean - white * slope)


class Fields:
    pass


class Tower:
    def __init__(self, index, rows, per, fields):
        self.__dict__.update(fields.__dict__)
        self.index, self.rows, self.per = index, rows, per
        self.wide = self.shifts.shape[1]
        self.across_heads = self.biases.shape[1]
        self.hidden = self.offsets.shape[1]
        self.panels = self.wide // LANES

    def at(self, owner):
        return pl.ds(pl.multiple_of(owner * self.rows, self.rows), self.rows)

    def token_place(self, owner):
        return self.token_grad.at[pl.ds(2 * owner, 2), pl.ds(0, self.per)]


def gradient_rows(towers):
    image, text = towers
    where, start = {}, 0
    for tower, name, rows in (
        (text, "contract", text.hidden),
        (text, "expand", text.wide),
        (image, "contract", image.hidden),
        (image, "expand", image.wide),
        (text, "outward", text.across_heads),
        (text, "inward", 3 * text.across_heads),
        (image, "outward", image.across_heads),
        (image, "inward", 3 * image.across_heads),
        (image, "vectors", 8),
        (text, "vectors", 8),
    ):
        width = tower.hidden if name == "expand" else tower.wide
        where[tower.index, name] = (start, rows, width)
        start += rows * (width // LANES)
    return where, start


def block_kernel(count, names, *refs):
    fields = [Fields(), Fields(), Fields()]
    for (index, name), ref in zip(names, refs):
        setattr(fields[index], name, ref)
    image = Tower(0, 2 * IMG_ROWS, IMG_ROWS, fields[0])
    text = Tower(1, 2 * TXT_ROWS, TXT_ROWS, fields[1])
    r = fields[2]
    places, _ = gradient_rows((image, text))
    deep = count // 4
    dp, mp = lax.axis_index("dp"), lax.axis_index("mp")
    flip, core_bit = mp // 2, lax.rem(mp, 2)
    core_mp = flip * 2 + 1 - core_bit
    across_mp = (1 - flip) * 2 + core_bit
    diag_mp = (1 - flip) * 2 + 1 - core_bit
    core, across, diag = (dp, core_mp), (dp, across_mp), (dp, diag_mp)
    own_mp = mp

    for tower in (text, image):
        tower.loads = {}
    for k, name in enumerate(LOADED):
        for tower in (text, image):
            source, target = getattr(tower, name + FAR), getattr(tower, name)
            copy = pltpu.make_async_copy(source, target, r.load_sems.at[2 * k + tower.index])
            copy.start()
            tower.loads[name] = copy
    r.blank[...] = jnp.zeros(r.blank.shape, FULL)
    blank_store = pltpu.make_async_copy(
        r.blank,
        image.token_grad.at[:, pl.ds(image.per, image.token_grad.shape[1] - image.per)],
        r.store_sems.at[7],
    )
    blank_store.start()
    barrier = pltpu.get_barrier_semaphore()
    friends = [core, across, diag] + [(lax.rem(dp + k, count), mp) for k in range(1, count)]
    for friend in friends:
        pl.semaphore_signal(barrier, inc=1, device_id=friend, device_id_type=MESH)
    pl.semaphore_wait(barrier, len(friends))

    scatter_sems = r.scatter_send, r.scatter_recv
    gather_sems = r.gather_send, r.gather_recv
    swap_sems = r.swap_send, r.swap_recv
    spread_sems = r.spread_send, r.spread_recv
    trade_sems = r.trade_send, r.trade_recv

    def remote(src, dst, group, k, peer):
        return pltpu.make_async_remote_copy(
            src_ref=src,
            dst_ref=dst,
            send_sem=group[0].at[k],
            recv_sem=group[1].at[k],
            device_id=peer,
            device_id_type=MESH,
        )

    class Scatter:
        def __init__(self, tower, phase, bank):
            self.tower = tower
            self.parts, self.near_buf, self.over_buf = (
                (tower.parts1, tower.near1, tower.over1)
                if bank
                else (tower.parts0, tower.near0, tower.over0)
            )
            k = (phase * 2 + tower.index) * 3
            self.far = remote(self.parts.at[tower.at(diag_mp)], self.near_buf.at[0], scatter_sems, k, core)
            self.near = remote(self.parts.at[tower.at(core_mp)], self.near_buf.at[1], scatter_sems, k + 1, core)
            self.over = remote(self.near_buf.at[0], self.over_buf, scatter_sems, k + 2, across)

        def send_over(self):
            self.far.wait()
            self.near_buf[0] = self.near_buf[0] + self.parts[self.tower.at(across_mp), :]
            self.over.start()

        def result(self):
            self.near.wait()
            self.over.wait()
            return self.parts[self.tower.at(own_mp), :] + self.near_buf[1] + self.over_buf[...]

    class Gather:
        def __init__(self, tower, phase):
            k = (phase * 2 + tower.index) * 3
            if phase == 2:
                source, mine, passed = (
                    tower.back,
                    tower.token_place(own_mp),
                    tower.token_place(across_mp),
                )
            else:
                mine = source = tower.carried.at[tower.at(own_mp)]
                passed = tower.carried.at[tower.at(across_mp)]
            self.one = remote(source, mine, gather_sems, k, across)
            self.two = remote(source, mine, gather_sems, k + 1, core)
            self.on = remote(passed, passed, gather_sems, k + 2, core)

        def start(self):
            self.one.start()
            self.two.start()

        def got_core(self):
            self.two.wait_recv()

        def got_across(self):
            self.one.wait_recv()
            self.on.start()

        def got_diag(self):
            self.on.wait_recv()

        def sent(self):
            self.one.wait_send()
            self.two.wait_send()
            self.on.wait_send()

    def length(example):
        return jnp.where(r.resolution[example] == 1, HIGH_LEN, LOW_LEN)

    def live(tower, owner, places_):
        if tower is text:
            return None
        first, second = length(2 * owner), length(2 * owner + 1) + tower.per
        return places_ < jnp.where(places_ < tower.per, first, second)

    def allowed(tower, owner):
        shape = (tower.rows, tower.rows)
        query = lax.broadcasted_iota(jnp.int32, shape, 0)
        key = lax.broadcasted_iota(jnp.int32, shape, 1)
        key_start = jnp.where(query < tower.per, 0, tower.per)
        if tower is text:
            end = query + 1
        else:
            first, second = length(2 * owner), length(2 * owner + 1) + tower.per
            end = jnp.where(query < tower.per, first, second)
        return jnp.logical_and(key >= key_start, key < end)

    def chosen_places(tower, owner):
        if tower is text:
            return r.ends[2 * owner], r.ends[2 * owner + 1] + tower.per
        return 0, tower.per

    def chosen_row(tower, example, read):
        first = example * tower.per
        if tower is image:
            return read(first, 16)[0:1]
        place = lax.broadcasted_iota(jnp.int32, (tower.per, 1), 0)
        rows = read(first, tower.per)
        return col_sum(jnp.where(place == r.ends[example], rows, 0.0))

    def softmax(tower, scores, mask):
        scores = jnp.where(mask, scores * HEAD ** (-0.5), MASKED)
        top = jnp.max(scores, axis=1, keepdims=True)
        weights = jnp.exp(scores - top)
        return weights * (1.0 / row_sum(weights))

    def owner_of(j):
        return lax.rem(flip + 1 - j // 2, 2) * 2 + lax.rem(core_bit + 1 - lax.rem(j, 2), 2)

    def prepare(tower):
        for name in ("tokens", "inward", "outward"):
            tower.loads[name].wait()
        heads = tower.across_heads
        if tower is text:
            for k in range(3):
                tower.joined[:, k * heads : (k + 1) * heads] = tower.inward[k]
        tower.bias_row[:, 0:heads] = tower.biases[0:1, :]
        tower.bias_row[:, heads : 2 * heads] = jnp.zeros((1, heads), FULL)
        tower.bias_row[:, 2 * heads : 3 * heads] = tower.biases[1:2, :]

    def rows_of(tower, owner):
        if tower is text:
            return tower.tokens[tower.at(owner), :].astype(FULL)
        pair = [tower.tokens[2 * owner + k].astype(FULL)[0 : tower.per] for k in range(2)]
        return jnp.concatenate(pair, axis=0)

    def into_heads(tower, normed):
        if tower is text:
            return mm(normed, tower.joined[...])
        return mm_nt(normed, tower.inward[...].reshape(3 * tower.across_heads, tower.wide))

    def out_of_heads(tower, grads):
        if tower is text:
            return mm_nt(grads, tower.joined[...])
        return mm(grads, tower.inward[...].reshape(3 * tower.across_heads, tower.wide))

    def attend(tower, owner):
        at, heads = tower.at(owner), tower.across_heads
        white, _ = whitened(rows_of(tower, owner))
        normed = (white * tower.norms[0:1, :] + tower.norms[1:2, :]).astype(LOW)
        tower.normed[at, :] = normed
        qkv = (into_heads(tower, normed) + tower.bias_row[...]).astype(LOW)
        tower.qkv[at, :] = qkv
        mask = allowed(tower, owner)
        mixed = []
        for h in range(heads // HEAD):
            query, key, value = (
                qkv[:, k * heads + h * HEAD : k * heads + (h + 1) * HEAD] for k in range(3)
            )
            weights = softmax(tower, mm_nt(query, key), mask)
            mixed.append(mm(weights.astype(LOW), value).astype(LOW))
        mixed = jnp.concatenate(mixed, axis=1)
        tower.mixed[at, :] = mixed
        tower.parts0[at, :] = mm(mixed, tower.outward[...])

    def attend_all(tower, scatter):
        def body(j, carry):
            attend(tower, owner_of(j))

            @pl.when(j == 0)
            def _():
                scatter.far.start()

            if tower is text:

                @pl.when(j == 1)
                def _():
                    scatter.send_over()

            @pl.when(j == 2)
            def _():
                scatter.near.start()

            return carry

        lax.fori_loop(0, 4, body, 0)
        tower.own_tokens[...] = rows_of(tower, own_mp).astype(LOW)

    def second_norm(tower, scatter):
        at = tower.at(own_mp)
        mine = tower.own_tokens[...].astype(FULL)
        resid = mine + scatter.result() + tower.shifts[0:1, :]
        tower.resid[...] = resid
        white, _ = whitened(resid)
        normed = (white * tower.norms[2:3, :] + tower.norms[3:4, :]).astype(LOW)
        tower.carried[at, :] = normed.astype(FULL)

    def feed(tower, owner):
        at = tower.at(owner)
        normed = tower.carried[at, :].astype(LOW)
        tower.normed_two[at, :] = normed
        hidden = mm(normed, tower.expand[...]) + tower.offsets[...]
        gate = 1.0 / (1.0 + jnp.exp(-1.702 * hidden))
        active = (hidden * gate).astype(LOW)
        tower.active[at, :] = active
        tower.slope[at, :] = (gate * (1.0 + 1.702 * hidden * (1.0 - gate))).astype(LOW)
        tower.parts1[at, :] = mm(active, tower.contract[...])

    scatters = [[Scatter(t, phase, phase == 1) for t in (image, text)] for phase in range(4)]
    gathers = [[Gather(t, phase) for t in (image, text)] for phase in range(4)]

    every = r.every
    peers = (core, across, diag)

    def swap_all(buffer, tower, step):
        mine = buffer.at[own_mp]
        copies = [
            remote(mine, mine, swap_sems, (2 * step + tower.index) * 3 + k, peer)
            for k, peer in enumerate(peers)
        ]
        for copy in copies:
            copy.start()
        return copies

    def sum_of(buffer):
        return buffer[0] + buffer[1] + buffer[2] + buffer[3]

    def chosen_first(tower):
        def token_rows(first, rows):
            if tower is image:
                return tower.tokens[first // tower.per, 0:rows, :].astype(FULL)
            return tower.tokens[first : first + rows, :].astype(FULL)

        def part_rows(first, rows):
            return tower.parts0[first : first + rows, :]

        for e in range(8):
            tower.first[own_mp, e : e + 1, :] = chosen_row(tower, e, part_rows)
            tower.early[e : e + 1, :] = chosen_row(tower, e, token_rows) + tower.shifts[0:1, :]
        return swap_all(tower.first, tower, 0)

    def chosen_second(tower, copies):
        for copy in copies:
            copy.wait()
        resid = tower.early[...] + sum_of(tower.first)
        tower.early[...] = resid
        white, _ = whitened(resid)
        normed = (white * tower.norms[2:3, :] + tower.norms[3:4, :]).astype(LOW)
        hidden = mm(normed, tower.expand[...]) + tower.offsets[...]
        active = (hidden * (1.0 / (1.0 + jnp.exp(-1.702 * hidden)))).astype(LOW)
        tower.second[own_mp] = mm(active, tower.contract[...])
        return swap_all(tower.second, tower, 1)

    def chosen_third(tower, copies):
        for copy in copies:
            copy.wait()
        final = tower.early[...] + sum_of(tower.second) + tower.shifts[1:2, :]
        for e in range(8):
            tower.top[e] = final[e : e + 1]
        for k in range(2):
            spot = 2 * tower.index + k
            every[own_mp, dp, spot : spot + 1, 0 : tower.wide] = tower.top[2 * own_mp + k]

    prepare(text)
    attend_all(text, scatters[0][1])
    prepare(image)
    attend_all(image, scatters[0][0])
    swaps = [chosen_first(tower) for tower in (image, text)]
    second_norm(text, scatters[0][1])
    for tower in (text, image):
        reload = pltpu.make_async_copy(
            tower.cotangent_far, tower.tokens, r.load_sems.at[2 * len(LOADED) + tower.index]
        )
        tower.loads["cotangent"] = reload
        reload.start()
        tower.loads["expand"].wait()
        tower.loads["contract"].wait()
    swaps = [chosen_second(tower, swaps[tower.index]) for tower in (image, text)]
    gathers[0][1].start()
    feed(text, own_mp)
    for k in range(2):
        mark = r.validity[2 * own_mp + k].astype(FULL)
        every[own_mp, dp, 2 + k : 3 + k, text.wide : text.wide + 128] = jnp.full((1, 128), mark, FULL)
    for tower in (image, text):
        chosen_third(tower, swaps[tower.index])
    mine = every.at[own_mp, dp]
    spread = [
        remote(mine, mine, spread_sems, k, (lax.rem(dp + k, count), mp)) for k in range(1, count)
    ]
    for copy in spread:
        copy.start()
    gathers[0][1].got_core()
    feed(text, core_mp)
    for copy in spread:
        copy.wait()
    one = remote(every.at[own_mp], every.at[own_mp], swap_sems, 12, across)
    two = remote(every.at[own_mp], every.at[own_mp], swap_sems, 13, core)
    on = remote(every.at[across_mp], every.at[across_mp], swap_sems, 14, core)
    one.start()
    two.start()
    scatters[0][0].send_over()
    gathers[0][1].got_across()
    feed(text, across_mp)
    one.wait_recv()
    on.start()
    gathers[0][1].got_diag()
    feed(text, diag_mp)
    two.wait_recv()
    on.wait_recv()
    for copy in (one, two, on):
        copy.wait_send()

    for place in range(count):
        for quarter in range(4):
            spot = (place * 4 + quarter) * 2
            block = every[quarter, place]
            image.every_row[spot : spot + 2, :] = block[0:2, :]
            text.every_row[spot : spot + 2, :] = block[2:4, 0 : text.wide]
            r.marks[spot : spot + 2, :] = block[2:4, text.wide : text.wide + 128]
    for tower in (text, image):
        tower.loads["embed"].wait()
    post = r.post_norms

    def head(tower, rows):
        lanes = slice(0, image.wide) if tower is image else slice(image.wide, image.wide + text.wide)
        white, scale = whitened(rows)
        low = (white * post[0:1, lanes] + post[1:2, lanes]).astype(LOW)
        raw = mm(low, tower.embed[...])
        inverse = lax.rsqrt(row_sum(raw * raw) + 1e-06)
        return lanes, white, scale, low, raw * inverse, inverse

    heads = [head(tower, tower.every_row[...]) for tower in (image, text)]
    unit_i, unit_t = heads[0][4], heads[1][4]
    marks = r.marks[...]
    examples = marks.shape[0]
    valid_col = marks[:, 0:1]
    valid_row = jnp.transpose(marks)[0:1, :]
    number = col_sum(valid_col)
    factor = jnp.exp(r.logit_scale[...])
    logits = factor * mm_nt(unit_i, unit_t, HIGHEST)
    by_row = jnp.where(valid_row > 0.5, logits, MASKED)
    by_col = jnp.where(valid_col > 0.5, logits, MASKED)
    row_top = jnp.max(by_row, axis=1, keepdims=True)
    row_lse = row_top + jnp.log(row_sum(jnp.exp(by_row - row_top)))
    col_top = jnp.max(by_col, axis=0, keepdims=True)
    col_lse = col_top + jnp.log(col_sum(jnp.exp(by_col - col_top)))
    diagonal = factor * row_sum(unit_i * unit_t)
    loss = col_sum(valid_col * (row_lse - 2.0 * diagonal)) + row_sum(valid_row * col_lse)
    r.loss[...] = loss / (2.0 * number)
    r.hits[...] = col_sum(valid_col * jnp.exp(diagonal - row_lse))
    row_id = lax.broadcasted_iota(jnp.int32, (examples, examples), 0)
    col_id = lax.broadcasted_iota(jnp.int32, (examples, examples), 1)
    same = jnp.where(row_id == col_id, 1.0, 0.0)
    pairs = (
        valid_col * (jnp.exp(by_row - row_lse) - same)
        + valid_row * (jnp.exp(by_col - col_lse) - same)
    ) / (2.0 * number)
    r.scale_grad[...] = col_sum(row_sum(pairs * logits))
    unit_grads = [
        factor * lax.dot(pairs, unit_t, precision=HIGHEST, preferred_element_type=FULL),
        factor * mm_tn(pairs, unit_i, HIGHEST),
    ]
    stores = []
    for tower, (lanes, white, scale, low, unit, inverse), grad in zip((image, text), heads, unit_grads):
        raw_grad = (inverse * (grad - unit * row_sum(unit * grad))).astype(LOW)
        spare = tower.parts1 if tower is image else tower.parts0
        home = spare.at[0 : tower.wide, 0 : tower.embed.shape[1]]
        home[...] = mm_tn(low, raw_grad)
        stores.append(pltpu.make_async_copy(home, tower.embed_grad, r.store_sems.at[tower.index]))
        stores[-1].start()
        low_grad = mm_nt(raw_grad, tower.embed[...])
        r.post_grad[0:1, lanes] = col_sum(low_grad * white)
        r.post_grad[1:2, lanes] = col_sum(low_grad)
        tower.every_row[...] = whitened_back(white, scale, post[0:1, lanes], low_grad)
        own = tower.every_row[pl.ds(pl.multiple_of(dp * 8, 8), 8), :]
        for k in range(8):
            tower.top[k] = own[k : k + 1, :]

    def grad_rows(tower, owner):
        place = lax.broadcasted_iota(jnp.int32, (tower.rows, 1), 0)
        values = rows_of(tower, owner)
        alive = live(tower, owner, place)
        if alive is not None:
            values = jnp.where(alive, values, 0.0)
        for k, at in enumerate(chosen_places(tower, owner)):
            values = values + jnp.where(place == at, tower.top[2 * owner + k], 0.0)
        return values

    def feed_back(tower, j, scatter):
        owner = owner_of(j)
        at = tower.at(owner)
        low = grad_rows(tower, owner).astype(LOW)
        tower.low_grad[at, :] = low
        active_grad = mm_nt(low, tower.contract[...]).astype(LOW).astype(FULL)
        hidden_grad = active_grad * tower.slope[at, :].astype(FULL)
        tower.offset_grad[...] = tower.offset_grad[...] + col_sum(hidden_grad)
        hidden_low = hidden_grad.astype(LOW)
        tower.slope[at, :] = hidden_low
        tower.parts0[at, :] = mm_nt(hidden_low, tower.expand[...])

        @pl.when(j == 0)
        def _():
            scatter.far.start()

        @pl.when(j == 2)
        def _():
            scatter.near.start()

    def put_back(tower, values):
        tower.back[...] = values.reshape(2, tower.per, tower.wide)

    def get_back(tower):
        return tower.back[...].reshape(tower.rows, tower.wide)

    summed = r.summed

    def put(tower, name, values, first=0):
        start, rows, width = places[tower.index, name]
        for k in range(width // LANES):
            to = pl.ds(pl.multiple_of(start + k * rows + first, 8), values.shape[0])
            summed[to, :] = values[:, k * LANES : (k + 1) * LANES]

    def outer(tower, name, left, right):
        def body(j, carry):
            cut = pl.ds(pl.multiple_of(j * LANES, LANES), LANES)
            put(tower, name, mm_tn(left[:, cut], right[...]), j * LANES)
            return carry

        lax.fori_loop(0, left.shape[1] // LANES, body, 0)

    rings = [r.ring0, r.ring1, r.ring2, r.ring3, r.ring4, r.ring5]
    tick, ticks = dp_sum_machine(
        count, summed.shape[0] // SPAN, summed, rings, r.dp_send, r.dp_recv, r.dp_credit
    )
    out_copy = pltpu.make_async_copy(summed, r.summed_far, r.store_sems.at[4])
    clock = [0]

    def go(number):
        def body(t, carry):
            tick(t)
            done = t - 1 - 4 * deep

            @pl.when(done >= 0)
            def _():
                at = pl.ds(pl.multiple_of(done * SPAN, SPAN), SPAN)
                pltpu.make_async_copy(
                    summed.at[at], r.summed_far.at[at], r.store_sems.at[4]
                ).start()

            return carry

        lax.fori_loop(clock[0], clock[0] + number, body, 0)
        clock[0] += number

    def until(number):
        go(number - clock[0])

    for copy in stores:
        copy.wait()
    for tower in (image, text):
        tower.loads["cotangent"].wait()
        tower.offset_grad[...] = jnp.zeros(tower.offset_grad.shape, FULL)
        tower.bias_grad[...] = jnp.zeros(tower.bias_grad.shape, FULL)
        grads = grad_rows(tower, own_mp)
        put_back(tower, grads)
        tower.mixed_vectors[own_mp] = jnp.zeros((8, tower.wide), FULL)
        tower.mixed_vectors[own_mp, 5:6, :] = col_sum(grads)

    def feed_back_loop(tower, first, last, scatter):
        def body(j, carry):
            feed_back(tower, j, scatter)
            return carry

        lax.fori_loop(first, last, body, 0)

    gathers[0][1].sent()
    feed_back_loop(text, 0, 4, scatters[2][1])
    outer(text, "contract", text.active, text.low_grad)
    outer(text, "expand", text.normed_two, text.slope)
    until(2)
    second_norm(image, scatters[0][0])
    gathers[0][0].start()
    scatters[2][1].send_over()
    feed(image, own_mp)
    until(3)
    gathers[0][0].got_core()
    feed(image, core_mp)
    until(5)
    gathers[0][0].got_across()
    feed(image, across_mp)
    gathers[0][0].got_diag()
    feed(image, diag_mp)
    gathers[0][0].sent()
    until(6)
    feed_back_loop(image, 0, 2, scatters[2][0])
    scatters[2][0].send_over()
    feed_back_loop(image, 2, 4, scatters[2][0])
    until(7)
    outer(image, "contract", image.active, image.low_grad)
    until(8)
    outer(image, "expand", image.normed_two, image.slope)

    def second_norm_back(tower, scatter, gather):
        normed_grad = scatter.result()
        white, scale = whitened(tower.resid[...])
        vectors = tower.mixed_vectors
        vectors[own_mp, 2:3, :] = col_sum(normed_grad * white)
        vectors[own_mp, 3:4, :] = col_sum(normed_grad)
        grads = get_back(tower) + whitened_back(white, scale, tower.norms[2:3, :], normed_grad)
        vectors[own_mp, 4:5, :] = col_sum(grads)
        put_back(tower, grads)
        tower.carried[tower.at(own_mp), :] = grads.astype(LOW).astype(FULL)
        gather.start()

    def attend_back(tower, owner):
        at, heads = tower.at(owner), tower.across_heads
        low = tower.carried[at, :].astype(LOW)
        tower.low_grad[at, :] = low
        mixed_grad = mm_nt(low, tower.outward[...]).astype(LOW)
        qkv = tower.qkv[at, :]
        mask = allowed(tower, owner)
        grads = [[], [], []]
        for h in range(heads // HEAD):
            query, key, value = (
                qkv[:, k * heads + h * HEAD : k * heads + (h + 1) * HEAD] for k in range(3)
            )
            weights = softmax(tower, mm_nt(query, key), mask)
            grad = mixed_grad[:, h * HEAD : (h + 1) * HEAD]
            weight_grad = mm_nt(grad, value)
            grads[2].append(mm_tn(weights.astype(LOW), grad))
            score_grad = weights * (weight_grad - row_sum(weight_grad * weights))
            score_grad = score_grad.astype(LOW)
            grads[0].append(mm(score_grad, key) * HEAD ** (-0.5))
            grads[1].append(mm_tn(score_grad, query) * HEAD ** (-0.5))
        joined = jnp.concatenate([part for kind in grads for part in kind], axis=1)
        tower.bias_grad[...] = tower.bias_grad[...] + col_sum(joined)
        low = joined.astype(LOW)
        tower.qkv[at, :] = low
        tower.parts0[at, :] = out_of_heads(tower, low)

    def outer_attention(tower):
        heads = tower.across_heads
        put(tower, "outward", mm_tn(tower.mixed[...], tower.low_grad[...]))
        for k in range(3):
            grads = tower.qkv[:, k * heads : (k + 1) * heads]
            if tower is image:
                put(tower, "inward", mm_tn(grads, tower.normed[...]), k * heads)
            else:
                part = mm_tn(tower.normed[...], grads)
                start, rows, _ = places[tower.index, "inward"]
                high = tower.wide // 2
                for side in range(2):
                    summed[start + k * high : start + (k + 1) * high, side * heads : (side + 1) * heads] = (
                        part[side * high : (side + 1) * high]
                    )

    second_norm_back(text, scatters[2][1], gathers[1][1])
    attend_back(text, own_mp)
    until(9)
    gathers[1][1].got_core()
    attend_back(text, core_mp)
    scatters[3][1].near.start()
    until(10)
    second_norm_back(image, scatters[2][0], gathers[1][0])
    attend_back(image, own_mp)
    until(11)
    gathers[1][0].got_core()
    attend_back(image, core_mp)
    scatters[3][0].near.start()
    until(12)
    gathers[1][1].got_across()
    attend_back(text, across_mp)
    until(13)
    gathers[1][1].got_diag()
    attend_back(text, diag_mp)
    scatters[3][1].far.start()
    until(14)
    gathers[1][1].sent()
    scatters[3][1].send_over()
    until(15)
    gathers[1][0].got_across()
    attend_back(image, across_mp)
    until(16)
    gathers[1][0].got_diag()
    attend_back(image, diag_mp)
    scatters[3][0].far.start()
    until(17)
    gathers[1][0].sent()
    scatters[3][0].send_over()
    for scatter in scatters[1]:
        scatter.far.start()
        scatter.near.start()
    outer_attention(text)
    until(18)
    outer_attention(image)
    until(19)

    def first_norm_back(tower, scatter, gather):
        normed_grad = scatter.result()
        white, scale = whitened(tower.own_tokens[...].astype(FULL))
        vectors = tower.mixed_vectors
        vectors[own_mp, 0:1, :] = col_sum(normed_grad * white)
        vectors[own_mp, 1:2, :] = col_sum(normed_grad)
        more = whitened_back(white, scale, tower.norms[0:1, :], normed_grad)
        put_back(tower, get_back(tower) + more)
        gather.start()
        store = pltpu.make_async_copy(
            tower.back, tower.token_place(own_mp), r.store_sems.at[2 + tower.index]
        )
        store.start()
        return store

    token_stores = [first_norm_back(text, scatters[3][1], gathers[2][1])]
    until(22)
    token_stores.append(first_norm_back(image, scatters[3][0], gathers[2][0]))
    for scatter in scatters[1]:
        scatter.send_over()
    trades = []
    for tower in (image, text):
        vectors = tower.mixed_vectors
        for k, peer in enumerate((core, across, diag)):
            mine = vectors.at[own_mp]
            trades.append(remote(mine, mine, trade_sems, 3 * tower.index + k, peer))
            trades[-1].start()
    until(32)

    def result_rows(tower, scatter, gather):
        values = tower.resid[...] + scatter.result() + tower.shifts[1:2, :]
        place = lax.broadcasted_iota(jnp.int32, (tower.rows, 1), 0)
        alive = live(tower, own_mp, place)
        if alive is not None:
            values = jnp.where(alive, values, 0.0)
        tower.carried[tower.at(own_mp), :] = values.astype(LOW).astype(FULL)
        gather.start()

    result_rows(text, scatters[1][1], gathers[3][1])
    result_rows(image, scatters[1][0], gathers[3][0])
    until(34)
    for gather in gathers[2]:
        gather.got_core()
        gather.got_across()
    until(36)
    for trade in trades:
        trade.wait()
    vec_start = places[0, "vectors"][0]
    left = summed.shape[0] - vec_start
    summed[vec_start:, :] = jnp.zeros((left, LANES), FULL)
    for tower in (image, text):
        vectors = tower.mixed_vectors
        sums = vectors[0] + vectors[1] + vectors[2] + vectors[3]
        vectors[own_mp] = sums
        heads = tower.across_heads
        vectors[own_mp, 6:7, :] = tower.offset_grad[...]
        vectors[own_mp, 7:8, 0:heads] = tower.bias_grad[:, 0:heads]
        vectors[own_mp, 7:8, heads : 2 * heads] = tower.bias_grad[:, 2 * heads : 3 * heads]
        put(tower, "vectors", vectors[own_mp])
    until(42)
    gathers[3][1].got_core()
    gathers[3][1].got_across()
    gathers[3][0].got_core()
    gathers[3][0].got_across()
    until(44)
    result_stores = []
    for tower in (text, image):
        gathers[3][tower.index].got_diag()
        for owner in range(4):
            at = tower.at(owner)
            values = tower.carried[at, :]
            if tower is text:
                tower.tokens[at, :] = values.astype(LOW)
            else:
                for k in range(2):
                    part = values[k * tower.per : (k + 1) * tower.per]
                    blank = jnp.zeros((tower.tokens.shape[1] - tower.per, tower.wide), FULL)
                    tower.tokens[2 * owner + k] = jnp.concatenate([part, blank], axis=0).astype(LOW)
        result_stores.append(
            pltpu.make_async_copy(tower.tokens, tower.result, r.store_sems.at[5 + tower.index])
        )
        result_stores[-1].start()
    until(ticks)
    for gather in gathers[2]:
        gather.got_diag()
    for gather in gathers[2] + gathers[3]:
        gather.sent()
    for copy in token_stores + result_stores + [blank_store]:
        copy.wait()
    out_copy.wait()


LOADED = ("tokens", "inward", "outward", "expand", "contract", "embed")
FAR = "_far"


def block_call(count, towers, post_norms, logit_scale, scalars, collective_id):
    names, args, in_specs = [], [], []
    outs, out_names, out_specs = [], [], []
    scratch, scratch_names = [], []
    vmem, smem, anywhere = pltpu.VMEM, pltpu.SMEM, pl.ANY

    def give(index, space, **named):
        for name, value in named.items():
            names.append((index, name))
            args.append(value)
            in_specs.append(pl.BlockSpec(memory_space=space))

    def take(index, space, kind=FULL, **named):
        for name, shape in named.items():
            out_names.append((index, name))
            outs.append(jax.ShapeDtypeStruct(shape, kind))
            out_specs.append(pl.BlockSpec(memory_space=space))

    def hold(index, **named):
        for name, what in named.items():
            scratch_names.append((index, name))
            scratch.append(what)

    examples = 8 * count
    sizes = []
    for index, tower in enumerate(towers):
        give(index, anywhere, cotangent_far=tower["cotangent"])
        for name in LOADED:
            give(index, anywhere, **{name + FAR: tower[name]})
            hold(index, **{name: vmem(tower[name].shape, LOW)})
        for name in ("norms", "biases", "shifts", "offsets"):
            give(index, vmem, **{name: tower[name]})
        rows, wide, spaces = 8 * IMG_ROWS, tower["tokens"].shape[-1], tower["tokens"].shape
        if index:
            rows, spaces = 8 * TXT_ROWS, (8, TXT_ROWS, wide)
        heads, hidden, quarter = tower["biases"].shape[1], tower["offsets"].shape[1], rows // 4
        size = Fields()
        size.index, size.wide, size.across_heads, size.hidden = index, wide, heads, hidden
        sizes.append(size)
        take(index, anywhere, token_grad=spaces, embed_grad=tower["embed"].shape)
        take(index, anywhere, LOW, result=tower["tokens"].shape)
        hold(
            index,
            joined=vmem((wide, 3 * heads), LOW),
            normed=vmem((rows, wide), LOW),
            qkv=vmem((rows, 3 * heads), LOW),
            mixed=vmem((rows, heads), LOW),
            normed_two=vmem((rows, wide), LOW),
            active=vmem((rows, hidden), LOW),
            slope=vmem((rows, hidden), LOW),
            bias_row=vmem((1, 3 * heads), FULL),
            resid=vmem((quarter, wide), FULL),
            carried=vmem((rows, wide), FULL),
            back=vmem((2, quarter // 2, wide), FULL),
            own_tokens=vmem((quarter, wide), LOW),
            low_grad=vmem((rows, wide), LOW),
            parts0=vmem((rows, wide), FULL),
            near0=vmem((2, quarter, wide), FULL),
            over0=vmem((quarter, wide), FULL),
            parts1=vmem((rows, wide), FULL),
            near1=vmem((2, quarter, wide), FULL),
            over1=vmem((quarter, wide), FULL),
            top=vmem((8, 1, wide), FULL),
            every_row=vmem((examples, wide), FULL),
            early=vmem((8, wide), FULL),
            first=vmem((4, 8, wide), FULL),
            second=vmem((4, 8, wide), FULL),
            offset_grad=vmem((1, hidden), FULL),
            bias_grad=vmem((1, 3 * heads), FULL),
            mixed_vectors=vmem((4, 8, wide), FULL),
        )
    _, held = gradient_rows(sizes)
    held += -held % SPAN
    give(2, vmem, post_norms=post_norms, logit_scale=logit_scale)
    give(2, smem, **scalars)
    take(2, anywhere, summed_far=(held, LANES))
    take(2, vmem, loss=(1, 1), hits=(1, 1), scale_grad=(1, 1), post_grad=post_norms.shape)
    wide = sizes[0].wide
    dma = pltpu.SemaphoreType.DMA
    rings = dp_rings()
    hold(
        2,
        summed=vmem((held, LANES), FULL),
        marks=vmem((examples, 128), FULL),
        every=vmem((4, count, 4, wide), FULL),
        load_sems=dma((2 * len(LOADED) + 2,)),
        store_sems=dma((8,)),
        blank=vmem((8, towers[0]["tokens"].shape[1] - IMG_ROWS, wide), FULL),
        scatter_send=dma((24,)),
        scatter_recv=dma((24,)),
        gather_send=dma((24,)),
        gather_recv=dma((24,)),
        swap_send=dma((15,)),
        swap_recv=dma((15,)),
        spread_send=dma((count,)),
        spread_recv=dma((count,)),
        trade_send=dma((6,)),
        trade_recv=dma((6,)),
        ring0=rings[0],
        ring1=rings[1],
        ring2=rings[2],
        ring3=rings[3],
        ring4=rings[4],
        ring5=rings[5],
        dp_send=rings[6],
        dp_recv=rings[7],
        dp_credit=rings[8],
    )
    results = pl.pallas_call(
        functools.partial(block_kernel, count, names + out_names + scratch_names),
        out_shape=outs,
        in_specs=in_specs,
        out_specs=out_specs,
        scratch_shapes=scratch,
        compiler_params=pltpu.CompilerParams(
            collective_id=collective_id, has_side_effects=True, vmem_limit_bytes=64 << 20
        ),
        name="block",
    )(*args)
    out = [Fields(), Fields(), Fields()]
    for (index, name), value in zip(out_names, results):
        setattr(out[index], name, value)
    return out, sizes


def finish_kernel(where, names, *refs):
    r = Fields()
    for name, ref in zip(names, refs):
        setattr(r, name, ref)
    copies = []

    def move(source, target):
        copies.append(pltpu.make_async_copy(source, target, r.sems.at[len(copies)]))
        copies[-1].start()

    def load(source, target):
        move(source, target)
        return copies[-1]

    def load_weight(index, name):
        start, rows, width = where[index, name]
        at = pl.ds(start, rows * (width // LANES))
        return load(r.summed.at[at], r.held.at[at])

    kinds, wide, heads = r.inward_t.shape
    high = wide // 2
    start, _, _ = where[0, "vectors"]
    vectors = load(r.summed.at[start : start + 40], r.vectors)
    rows_loaded = load(r.token_grad_t, r.text_rows)
    low_loaded = load(r.result_t, r.text_low)
    weights = [
        (index, name, load_weight(index, name), target)
        for index, name, target in (
            (0, "contract", r.contract_i),
            (0, "expand", r.expand_i),
            (0, "inward", r.inward_i),
            (0, "outward", r.outward_i),
            (1, "contract", r.contract_t),
            (1, "expand", r.expand_t),
            (1, "inward", None),
            (1, "outward", r.outward_t),
        )
    ]
    others = [
        (load(source, held), held, target)
        for source, held, target in (
            (r.token_grad_i, r.held_tokens, r.tokens_i),
            (r.embed_grad_i, r.held_embed_i, r.embed_i),
            (r.embed_grad_t, r.held_embed_t, r.embed_t),
            (r.result_i, r.held_result, r.image_result),
        )
    ]
    first = len(copies)
    for index, name, loaded, target in weights:
        loaded.wait()
        start, rows, width = where[index, name]
        if target is not None:
            for k in range(width // LANES):
                source = r.held.at[start + k * rows : start + (k + 1) * rows]
                move(source, target.at[:, k * LANES : (k + 1) * LANES])
            continue
        for k in range(kinds):
            for side in range(2):
                source = r.held.at[
                    start + k * high : start + (k + 1) * high, side * heads : (side + 1) * heads
                ]
                move(source, r.inward_t.at[k, side * high : (side + 1) * high])
    for loaded, held, target in others:
        loaded.wait()
        move(held, target)
    for loaded in (vectors, rows_loaded, low_loaded):
        loaded.wait()
    context, examples, _ = r.tokens_t.shape
    for e in range(examples):
        r.tokens_t[:, e, :] = r.text_rows[e][0:context]
        r.text_turned[:, e, :] = r.text_low[e * TXT_ROWS : (e + 1) * TXT_ROWS].astype(FULL)[0:context]
    r.text_result[...] = r.text_turned[...].astype(LOW)
    at = 0
    for norms, shifts, offsets, biases in (
        (r.norms_i, r.shifts_i, r.offsets_i, r.biases_i),
        (r.norms_t, r.shifts_t, r.offsets_t, r.biases_t),
    ):
        count = norms.shape[1] // LANES
        rows = jnp.concatenate([r.vectors[at + 8 * k : at + 8 * k + 8, :] for k in range(count)], axis=1)
        at += 8 * count
        norms[...] = rows[0:4]
        shifts[...] = rows[4:6]
        offsets[...] = rows[6:7]
        heads = biases.shape[1]
        biases[...] = jnp.concatenate([rows[7:8, 0:heads], rows[7:8, heads : 2 * heads]], axis=0)
    for copy in copies[first:]:
        copy.wait()


def finish_call(out, where, shapes, context, biases_i, biases_t):
    names, outs, out_specs = [], [], []
    given = dict(
        summed=out[2].summed_far,
        token_grad_i=out[0].token_grad,
        token_grad_t=out[1].token_grad,
        result_i=out[0].result,
        result_t=out[1].result,
        embed_grad_i=out[0].embed_grad,
        embed_grad_t=out[1].embed_grad,
    )

    def take(space, kind=FULL, **named):
        for name, shape in named.items():
            names.append(name)
            outs.append(jax.ShapeDtypeStruct(shape, kind))
            out_specs.append(pl.BlockSpec(memory_space=space))

    for name, shape in shapes.items():
        take(pl.ANY, **{name: shape})
    examples, patch, wide_i = out[0].token_grad.shape
    wide_t = out[1].token_grad.shape[2]
    take(pl.ANY, LOW, image_result=(examples, patch, wide_i))
    take(pltpu.VMEM, LOW, text_result=(context, examples, wide_t))
    take(pltpu.VMEM, tokens_t=(context, examples, wide_t))
    for name, shape in dict(norms=4, shifts=2, offsets=1).items():
        take(pltpu.VMEM, **{name + "_i": (shape, wide_i), name + "_t": (shape, wide_t)})
    take(pltpu.VMEM, biases_i=biases_i, biases_t=biases_t)
    scratch = dict(
        vectors=pltpu.VMEM((40, LANES), FULL),
        text_rows=pltpu.VMEM(out[1].token_grad.shape, FULL),
        text_low=pltpu.VMEM(out[1].result.shape, LOW),
        text_turned=pltpu.VMEM((context, examples, wide_t), FULL),
        held=pltpu.VMEM(out[2].summed_far.shape, FULL),
        held_tokens=pltpu.VMEM(out[0].token_grad.shape, FULL),
        held_embed_i=pltpu.VMEM(out[0].embed_grad.shape, FULL),
        held_embed_t=pltpu.VMEM(out[1].embed_grad.shape, FULL),
        held_result=pltpu.VMEM(out[0].result.shape, LOW),
        sems=pltpu.SemaphoreType.DMA((64,)),
    )
    results = pl.pallas_call(
        functools.partial(finish_kernel, where, list(given) + names + list(scratch)),
        out_shape=outs,
        in_specs=[pl.BlockSpec(memory_space=pl.ANY)] * len(given),
        out_specs=out_specs,
        scratch_shapes=list(scratch.values()),
        compiler_params=pltpu.CompilerParams(vmem_limit_bytes=62 << 20),
        name="finish",
    )(*given.values())
    fields = Fields()
    for name, value in zip(names, results):
        setattr(fields, name, value)
    return fields


def shards(
    count,
    image_tokens,
    image_norms,
    image_inward,
    image_biases,
    image_outward,
    image_shifts,
    image_expand,
    image_offsets,
    image_contract,
    image_embed,
    text_tokens,
    text_norms,
    text_inward,
    text_biases,
    text_outward,
    text_shifts,
    text_expand,
    text_offsets,
    text_contract,
    text_embed,
    post_norms,
    logit_scale,
    image_cotangent,
    text_cotangent,
    resolution,
    validity,
    text_ends,
):
    examples, patch, image_width = image_tokens.shape
    context, text_width = text_tokens.shape[1:]

    def fit(values):
        grow = ((0, 0), (0, TXT_ROWS - context), (0, 0))
        return jnp.pad(values, grow).reshape(-1, values.shape[2])

    image = dict(
        tokens=image_tokens,
        inward=jnp.swapaxes(image_inward, 1, 2),
        outward=image_outward,
        expand=image_expand,
        contract=image_contract,
        embed=image_embed,
        cotangent=image_cotangent,
        norms=image_norms,
        biases=image_biases,
        shifts=image_shifts,
        offsets=image_offsets.reshape(1, -1),
    )
    text = dict(
        tokens=fit(text_tokens),
        inward=text_inward,
        outward=text_outward,
        expand=text_expand,
        contract=text_contract,
        embed=text_embed,
        cotangent=fit(text_cotangent),
        norms=text_norms,
        biases=text_biases,
        shifts=text_shifts,
        offsets=text_offsets.reshape(1, -1),
    )
    scalars = dict(resolution=resolution, validity=validity, ends=text_ends)
    out, sizes = block_call(
        count, (image, text), post_norms, logit_scale.reshape(1, 1), scalars, 0
    )
    where, _ = gradient_rows(sizes)
    shapes = dict(
        contract_i=image_contract.shape,
        expand_i=image_expand.shape,
        outward_i=image_outward.shape,
        inward_i=(image_inward.shape[0] * image_inward.shape[2], image_width),
        embed_i=image_embed.shape,
        tokens_i=image_tokens.shape,
        contract_t=text_contract.shape,
        expand_t=text_expand.shape,
        outward_t=text_outward.shape,
        inward_t=text_inward.shape,
        embed_t=text_embed.shape,
    )
    end = finish_call(out, where, shapes, context, image_biases.shape, text_biases.shape)
    inward_i = end.inward_i.reshape(image_inward.shape[0], -1, image_width)
    return (
        end.image_result,
        jnp.swapaxes(end.text_result, 0, 1),
        out[2].loss.reshape(1),
        out[2].hits.reshape(1),
        end.tokens_i,
        jnp.swapaxes(end.tokens_t, 0, 1),
        end.norms_i,
        jnp.swapaxes(inward_i, 1, 2),
        end.biases_i,
        end.outward_i,
        end.shifts_i,
        end.expand_i,
        end.offsets_i.reshape(-1),
        end.contract_i,
        end.embed_i,
        end.norms_t,
        end.inward_t,
        end.biases_t,
        end.outward_t,
        end.shifts_t,
        end.expand_t,
        end.offsets_t.reshape(-1),
        end.contract_t,
        end.embed_t,
        out[2].post_grad,
        out[2].scale_grad.reshape(1),
    )


def solution(mesh):
    placed = (
        P("dp", None, None),
        P(),
        P(None, None, "mp"),
        P(None, "mp"),
        P("mp", None),
        P(),
        P(None, "mp"),
        P("mp"),
        P("mp", None),
        P(),
        P("dp", None, None),
        P(),
        P(None, None, "mp"),
        P(None, "mp"),
        P("mp", None),
        P(),
        P(None, "mp"),
        P("mp"),
        P("mp", None),
        P(),
        P(),
        P(),
        P("dp", None, None),
        P("dp", None, None),
        P("dp"),
        P("dp"),
        P("dp"),
    )
    return jax.shard_map(
        functools.partial(shards, mesh.shape["dp"]),
        mesh=mesh,
        in_specs=placed,
        out_specs=(
            P("dp", None, None),
            P("dp", None, None),
            P(),
            P(),
            P("dp", None, None),
            P("dp", None, None),
            P(),
            P(None, None, "mp"),
            P(None, "mp"),
            P("mp", None),
            P(),
            P(None, "mp"),
            P("mp"),
            P("mp", None),
            P(),
            P(),
            P(None, None, "mp"),
            P(None, "mp"),
            P("mp", None),
            P(),
            P(None, "mp"),
            P("mp"),
            P("mp", None),
            P(),
            P(),
            P(),
        ),
        check_vma=False,
    )
```

```python
import functools

import jax
import jax.numpy as jnp
from jax import lax
from jax.experimental import pallas as pl
from jax.experimental.pallas import tpu as pltpu
from jax.sharding import PartitionSpec as P

MESH = pl.DeviceIdType.MESH
HEAD = 64
LOW_LEN = 50
HIGH_LEN = 101
IMG_ROWS = 104
TXT_ROWS = 80
SPAN = 256
SLOTS = 4
LANES = 256

EPSILON = 1e-05
MASKED = -1000000000.0
HIGHEST = lax.Precision.HIGHEST


def dp_sum_machine(count, blocks, total, rings, sends, recvs, credits):
    places = count // 2
    deep = places // 2
    dp, mp = lax.axis_index("dp"), lax.axis_index("mp")
    side, place = lax.rem(dp, 2), dp // 2
    low = place < deep
    depth = jnp.where(low, place, places - 1 - place)
    inner = jnp.where(low, place + 1, place - 1)
    outer = jnp.clip(jnp.where(low, place - 1, place + 1), 0, places - 1)
    half = jnp.where(low, 0, 1)
    pair_id = (place * 2 + 1 - side, mp)
    inner_id = (inner * 2 + side, mp)
    outer_id = (outer * 2 + side, mp)
    quarter = SPAN // 4

    def part(offset, size):
        def at(block):
            start = pl.multiple_of(block * SPAN + offset, quarter)
            return total.at[pl.ds(start, size)]

        return at

    kept = part(side * quarter, quarter)
    given = part((1 - side) * quarter, quarter)
    whole = part(2 * quarter, 2 * quarter)
    mid_kept = part((2 + half) * quarter, quarter)
    mid_given = part((3 - half) * quarter, quarter)
    middle = depth == deep - 1
    not_middle = depth < deep - 1
    not_end = depth > 0
    yes = depth >= 0

    kinds = [
        (yes, 0, given, pair_id, yes, 0, pair_id, rings[0], kept),
        (not_middle, depth, whole, inner_id, not_end, depth - 1, outer_id, rings[1], whole),
        (not_middle, depth + 1, kept, inner_id, not_end, depth, outer_id, rings[2], kept),
        (middle, deep - 1, mid_given, inner_id, middle, deep - 1, inner_id, rings[3], mid_kept),
        (middle, deep, mid_kept, pair_id, middle, deep, pair_id, rings[4], mid_kept),
        (middle, deep, kept, inner_id, middle, deep, inner_id, rings[5], kept),
        (middle, deep + 1, mid_kept, inner_id, middle, deep + 1, inner_id, None, mid_given),
        (not_end, 2 * deep - depth, kept, outer_id, not_middle, 2 * deep - depth - 1, inner_id, None, kept),
        (not_end, 2 * deep + 1 - depth, whole, outer_id, not_middle, 2 * deep - depth, inner_id, None, whole),
        (yes, 2 * deep, kept, pair_id, yes, 2 * deep, pair_id, None, given),
    ]

    def copy(k, kind, block):
        _, _, src, target, _, _, _, ring, land = kind
        slot = lax.rem(block, SLOTS)
        dst = src(block) if ring is None else ring.at[slot]
        return pltpu.make_async_remote_copy(
            src_ref=src(block),
            dst_ref=dst,
            send_sem=sends.at[k, slot],
            recv_sem=recvs.at[k, slot],
            device_id=target,
            device_id_type=MESH,
        )

    def valid(block):
        return jnp.logical_and(block >= 0, block < blocks)

    def start(t):
        for k, kind in enumerate(kinds):
            block = t - 2 * kind[1]

            @pl.when(jnp.logical_and(kind[0], valid(block)))
            def _():
                @pl.when(block >= SLOTS)
                def _():
                    pl.semaphore_wait(credits.at[k], 1)

                copy(k, kind, block).start()

    def finish(t):
        for k, kind in enumerate(kinds):
            sends_it, sent_stage, _, _, takes_it, got_stage, source, ring, land = kind
            sent = t - 2 * sent_stage
            got = t - 2 * got_stage

            @pl.when(jnp.logical_and(sends_it, valid(sent)))
            def _():
                copy(k, kind, sent).wait_send()

            @pl.when(jnp.logical_and(takes_it, valid(got)))
            def _():
                copy(k, kind, got).wait_recv()
                if ring is not None:
                    here = land(got)
                    here[...] = here[...] + ring[lax.rem(got, SLOTS)]

                @pl.when(got < blocks - SLOTS)
                def _():
                    pl.semaphore_signal(credits.at[k], inc=1, device_id=source, device_id_type=MESH)

    def tick(t):
        start(t)

        @pl.when(t > 0)
        def _():
            finish(t - 1)

    return tick, blocks + 4 * deep + 1


def dp_rings():
    quarter = SPAN // 4
    sizes = [quarter, 2 * quarter, quarter, quarter, quarter, quarter]
    return [pltpu.VMEM((SLOTS, size, LANES), jnp.float32) for size in sizes] + [
        pltpu.SemaphoreType.DMA((10, SLOTS)),
        pltpu.SemaphoreType.DMA((10, SLOTS)),
        pltpu.SemaphoreType.REGULAR((10,)),
    ]


LOW, FULL = jnp.bfloat16, jnp.float32


def mm(left, right):
    return jnp.dot(left, right, preferred_element_type=FULL)


def mm_nt(left, right, precision=None):
    dims = (((1,), (1,)), ((), ()))
    return lax.dot_general(left, right, dims, precision=precision, preferred_element_type=FULL)


def mm_tn(left, right, precision=None):
    dims = (((0,), (0,)), ((), ()))
    return lax.dot_general(left, right, dims, precision=precision, preferred_element_type=FULL)


def row_sum(values):
    return jnp.sum(values, axis=1, keepdims=True)


def col_sum(values):
    return jnp.sum(values, axis=0, keepdims=True)


def whitened(values):
    width = values.shape[1]
    centred = values - row_sum(values) * (1.0 / width)
    scale = lax.rsqrt(row_sum(centred * centred) * (1.0 / width) + EPSILON)
    return centred * scale, scale


def whitened_back(white, scale, gain, gradient):
    width = white.shape[1]
    inner = gradient * gain
    mean = row_sum(inner) * (1.0 / width)
    slope = row_sum(inner * white) * (1.0 / width)
    return scale * (inner - mean - white * slope)


class Fields:
    pass


class Tower:
    def __init__(self, index, rows, per, fields):
        self.__dict__.update(fields.__dict__)
        self.index, self.rows, self.per = index, rows, per
        self.wide = self.shifts.shape[1]
        self.across_heads = self.biases.shape[1]
        self.hidden = self.offsets.shape[0] * 128
        self.panels = self.wide // LANES

    def at(self, owner):
        return pl.ds(pl.multiple_of(owner * self.rows, self.rows), self.rows)

    def token_place(self, owner):
        return self.token_grad.at[pl.ds(2 * owner, 2), pl.ds(0, self.per)]


def gradient_rows(towers):
    image, text = towers
    where, start = {}, 0
    for tower, name, rows in (
        (text, "contract", text.hidden),
        (text, "expand", text.wide),
        (image, "contract", image.hidden),
        (image, "expand", image.wide),
        (text, "outward", text.across_heads),
        (text, "inward", 3 * text.across_heads),
        (image, "outward", image.across_heads),
        (image, "inward", 3 * image.across_heads),
        (image, "vectors", 8),
        (text, "vectors", 8),
    ):
        width = tower.hidden if name == "expand" else tower.wide
        where[tower.index, name] = (start, rows, width)
        start += rows * (width // LANES)
    return where, start


def block_kernel(count, names, *refs):
    fields = [Fields(), Fields(), Fields()]
    for (index, name), ref in zip(names, refs):
        setattr(fields[index], name, ref)
    image = Tower(0, 2 * IMG_ROWS, IMG_ROWS, fields[0])
    text = Tower(1, 2 * TXT_ROWS, TXT_ROWS, fields[1])
    r = fields[2]
    places, _ = gradient_rows((image, text))
    deep = count // 4
    dp, mp = lax.axis_index("dp"), lax.axis_index("mp")
    flip, core_bit = mp // 2, lax.rem(mp, 2)
    core_mp = flip * 2 + 1 - core_bit
    across_mp = (1 - flip) * 2 + core_bit
    diag_mp = (1 - flip) * 2 + 1 - core_bit
    core, across, diag = (dp, core_mp), (dp, across_mp), (dp, diag_mp)
    own_mp = mp

    for tower in (text, image):
        tower.loads = {}
    for k, name in enumerate(LOADED):
        for tower in (text, image):
            source, target = getattr(tower, name + FAR), getattr(tower, name)
            copy = pltpu.make_async_copy(source, target, r.load_sems.at[2 * k + tower.index])
            copy.start()
            tower.loads[name] = copy
    r.blank[...] = jnp.zeros(r.blank.shape, FULL)
    blank_store = pltpu.make_async_copy(
        r.blank,
        image.token_grad.at[:, pl.ds(image.per, image.token_grad.shape[1] - image.per)],
        r.store_sems.at[7],
    )
    blank_store.start()
    barrier = pltpu.get_barrier_semaphore()
    friends = [core, across, diag] + [(lax.rem(dp + k, count), mp) for k in range(1, count)]
    for friend in friends:
        pl.semaphore_signal(barrier, inc=1, device_id=friend, device_id_type=MESH)

    scatter_sems = r.scatter_send, r.scatter_recv
    gather_sems = r.gather_send, r.gather_recv
    swap_sems = r.swap_send, r.swap_recv
    spread_sems = r.spread_send, r.spread_recv
    trade_sems = r.trade_send, r.trade_recv

    def remote(src, dst, group, k, peer):
        return pltpu.make_async_remote_copy(
            src_ref=src,
            dst_ref=dst,
            send_sem=group[0].at[k],
            recv_sem=group[1].at[k],
            device_id=peer,
            device_id_type=MESH,
        )

    class Scatter:
        def __init__(self, tower, phase, bank):
            self.tower = tower
            self.parts, self.near_buf, self.over_buf = (
                (tower.parts1, tower.near1, tower.over1)
                if bank
                else (tower.parts0, tower.near0, tower.over0)
            )
            k = (phase * 2 + tower.index) * 3
            self.far = remote(self.parts.at[tower.at(diag_mp)], self.near_buf.at[0], scatter_sems, k, core)
            self.near = remote(self.parts.at[tower.at(core_mp)], self.near_buf.at[1], scatter_sems, k + 1, core)
            self.over = remote(self.near_buf.at[0], self.over_buf, scatter_sems, k + 2, across)

        def send_over(self):
            self.far.wait()
            self.near_buf[0] = self.near_buf[0] + self.parts[self.tower.at(across_mp), :]
            self.over.start()

        def result(self):
            self.near.wait()
            self.over.wait()
            return self.parts[self.tower.at(own_mp), :] + self.near_buf[1] + self.over_buf[...]

    class Gather:
        def __init__(self, tower, phase):
            k = (phase * 2 + tower.index) * 3
            if phase == 2:
                source, mine, passed = (
                    tower.back,
                    tower.token_place(own_mp),
                    tower.token_place(across_mp),
                )
            else:
                mine = source = tower.carried.at[tower.at(own_mp)]
                passed = tower.carried.at[tower.at(across_mp)]
            self.one = remote(source, mine, gather_sems, k, across)
            self.two = remote(source, mine, gather_sems, k + 1, core)
            self.on = remote(passed, passed, gather_sems, k + 2, core)

        def start(self):
            self.one.start()
            self.two.start()

        def got_core(self):
            self.two.wait_recv()

        def got_across(self):
            self.one.wait_recv()
            self.on.start()

        def got_diag(self):
            self.on.wait_recv()

        def sent(self):
            self.one.wait_send()
            self.two.wait_send()
            self.on.wait_send()

    def length(example):
        return jnp.where(r.resolution[example] == 1, HIGH_LEN, LOW_LEN)

    def live(tower, owner, places_):
        if tower is text:
            return None
        first, second = length(2 * owner), length(2 * owner + 1) + tower.per
        return places_ < jnp.where(places_ < tower.per, first, second)

    def allowed(tower, owner):
        shape = (tower.rows, tower.rows)
        query = lax.broadcasted_iota(jnp.int32, shape, 0)
        key = lax.broadcasted_iota(jnp.int32, shape, 1)
        key_start = jnp.where(query < tower.per, 0, tower.per)
        if tower is text:
            end = query + 1
        else:
            first, second = length(2 * owner), length(2 * owner + 1) + tower.per
            end = jnp.where(query < tower.per, first, second)
        return jnp.logical_and(key >= key_start, key < end)

    def chosen_places(tower, owner):
        if tower is text:
            return r.ends[2 * owner], r.ends[2 * owner + 1] + tower.per
        return 0, tower.per

    def chosen_row(tower, example, read):
        first = example * tower.per
        if tower is image:
            return read(first, 16)[0:1]
        place = lax.broadcasted_iota(jnp.int32, (tower.per, 1), 0)
        rows = read(first, tower.per)
        return col_sum(jnp.where(place == r.ends[example], rows, 0.0))

    def softmax(tower, scores, mask):
        scores = jnp.where(mask, scores * HEAD ** (-0.5), MASKED)
        top = jnp.max(scores, axis=1, keepdims=True)
        weights = jnp.exp(scores - top)
        return weights * (1.0 / row_sum(weights))

    def owner_of(j):
        return lax.rem(flip + 1 - j // 2, 2) * 2 + lax.rem(core_bit + 1 - lax.rem(j, 2), 2)

    def prepare(tower):
        for name in ("tokens", "inward", "outward"):
            tower.loads[name].wait()
        heads = tower.across_heads
        if tower is text:
            for k in range(3):
                tower.joined[:, k * heads : (k + 1) * heads] = tower.inward[k]
        for k in range(tower.hidden // 128):
            tower.offset_row[:, k * 128 : (k + 1) * 128] = tower.offsets[k : k + 1, :]
        tower.bias_row[:, 0:heads] = tower.biases[0:1, :]
        tower.bias_row[:, heads : 2 * heads] = jnp.zeros((1, heads), FULL)
        tower.bias_row[:, 2 * heads : 3 * heads] = tower.biases[1:2, :]

    def rows_of(tower, owner):
        if tower is text:
            return tower.tokens[tower.at(owner), :].astype(FULL)
        pair = [tower.tokens[2 * owner + k].astype(FULL)[0 : tower.per] for k in range(2)]
        return jnp.concatenate(pair, axis=0)

    def into_heads(tower, normed):
        if tower is text:
            return mm(normed, tower.joined[...])
        return mm_nt(normed, tower.inward[...].reshape(3 * tower.across_heads, tower.wide))

    def out_of_heads(tower, grads):
        if tower is text:
            return mm_nt(grads, tower.joined[...])
        return mm(grads, tower.inward[...].reshape(3 * tower.across_heads, tower.wide))

    def attend(tower, owner):
        at, heads = tower.at(owner), tower.across_heads
        white, _ = whitened(rows_of(tower, owner))
        normed = (white * tower.norms[0:1, :] + tower.norms[1:2, :]).astype(LOW)
        tower.normed[at, :] = normed
        qkv = (into_heads(tower, normed) + tower.bias_row[...]).astype(LOW)
        tower.qkv[at, :] = qkv
        mask = allowed(tower, owner)
        mixed = []
        for h in range(heads // HEAD):
            query, key, value = (
                qkv[:, k * heads + h * HEAD : k * heads + (h + 1) * HEAD] for k in range(3)
            )
            weights = softmax(tower, mm_nt(query, key), mask)
            mixed.append(mm(weights.astype(LOW), value).astype(LOW))
        mixed = jnp.concatenate(mixed, axis=1)
        tower.mixed[at, :] = mixed
        tower.parts0[at, :] = mm(mixed, tower.outward[...])

    def attend_all(tower, scatter):
        def body(j, carry):
            attend(tower, owner_of(j))

            @pl.when(j == 0)
            def _():
                scatter.far.start()

            if tower is text:

                @pl.when(j == 1)
                def _():
                    scatter.send_over()

            @pl.when(j == 2)
            def _():
                scatter.near.start()

            return carry

        lax.fori_loop(0, 4, body, 0)
        tower.own_tokens[...] = rows_of(tower, own_mp).astype(LOW)

    def second_norm(tower, scatter):
        at = tower.at(own_mp)
        mine = tower.own_tokens[...].astype(FULL)
        resid = mine + scatter.result() + tower.shifts[0:1, :]
        tower.resid[...] = resid
        white, _ = whitened(resid)
        normed = (white * tower.norms[2:3, :] + tower.norms[3:4, :]).astype(LOW)
        tower.carried[at, :] = normed.astype(FULL)

    def feed(tower, owner):
        at = tower.at(owner)
        normed = tower.carried[at, :].astype(LOW)
        tower.normed_two[at, :] = normed
        hidden = mm(normed, tower.expand[...]) + tower.offset_row[...]
        gate = 1.0 / (1.0 + jnp.exp(-1.702 * hidden))
        active = (hidden * gate).astype(LOW)
        tower.active[at, :] = active
        tower.slope[at, :] = (gate * (1.0 + 1.702 * hidden * (1.0 - gate))).astype(LOW)
        tower.parts1[at, :] = mm(active, tower.contract[...])

    scatters = [[Scatter(t, phase, phase == 1) for t in (image, text)] for phase in range(4)]
    gathers = [[Gather(t, phase) for t in (image, text)] for phase in range(4)]

    every = r.every
    peers = (core, across, diag)

    def swap_all(buffer, tower, step):
        mine = buffer.at[own_mp]
        copies = [
            remote(mine, mine, swap_sems, (2 * step + tower.index) * 3 + k, peer)
            for k, peer in enumerate(peers)
        ]
        for copy in copies:
            copy.start()
        return copies

    def sum_of(buffer):
        return buffer[0] + buffer[1] + buffer[2] + buffer[3]

    def chosen_first(tower):
        def token_rows(first, rows):
            if tower is image:
                return tower.tokens[first // tower.per, 0:rows, :].astype(FULL)
            return tower.tokens[first : first + rows, :].astype(FULL)

        def part_rows(first, rows):
            return tower.parts0[first : first + rows, :]

        for e in range(8):
            tower.first[own_mp, e : e + 1, :] = chosen_row(tower, e, part_rows)
            tower.early[e : e + 1, :] = chosen_row(tower, e, token_rows) + tower.shifts[0:1, :]
        return swap_all(tower.first, tower, 0)

    def chosen_second(tower, copies):
        for copy in copies:
            copy.wait()
        resid = tower.early[...] + sum_of(tower.first)
        tower.early[...] = resid
        white, _ = whitened(resid)
        normed = (white * tower.norms[2:3, :] + tower.norms[3:4, :]).astype(LOW)
        hidden = mm(normed, tower.expand[...]) + tower.offset_row[...]
        active = (hidden * (1.0 / (1.0 + jnp.exp(-1.702 * hidden)))).astype(LOW)
        tower.second[own_mp] = mm(active, tower.contract[...])
        return swap_all(tower.second, tower, 1)

    def chosen_third(tower, copies):
        for copy in copies:
            copy.wait()
        final = tower.early[...] + sum_of(tower.second) + tower.shifts[1:2, :]
        for e in range(8):
            tower.top[e] = final[e : e + 1]
        for k in range(2):
            spot = 2 * tower.index + k
            every[own_mp, dp, spot : spot + 1, 0 : tower.wide] = tower.top[2 * own_mp + k]

    prepare(text)
    prepare(image)
    pl.semaphore_wait(barrier, len(friends))
    attend_all(text, scatters[0][1])
    attend_all(image, scatters[0][0])
    swaps = [chosen_first(tower) for tower in (image, text)]
    second_norm(text, scatters[0][1])
    for tower in (text, image):
        reload = pltpu.make_async_copy(
            tower.cotangent_far, tower.tokens, r.load_sems.at[2 * len(LOADED) + tower.index]
        )
        tower.loads["cotangent"] = reload
        reload.start()
        tower.loads["expand"].wait()
        tower.loads["contract"].wait()
    swaps = [chosen_second(tower, swaps[tower.index]) for tower in (image, text)]
    gathers[0][1].start()
    feed(text, own_mp)
    for k in range(2):
        mark = r.validity[2 * own_mp + k].astype(FULL)
        every[own_mp, dp, 2 + k : 3 + k, text.wide : text.wide + 128] = jnp.full((1, 128), mark, FULL)
    for tower in (image, text):
        chosen_third(tower, swaps[tower.index])
    mine = every.at[own_mp, dp]
    spread = [
        remote(mine, mine, spread_sems, k, (lax.rem(dp + k, count), mp)) for k in range(1, count)
    ]
    for copy in spread:
        copy.start()
    gathers[0][1].got_core()
    feed(text, core_mp)
    for copy in spread:
        copy.wait()
    one = remote(every.at[own_mp], every.at[own_mp], swap_sems, 12, across)
    two = remote(every.at[own_mp], every.at[own_mp], swap_sems, 13, core)
    on = remote(every.at[across_mp], every.at[across_mp], swap_sems, 14, core)
    one.start()
    two.start()
    scatters[0][0].send_over()
    gathers[0][1].got_across()
    feed(text, across_mp)
    one.wait_recv()
    on.start()
    gathers[0][1].got_diag()
    feed(text, diag_mp)
    two.wait_recv()
    on.wait_recv()
    for copy in (one, two, on):
        copy.wait_send()

    for place in range(count):
        for quarter in range(4):
            spot = (place * 4 + quarter) * 2
            block = every[quarter, place]
            image.every_row[spot : spot + 2, :] = block[0:2, :]
            text.every_row[spot : spot + 2, :] = block[2:4, 0 : text.wide]
            r.marks[spot : spot + 2, :] = block[2:4, text.wide : text.wide + 128]
    for tower in (text, image):
        tower.loads["embed"].wait()
    post = r.post_norms

    def head(tower, rows):
        lanes = slice(0, image.wide) if tower is image else slice(image.wide, image.wide + text.wide)
        white, scale = whitened(rows)
        low = (white * post[0:1, lanes] + post[1:2, lanes]).astype(LOW)
        raw = mm(low, tower.embed[...])
        inverse = lax.rsqrt(row_sum(raw * raw) + 1e-06)
        return lanes, white, scale, low, raw * inverse, inverse

    heads = [head(tower, tower.every_row[...]) for tower in (image, text)]
    unit_i, unit_t = heads[0][4], heads[1][4]
    marks = r.marks[...]
    examples = marks.shape[0]
    valid_col = marks[:, 0:1]
    valid_row = jnp.transpose(marks)[0:1, :]
    number = col_sum(valid_col)
    factor = jnp.exp(r.logit_scale[...])
    logits = factor * mm_nt(unit_i, unit_t, HIGHEST)
    by_row = jnp.where(valid_row > 0.5, logits, MASKED)
    by_col = jnp.where(valid_col > 0.5, logits, MASKED)
    row_top = jnp.max(by_row, axis=1, keepdims=True)
    row_lse = row_top + jnp.log(row_sum(jnp.exp(by_row - row_top)))
    col_top = jnp.max(by_col, axis=0, keepdims=True)
    col_lse = col_top + jnp.log(col_sum(jnp.exp(by_col - col_top)))
    diagonal = factor * row_sum(unit_i * unit_t)
    loss = col_sum(valid_col * (row_lse - 2.0 * diagonal)) + row_sum(valid_row * col_lse)
    r.loss[...] = loss / (2.0 * number)
    r.hits[...] = col_sum(valid_col * jnp.exp(diagonal - row_lse))
    row_id = lax.broadcasted_iota(jnp.int32, (examples, examples), 0)
    col_id = lax.broadcasted_iota(jnp.int32, (examples, examples), 1)
    same = jnp.where(row_id == col_id, 1.0, 0.0)
    pairs = (
        valid_col * (jnp.exp(by_row - row_lse) - same)
        + valid_row * (jnp.exp(by_col - col_lse) - same)
    ) / (2.0 * number)
    r.scale_grad[...] = col_sum(row_sum(pairs * logits))
    unit_grads = [
        factor * lax.dot(pairs, unit_t, precision=HIGHEST, preferred_element_type=FULL),
        factor * mm_tn(pairs, unit_i, HIGHEST),
    ]
    stores = []
    for tower, (lanes, white, scale, low, unit, inverse), grad in zip((image, text), heads, unit_grads):
        raw_grad = (inverse * (grad - unit * row_sum(unit * grad))).astype(LOW)
        spare = tower.parts1 if tower is image else tower.parts0
        home = spare.at[0 : tower.wide, 0 : tower.embed.shape[1]]
        home[...] = mm_tn(low, raw_grad)
        stores.append(pltpu.make_async_copy(home, tower.embed_grad, r.store_sems.at[tower.index]))
        stores[-1].start()
        low_grad = mm_nt(raw_grad, tower.embed[...])
        r.post_grad[0:1, lanes] = col_sum(low_grad * white)
        r.post_grad[1:2, lanes] = col_sum(low_grad)
        tower.every_row[...] = whitened_back(white, scale, post[0:1, lanes], low_grad)
        own = tower.every_row[pl.ds(pl.multiple_of(dp * 8, 8), 8), :]
        for k in range(8):
            tower.top[k] = own[k : k + 1, :]

    def grad_rows(tower, owner):
        place = lax.broadcasted_iota(jnp.int32, (tower.rows, 1), 0)
        values = rows_of(tower, owner)
        alive = live(tower, owner, place)
        if alive is not None:
            values = jnp.where(alive, values, 0.0)
        for k, at in enumerate(chosen_places(tower, owner)):
            values = values + jnp.where(place == at, tower.top[2 * owner + k], 0.0)
        return values

    def low_rows(tower):
        def body(owner, carry):
            tower.low_grad[tower.at(owner), :] = grad_rows(tower, owner).astype(LOW)
            return carry

        lax.fori_loop(0, 4, body, 0)

    def feed_back(tower, j, scatter):
        owner = owner_of(j)
        at = tower.at(owner)
        low = tower.low_grad[at, :]
        active_grad = mm_nt(low, tower.contract[...]).astype(LOW).astype(FULL)
        hidden_grad = active_grad * tower.slope[at, :].astype(FULL)
        tower.offset_grad[...] = tower.offset_grad[...] + col_sum(hidden_grad)
        hidden_low = hidden_grad.astype(LOW)
        tower.slope[at, :] = hidden_low
        tower.parts0[at, :] = mm_nt(hidden_low, tower.expand[...])

        @pl.when(j == 0)
        def _():
            scatter.far.start()

        @pl.when(j == 2)
        def _():
            scatter.near.start()

    def put_back(tower, values):
        tower.back[...] = values.reshape(2, tower.per, tower.wide)

    def get_back(tower):
        return tower.back[...].reshape(tower.rows, tower.wide)

    summed = r.summed

    def put(tower, name, values, first=0):
        start, rows, width = places[tower.index, name]
        for k in range(width // LANES):
            to = pl.ds(pl.multiple_of(start + k * rows + first, 8), values.shape[0])
            summed[to, :] = values[:, k * LANES : (k + 1) * LANES]

    def outer(tower, name, left, right):
        def body(j, carry):
            cut = pl.ds(pl.multiple_of(j * LANES, LANES), LANES)
            put(tower, name, mm_tn(left[:, cut], right[...]), j * LANES)
            return carry

        lax.fori_loop(0, left.shape[1] // LANES, body, 0)

    rings = [r.ring0, r.ring1, r.ring2, r.ring3, r.ring4, r.ring5]
    tick, ticks = dp_sum_machine(
        count, summed.shape[0] // SPAN, summed, rings, r.dp_send, r.dp_recv, r.dp_credit
    )
    out_copy = pltpu.make_async_copy(summed, r.summed_far, r.store_sems.at[4])
    clock = [0]

    def go(number):
        def body(t, carry):
            tick(t)
            done = t - 1 - 4 * deep

            @pl.when(done >= 0)
            def _():
                at = pl.ds(pl.multiple_of(done * SPAN, SPAN), SPAN)
                pltpu.make_async_copy(
                    summed.at[at], r.summed_far.at[at], r.store_sems.at[4]
                ).start()

            return carry

        lax.fori_loop(clock[0], clock[0] + number, body, 0)
        clock[0] += number

    def until(number):
        go(number - clock[0])

    for copy in stores:
        copy.wait()

    def begin_back(tower):
        tower.loads["cotangent"].wait()
        tower.offset_grad[...] = jnp.zeros(tower.offset_grad.shape, FULL)
        tower.bias_grad[...] = jnp.zeros(tower.bias_grad.shape, FULL)
        grads = grad_rows(tower, own_mp)
        put_back(tower, grads)
        tower.mixed_vectors[own_mp] = jnp.zeros((8, tower.wide), FULL)
        tower.mixed_vectors[own_mp, 5:6, :] = col_sum(grads)

    def feed_back_loop(tower, first, last, scatter):
        def body(j, carry):
            feed_back(tower, j, scatter)
            return carry

        lax.fori_loop(first, last, body, 0)

    begin_back(text)
    low_rows(text)
    outer(text, "contract", text.active, text.low_grad)
    until(1)
    gathers[0][1].sent()
    feed_back_loop(text, 0, 4, scatters[2][1])
    until(2)
    outer(text, "expand", text.normed_two, text.slope)
    begin_back(image)
    until(3)
    second_norm(image, scatters[0][0])
    gathers[0][0].start()
    scatters[2][1].send_over()
    feed(image, own_mp)
    until(4)
    low_rows(image)
    gathers[0][0].got_core()
    feed(image, core_mp)
    until(5)
    feed_back_loop(image, 2, 4, scatters[2][0])
    until(6)
    gathers[0][0].got_across()
    feed(image, across_mp)
    gathers[0][0].got_diag()
    feed(image, diag_mp)
    outer(image, "contract", image.active, image.low_grad)
    until(7)
    gathers[0][0].sent()
    feed_back_loop(image, 0, 2, scatters[2][0])
    scatters[2][0].send_over()
    until(9)

    def second_norm_back(tower, scatter, gather):
        normed_grad = scatter.result()
        white, scale = whitened(tower.resid[...])
        vectors = tower.mixed_vectors
        vectors[own_mp, 2:3, :] = col_sum(normed_grad * white)
        vectors[own_mp, 3:4, :] = col_sum(normed_grad)
        grads = get_back(tower) + whitened_back(white, scale, tower.norms[2:3, :], normed_grad)
        vectors[own_mp, 4:5, :] = col_sum(grads)
        put_back(tower, grads)
        tower.carried[tower.at(own_mp), :] = grads.astype(LOW).astype(FULL)
        gather.start()

    def attend_back(tower, owner):
        at, heads = tower.at(owner), tower.across_heads
        low = tower.carried[at, :].astype(LOW)
        tower.low_grad[at, :] = low
        mixed_grad = mm_nt(low, tower.outward[...]).astype(LOW)
        qkv = tower.qkv[at, :]
        mask = allowed(tower, owner)
        grads = [[], [], []]
        for h in range(heads // HEAD):
            query, key, value = (
                qkv[:, k * heads + h * HEAD : k * heads + (h + 1) * HEAD] for k in range(3)
            )
            weights = softmax(tower, mm_nt(query, key), mask)
            grad = mixed_grad[:, h * HEAD : (h + 1) * HEAD]
            weight_grad = mm_nt(grad, value)
            grads[2].append(mm_tn(weights.astype(LOW), grad))
            score_grad = weights * (weight_grad - row_sum(weight_grad * weights))
            score_grad = score_grad.astype(LOW)
            grads[0].append(mm(score_grad, key) * HEAD ** (-0.5))
            grads[1].append(mm_tn(score_grad, query) * HEAD ** (-0.5))
        joined = jnp.concatenate([part for kind in grads for part in kind], axis=1)
        tower.bias_grad[...] = tower.bias_grad[...] + col_sum(joined)
        low = joined.astype(LOW)
        tower.qkv[at, :] = low
        tower.parts0[at, :] = out_of_heads(tower, low)

    def outer_attention(tower):
        heads = tower.across_heads
        put(tower, "outward", mm_tn(tower.mixed[...], tower.low_grad[...]))
        for k in range(3):
            grads = tower.qkv[:, k * heads : (k + 1) * heads]
            if tower is image:
                put(tower, "inward", mm_tn(grads, tower.normed[...]), k * heads)
            else:
                part = mm_tn(tower.normed[...], grads)
                start, rows, _ = places[tower.index, "inward"]
                high = tower.wide // 2
                for side in range(2):
                    summed[start + k * high : start + (k + 1) * high, side * heads : (side + 1) * heads] = (
                        part[side * high : (side + 1) * high]
                    )

    second_norm_back(text, scatters[2][1], gathers[1][1])
    attend_back(text, own_mp)
    until(10)
    outer(image, "expand", image.normed_two, image.slope)
    until(11)
    second_norm_back(image, scatters[2][0], gathers[1][0])
    gathers[1][1].got_core()
    attend_back(text, core_mp)
    scatters[3][1].near.start()
    until(12)
    attend_back(image, own_mp)
    until(13)
    gathers[1][0].got_core()
    attend_back(image, core_mp)
    scatters[3][0].near.start()
    until(14)
    gathers[1][1].got_across()
    attend_back(text, across_mp)
    until(15)
    gathers[1][1].got_diag()
    attend_back(text, diag_mp)
    scatters[3][1].far.start()
    until(16)
    gathers[1][1].sent()
    scatters[3][1].send_over()
    gathers[1][0].got_across()
    attend_back(image, across_mp)
    until(17)
    gathers[1][0].got_diag()
    attend_back(image, diag_mp)
    scatters[3][0].far.start()
    until(18)
    gathers[1][0].sent()
    scatters[3][0].send_over()
    for scatter in scatters[1]:
        scatter.far.start()
        scatter.near.start()
    outer_attention(text)
    until(19)
    outer_attention(image)
    until(20)

    def first_norm_back(tower, scatter, gather):
        normed_grad = scatter.result()
        white, scale = whitened(tower.own_tokens[...].astype(FULL))
        vectors = tower.mixed_vectors
        vectors[own_mp, 0:1, :] = col_sum(normed_grad * white)
        vectors[own_mp, 1:2, :] = col_sum(normed_grad)
        more = whitened_back(white, scale, tower.norms[0:1, :], normed_grad)
        put_back(tower, get_back(tower) + more)
        gather.start()
        store = pltpu.make_async_copy(
            tower.back, tower.token_place(own_mp), r.store_sems.at[2 + tower.index]
        )
        store.start()
        return store

    token_stores = [first_norm_back(text, scatters[3][1], gathers[2][1])]
    until(23)
    token_stores.append(first_norm_back(image, scatters[3][0], gathers[2][0]))
    for scatter in scatters[1]:
        scatter.send_over()
    trades = []
    for tower in (image, text):
        vectors = tower.mixed_vectors
        for k, peer in enumerate((core, across, diag)):
            mine = vectors.at[own_mp]
            trades.append(remote(mine, mine, trade_sems, 3 * tower.index + k, peer))
            trades[-1].start()
    until(33)

    def result_rows(tower, scatter, gather):
        values = tower.resid[...] + scatter.result() + tower.shifts[1:2, :]
        place = lax.broadcasted_iota(jnp.int32, (tower.rows, 1), 0)
        alive = live(tower, own_mp, place)
        if alive is not None:
            values = jnp.where(alive, values, 0.0)
        tower.carried[tower.at(own_mp), :] = values.astype(LOW).astype(FULL)
        gather.start()

    result_rows(text, scatters[1][1], gathers[3][1])
    result_rows(image, scatters[1][0], gathers[3][0])
    until(35)
    for gather in gathers[2]:
        gather.got_core()
        gather.got_across()
    until(37)
    for trade in trades:
        trade.wait()
    vec_start = places[0, "vectors"][0]
    left = summed.shape[0] - vec_start
    summed[vec_start:, :] = jnp.zeros((left, LANES), FULL)
    for tower in (image, text):
        vectors = tower.mixed_vectors
        sums = vectors[0] + vectors[1] + vectors[2] + vectors[3]
        vectors[own_mp] = sums
        heads = tower.across_heads
        vectors[own_mp, 6:7, :] = tower.offset_grad[...]
        vectors[own_mp, 7:8, 0:heads] = tower.bias_grad[:, 0:heads]
        vectors[own_mp, 7:8, heads : 2 * heads] = tower.bias_grad[:, 2 * heads : 3 * heads]
        put(tower, "vectors", vectors[own_mp])
    until(43)
    gathers[3][1].got_core()
    gathers[3][1].got_across()
    gathers[3][0].got_core()
    gathers[3][0].got_across()
    until(45)
    result_stores = []
    for tower in (text, image):
        gathers[3][tower.index].got_diag()
        for owner in range(4):
            at = tower.at(owner)
            values = tower.carried[at, :]
            if tower is text:
                tower.tokens[at, :] = values.astype(LOW)
            else:
                for k in range(2):
                    part = values[k * tower.per : (k + 1) * tower.per]
                    blank = jnp.zeros((tower.tokens.shape[1] - tower.per, tower.wide), FULL)
                    tower.tokens[2 * owner + k] = jnp.concatenate([part, blank], axis=0).astype(LOW)
        result_stores.append(
            pltpu.make_async_copy(tower.tokens, tower.result, r.store_sems.at[5 + tower.index])
        )
        result_stores[-1].start()
    until(ticks)
    for gather in gathers[2]:
        gather.got_diag()
    for gather in gathers[2] + gathers[3]:
        gather.sent()
    for copy in token_stores + result_stores + [blank_store]:
        copy.wait()
    out_copy.wait()


LOADED = ("tokens", "inward", "outward", "expand", "contract", "embed")
FAR = "_far"


def block_call(count, towers, post_norms, logit_scale, scalars, collective_id):
    names, args, in_specs = [], [], []
    outs, out_names, out_specs = [], [], []
    scratch, scratch_names = [], []
    vmem, smem, anywhere = pltpu.VMEM, pltpu.SMEM, pl.ANY

    def give(index, space, **named):
        for name, value in named.items():
            names.append((index, name))
            args.append(value)
            in_specs.append(pl.BlockSpec(memory_space=space))

    def take(index, space, kind=FULL, **named):
        for name, shape in named.items():
            out_names.append((index, name))
            outs.append(jax.ShapeDtypeStruct(shape, kind))
            out_specs.append(pl.BlockSpec(memory_space=space))

    def hold(index, **named):
        for name, what in named.items():
            scratch_names.append((index, name))
            scratch.append(what)

    examples = 8 * count
    sizes = []
    for index, tower in enumerate(towers):
        give(index, anywhere, cotangent_far=tower["cotangent"])
        for name in LOADED:
            give(index, anywhere, **{name + FAR: tower[name]})
            hold(index, **{name: vmem(tower[name].shape, LOW)})
        for name in ("norms", "biases", "shifts", "offsets"):
            give(index, vmem, **{name: tower[name]})
        rows, wide, spaces = 8 * IMG_ROWS, tower["tokens"].shape[-1], tower["tokens"].shape
        if index:
            rows, spaces = 8 * TXT_ROWS, (8, TXT_ROWS, wide)
        heads, hidden, quarter = tower["biases"].shape[1], tower["offsets"].size, rows // 4
        size = Fields()
        size.index, size.wide, size.across_heads, size.hidden = index, wide, heads, hidden
        sizes.append(size)
        take(index, anywhere, token_grad=spaces, embed_grad=tower["embed"].shape)
        take(index, anywhere, LOW, result=tower["tokens"].shape)
        hold(
            index,
            joined=vmem((wide, 3 * heads), LOW),
            normed=vmem((rows, wide), LOW),
            qkv=vmem((rows, 3 * heads), LOW),
            mixed=vmem((rows, heads), LOW),
            normed_two=vmem((rows, wide), LOW),
            active=vmem((rows, hidden), LOW),
            slope=vmem((rows, hidden), LOW),
            bias_row=vmem((1, 3 * heads), FULL),
            offset_row=vmem((1, hidden), FULL),
            resid=vmem((quarter, wide), FULL),
            carried=vmem((rows, wide), FULL),
            back=vmem((2, quarter // 2, wide), FULL),
            own_tokens=vmem((quarter, wide), LOW),
            low_grad=vmem((rows, wide), LOW),
            parts0=vmem((rows, wide), FULL),
            near0=vmem((2, quarter, wide), FULL),
            over0=vmem((quarter, wide), FULL),
            parts1=vmem((rows, wide), FULL),
            near1=vmem((2, quarter, wide), FULL),
            over1=vmem((quarter, wide), FULL),
            top=vmem((8, 1, wide), FULL),
            every_row=vmem((examples, wide), FULL),
            early=vmem((8, wide), FULL),
            first=vmem((4, 8, wide), FULL),
            second=vmem((4, 8, wide), FULL),
            offset_grad=vmem((1, hidden), FULL),
            bias_grad=vmem((1, 3 * heads), FULL),
            mixed_vectors=vmem((4, 8, wide), FULL),
        )
    _, held = gradient_rows(sizes)
    held += -held % SPAN
    give(2, vmem, post_norms=post_norms, logit_scale=logit_scale)
    give(2, smem, **scalars)
    take(2, anywhere, summed_far=(held, LANES))
    take(2, vmem, loss=(1, 1), hits=(1, 1), scale_grad=(1, 1), post_grad=post_norms.shape)
    wide = sizes[0].wide
    dma = pltpu.SemaphoreType.DMA
    rings = dp_rings()
    hold(
        2,
        summed=vmem((held, LANES), FULL),
        marks=vmem((examples, 128), FULL),
        every=vmem((4, count, 4, wide), FULL),
        load_sems=dma((2 * len(LOADED) + 2,)),
        store_sems=dma((8,)),
        blank=vmem((8, towers[0]["tokens"].shape[1] - IMG_ROWS, wide), FULL),
        scatter_send=dma((24,)),
        scatter_recv=dma((24,)),
        gather_send=dma((24,)),
        gather_recv=dma((24,)),
        swap_send=dma((15,)),
        swap_recv=dma((15,)),
        spread_send=dma((count,)),
        spread_recv=dma((count,)),
        trade_send=dma((6,)),
        trade_recv=dma((6,)),
        ring0=rings[0],
        ring1=rings[1],
        ring2=rings[2],
        ring3=rings[3],
        ring4=rings[4],
        ring5=rings[5],
        dp_send=rings[6],
        dp_recv=rings[7],
        dp_credit=rings[8],
    )
    results = pl.pallas_call(
        functools.partial(block_kernel, count, names + out_names + scratch_names),
        out_shape=outs,
        in_specs=in_specs,
        out_specs=out_specs,
        scratch_shapes=scratch,
        compiler_params=pltpu.CompilerParams(
            collective_id=collective_id, has_side_effects=True, vmem_limit_bytes=64 << 20
        ),
        name="block",
    )(*args)
    out = [Fields(), Fields(), Fields()]
    for (index, name), value in zip(out_names, results):
        setattr(out[index], name, value)
    return out, sizes


def finish_kernel(where, names, *refs):
    r = Fields()
    for name, ref in zip(names, refs):
        setattr(r, name, ref)
    copies = []

    def move(source, target):
        copies.append(pltpu.make_async_copy(source, target, r.sems.at[len(copies)]))
        copies[-1].start()

    def load(source, target):
        move(source, target)
        return copies[-1]

    def load_weight(index, name):
        start, rows, width = where[index, name]
        at = pl.ds(start, rows * (width // LANES))
        return load(r.summed.at[at], r.held.at[at])

    kinds, wide, heads = r.inward_t.shape
    high = wide // 2
    start, _, _ = where[0, "vectors"]
    vectors = load(r.summed.at[start : start + 40], r.vectors)
    rows_loaded = load(r.token_grad_t, r.text_rows)
    low_loaded = load(r.result_t, r.text_low)
    weights = [
        (index, name, load_weight(index, name), target)
        for index, name, target in (
            (0, "contract", r.contract_i),
            (0, "expand", r.expand_i),
            (0, "inward", r.inward_i),
            (0, "outward", r.outward_i),
            (1, "contract", r.contract_t),
            (1, "expand", r.expand_t),
            (1, "inward", None),
            (1, "outward", r.outward_t),
        )
    ]
    others = [
        (load(source, held), held, target)
        for source, held, target in (
            (r.token_grad_i, r.held_tokens, r.tokens_i),
            (r.embed_grad_i, r.held_embed_i, r.embed_i),
            (r.embed_grad_t, r.held_embed_t, r.embed_t),
            (r.result_i, r.held_result, r.image_result),
        )
    ]
    first = len(copies)
    for index, name, loaded, target in weights:
        loaded.wait()
        start, rows, width = where[index, name]
        if target is not None:
            for k in range(width // LANES):
                source = r.held.at[start + k * rows : start + (k + 1) * rows]
                move(source, target.at[:, k * LANES : (k + 1) * LANES])
            continue
        for k in range(kinds):
            for side in range(2):
                source = r.held.at[
                    start + k * high : start + (k + 1) * high, side * heads : (side + 1) * heads
                ]
                move(source, r.inward_t.at[k, side * high : (side + 1) * high])
    for loaded, held, target in others:
        loaded.wait()
        move(held, target)
    for loaded in (vectors, rows_loaded, low_loaded):
        loaded.wait()
    context, examples, _ = r.tokens_t.shape
    for e in range(examples):
        r.tokens_t[:, e, :] = r.text_rows[e][0:context]
        r.text_turned[:, e, :] = r.text_low[e * TXT_ROWS : (e + 1) * TXT_ROWS].astype(FULL)[0:context]
    r.text_result[...] = r.text_turned[...].astype(LOW)
    at = 0
    for norms, shifts, offsets, biases in (
        (r.norms_i, r.shifts_i, r.offsets_i, r.biases_i),
        (r.norms_t, r.shifts_t, r.offsets_t, r.biases_t),
    ):
        count = norms.shape[1] // LANES
        rows = jnp.concatenate([r.vectors[at + 8 * k : at + 8 * k + 8, :] for k in range(count)], axis=1)
        at += 8 * count
        norms[...] = rows[0:4]
        shifts[...] = rows[4:6]
        offsets[...] = jnp.concatenate(
            [rows[6:7, k * 128 : (k + 1) * 128] for k in range(offsets.shape[0])], axis=0
        )
        heads = biases.shape[1]
        biases[...] = jnp.concatenate([rows[7:8, 0:heads], rows[7:8, heads : 2 * heads]], axis=0)
    for copy in copies[first:]:
        copy.wait()


def finish_call(out, where, shapes, context, biases_i, biases_t):
    names, outs, out_specs = [], [], []
    given = dict(
        summed=out[2].summed_far,
        token_grad_i=out[0].token_grad,
        token_grad_t=out[1].token_grad,
        result_i=out[0].result,
        result_t=out[1].result,
        embed_grad_i=out[0].embed_grad,
        embed_grad_t=out[1].embed_grad,
    )

    def take(space, kind=FULL, **named):
        for name, shape in named.items():
            names.append(name)
            outs.append(jax.ShapeDtypeStruct(shape, kind))
            out_specs.append(pl.BlockSpec(memory_space=space))

    for name, shape in shapes.items():
        take(pl.ANY, **{name: shape})
    examples, patch, wide_i = out[0].token_grad.shape
    wide_t = out[1].token_grad.shape[2]
    take(pl.ANY, LOW, image_result=(examples, patch, wide_i))
    take(pltpu.VMEM, LOW, text_result=(context, examples, wide_t))
    take(pltpu.VMEM, tokens_t=(context, examples, wide_t))
    for name, shape in dict(norms=4, shifts=2).items():
        take(pltpu.VMEM, **{name + "_i": (shape, wide_i), name + "_t": (shape, wide_t)})
    take(pltpu.VMEM, offsets_i=(shapes["expand_i"][1] // 128, 128))
    take(pltpu.VMEM, offsets_t=(shapes["expand_t"][1] // 128, 128))
    take(pltpu.VMEM, biases_i=biases_i, biases_t=biases_t)
    scratch = dict(
        vectors=pltpu.VMEM((40, LANES), FULL),
        text_rows=pltpu.VMEM(out[1].token_grad.shape, FULL),
        text_low=pltpu.VMEM(out[1].result.shape, LOW),
        text_turned=pltpu.VMEM((context, examples, wide_t), FULL),
        held=pltpu.VMEM(out[2].summed_far.shape, FULL),
        held_tokens=pltpu.VMEM(out[0].token_grad.shape, FULL),
        held_embed_i=pltpu.VMEM(out[0].embed_grad.shape, FULL),
        held_embed_t=pltpu.VMEM(out[1].embed_grad.shape, FULL),
        held_result=pltpu.VMEM(out[0].result.shape, LOW),
        sems=pltpu.SemaphoreType.DMA((64,)),
    )
    results = pl.pallas_call(
        functools.partial(finish_kernel, where, list(given) + names + list(scratch)),
        out_shape=outs,
        in_specs=[pl.BlockSpec(memory_space=pl.ANY)] * len(given),
        out_specs=out_specs,
        scratch_shapes=list(scratch.values()),
        compiler_params=pltpu.CompilerParams(vmem_limit_bytes=62 << 20),
        name="finish",
    )(*given.values())
    fields = Fields()
    for name, value in zip(names, results):
        setattr(fields, name, value)
    return fields


def shards(
    count,
    image_tokens,
    image_norms,
    image_inward,
    image_biases,
    image_outward,
    image_shifts,
    image_expand,
    image_offsets,
    image_contract,
    image_embed,
    text_tokens,
    text_norms,
    text_inward,
    text_biases,
    text_outward,
    text_shifts,
    text_expand,
    text_offsets,
    text_contract,
    text_embed,
    post_norms,
    logit_scale,
    image_cotangent,
    text_cotangent,
    resolution,
    validity,
    text_ends,
):
    examples, patch, image_width = image_tokens.shape
    context, text_width = text_tokens.shape[1:]

    def fit(values):
        grow = ((0, 0), (0, TXT_ROWS - context), (0, 0))
        return jnp.pad(values, grow).reshape(-1, values.shape[2])

    image = dict(
        tokens=image_tokens,
        inward=jnp.swapaxes(image_inward, 1, 2),
        outward=image_outward,
        expand=image_expand,
        contract=image_contract,
        embed=image_embed,
        cotangent=image_cotangent,
        norms=image_norms,
        biases=image_biases,
        shifts=image_shifts,
        offsets=image_offsets.reshape(-1, 128),
    )
    text = dict(
        tokens=fit(text_tokens),
        inward=text_inward,
        outward=text_outward,
        expand=text_expand,
        contract=text_contract,
        embed=text_embed,
        cotangent=fit(text_cotangent),
        norms=text_norms,
        biases=text_biases,
        shifts=text_shifts,
        offsets=text_offsets.reshape(-1, 128),
    )
    scalars = dict(resolution=resolution, validity=validity, ends=text_ends)
    out, sizes = block_call(
        count, (image, text), post_norms, logit_scale.reshape(1, 1), scalars, 0
    )
    where, _ = gradient_rows(sizes)
    shapes = dict(
        contract_i=image_contract.shape,
        expand_i=image_expand.shape,
        outward_i=image_outward.shape,
        inward_i=(image_inward.shape[0] * image_inward.shape[2], image_width),
        embed_i=image_embed.shape,
        tokens_i=image_tokens.shape,
        contract_t=text_contract.shape,
        expand_t=text_expand.shape,
        outward_t=text_outward.shape,
        inward_t=text_inward.shape,
        embed_t=text_embed.shape,
    )
    end = finish_call(out, where, shapes, context, image_biases.shape, text_biases.shape)
    inward_i = end.inward_i.reshape(image_inward.shape[0], -1, image_width)
    return (
        end.image_result,
        jnp.swapaxes(end.text_result, 0, 1),
        out[2].loss.reshape(1),
        out[2].hits.reshape(1),
        end.tokens_i,
        jnp.swapaxes(end.tokens_t, 0, 1),
        end.norms_i,
        jnp.swapaxes(inward_i, 1, 2),
        end.biases_i,
        end.outward_i,
        end.shifts_i,
        end.expand_i,
        end.offsets_i.reshape(-1),
        end.contract_i,
        end.embed_i,
        end.norms_t,
        end.inward_t,
        end.biases_t,
        end.outward_t,
        end.shifts_t,
        end.expand_t,
        end.offsets_t.reshape(-1),
        end.contract_t,
        end.embed_t,
        out[2].post_grad,
        out[2].scale_grad.reshape(1),
    )


def solution(mesh):
    placed = (
        P("dp", None, None),
        P(),
        P(None, None, "mp"),
        P(None, "mp"),
        P("mp", None),
        P(),
        P(None, "mp"),
        P("mp"),
        P("mp", None),
        P(),
        P("dp", None, None),
        P(),
        P(None, None, "mp"),
        P(None, "mp"),
        P("mp", None),
        P(),
        P(None, "mp"),
        P("mp"),
        P("mp", None),
        P(),
        P(),
        P(),
        P("dp", None, None),
        P("dp", None, None),
        P("dp"),
        P("dp"),
        P("dp"),
    )
    return jax.shard_map(
        functools.partial(shards, mesh.shape["dp"]),
        mesh=mesh,
        in_specs=placed,
        out_specs=(
            P("dp", None, None),
            P("dp", None, None),
            P(),
            P(),
            P("dp", None, None),
            P("dp", None, None),
            P(),
            P(None, None, "mp"),
            P(None, "mp"),
            P("mp", None),
            P(),
            P(None, "mp"),
            P("mp"),
            P("mp", None),
            P(),
            P(),
            P(None, None, "mp"),
            P(None, "mp"),
            P("mp", None),
            P(),
            P(None, "mp"),
            P("mp"),
            P("mp", None),
            P(),
            P(),
            P(),
        ),
        check_vma=False,
    )
```

```python
import functools

import jax
import jax.numpy as jnp
from jax import lax
from jax.experimental import pallas as pl
from jax.experimental.pallas import tpu as pltpu
from jax.sharding import PartitionSpec as P

MESH = pl.DeviceIdType.MESH
HEAD = 64
LOW_LEN = 50
HIGH_LEN = 101
IMG_ROWS = 104
TXT_ROWS = 80
SPAN = 224
SLOTS = 4
LANES = 256

EPSILON = 1e-05
MASKED = -1000000000.0
HIGHEST = lax.Precision.HIGHEST


def dp_sum_machine(count, blocks, total, rings, sends, recvs, credits):
    places = count // 2
    deep = places // 2
    dp, mp = lax.axis_index("dp"), lax.axis_index("mp")
    side, place = lax.rem(dp, 2), dp // 2
    low = place < deep
    depth = jnp.where(low, place, places - 1 - place)
    inner = jnp.where(low, place + 1, place - 1)
    outer = jnp.clip(jnp.where(low, place - 1, place + 1), 0, places - 1)
    half = jnp.where(low, 0, 1)
    pair_id = (place * 2 + 1 - side, mp)
    inner_id = (inner * 2 + side, mp)
    outer_id = (outer * 2 + side, mp)
    quarter = SPAN // 4

    def part(offset, size):
        def at(block):
            start = pl.multiple_of(block * SPAN + offset, quarter)
            return total.at[pl.ds(start, size)]

        return at

    kept = part(side * quarter, quarter)
    given = part((1 - side) * quarter, quarter)
    whole = part(2 * quarter, 2 * quarter)
    mid_kept = part((2 + half) * quarter, quarter)
    mid_given = part((3 - half) * quarter, quarter)
    middle = depth == deep - 1
    not_middle = depth < deep - 1
    not_end = depth > 0
    yes = depth >= 0

    kinds = [
        (yes, 0, given, pair_id, yes, 0, pair_id, rings[0], kept),
        (not_middle, depth, whole, inner_id, not_end, depth - 1, outer_id, rings[1], whole),
        (not_middle, depth + 1, kept, inner_id, not_end, depth, outer_id, rings[2], kept),
        (middle, deep - 1, mid_given, inner_id, middle, deep - 1, inner_id, rings[3], mid_kept),
        (middle, deep, mid_kept, pair_id, middle, deep, pair_id, rings[4], mid_kept),
        (middle, deep, kept, inner_id, middle, deep, inner_id, rings[5], kept),
        (middle, deep + 1, mid_kept, inner_id, middle, deep + 1, inner_id, None, mid_given),
        (not_end, 2 * deep - depth, kept, outer_id, not_middle, 2 * deep - depth - 1, inner_id, None, kept),
        (not_end, 2 * deep + 1 - depth, whole, outer_id, not_middle, 2 * deep - depth, inner_id, None, whole),
        (yes, 2 * deep, kept, pair_id, yes, 2 * deep, pair_id, None, given),
    ]

    def copy(k, kind, block):
        _, _, src, target, _, _, _, ring, land = kind
        slot = lax.rem(block, SLOTS)
        dst = src(block) if ring is None else ring.at[slot]
        return pltpu.make_async_remote_copy(
            src_ref=src(block),
            dst_ref=dst,
            send_sem=sends.at[k, slot],
            recv_sem=recvs.at[k, slot],
            device_id=target,
            device_id_type=MESH,
        )

    def valid(block):
        return jnp.logical_and(block >= 0, block < blocks)

    def start(t):
        for k, kind in enumerate(kinds):
            block = t - 2 * kind[1]

            @pl.when(jnp.logical_and(kind[0], valid(block)))
            def _():
                @pl.when(block >= SLOTS)
                def _():
                    pl.semaphore_wait(credits.at[k], 1)

                copy(k, kind, block).start()

    def finish(t):
        for k, kind in enumerate(kinds):
            sends_it, sent_stage, _, _, takes_it, got_stage, source, ring, land = kind
            sent = t - 2 * sent_stage
            got = t - 2 * got_stage

            @pl.when(jnp.logical_and(sends_it, valid(sent)))
            def _():
                copy(k, kind, sent).wait_send()

            @pl.when(jnp.logical_and(takes_it, valid(got)))
            def _():
                copy(k, kind, got).wait_recv()
                if ring is not None:
                    here = land(got)
                    here[...] = here[...] + ring[lax.rem(got, SLOTS)]

                @pl.when(got < blocks - SLOTS)
                def _():
                    pl.semaphore_signal(credits.at[k], inc=1, device_id=source, device_id_type=MESH)

    def tick(t):
        start(t)

        @pl.when(t > 0)
        def _():
            finish(t - 1)

    return tick, blocks + 4 * deep + 1


def dp_rings():
    quarter = SPAN // 4
    sizes = [quarter, 2 * quarter, quarter, quarter, quarter, quarter]
    return [pltpu.VMEM((SLOTS, size, LANES), jnp.float32) for size in sizes] + [
        pltpu.SemaphoreType.DMA((10, SLOTS)),
        pltpu.SemaphoreType.DMA((10, SLOTS)),
        pltpu.SemaphoreType.REGULAR((10,)),
    ]


LOW, FULL = jnp.bfloat16, jnp.float32


def mm(left, right):
    return jnp.dot(left, right, preferred_element_type=FULL)


def mm_nt(left, right, precision=None):
    dims = (((1,), (1,)), ((), ()))
    return lax.dot_general(left, right, dims, precision=precision, preferred_element_type=FULL)


def mm_tn(left, right, precision=None):
    dims = (((0,), (0,)), ((), ()))
    return lax.dot_general(left, right, dims, precision=precision, preferred_element_type=FULL)


def row_sum(values):
    return jnp.sum(values, axis=1, keepdims=True)


def col_sum(values):
    return jnp.sum(values, axis=0, keepdims=True)


def whitened(values):
    width = values.shape[1]
    centred = values - row_sum(values) * (1.0 / width)
    scale = lax.rsqrt(row_sum(centred * centred) * (1.0 / width) + EPSILON)
    return centred * scale, scale


def whitened_back(white, scale, gain, gradient):
    width = white.shape[1]
    inner = gradient * gain
    mean = row_sum(inner) * (1.0 / width)
    slope = row_sum(inner * white) * (1.0 / width)
    return scale * (inner - mean - white * slope)


class Fields:
    pass


class Tower:
    def __init__(self, index, rows, per, fields):
        self.__dict__.update(fields.__dict__)
        self.index, self.rows, self.per = index, rows, per
        self.wide = self.shifts.shape[1]
        self.across_heads = self.biases.shape[1]
        self.hidden = self.offsets.shape[0] * 128
        self.panels = self.wide // LANES

    def at(self, owner):
        return pl.ds(pl.multiple_of(owner * self.rows, self.rows), self.rows)

    def token_place(self, owner):
        return self.token_grad.at[pl.ds(2 * owner, 2), pl.ds(0, self.per)]


def gradient_rows(towers):
    image, text = towers
    where, start = {}, 0
    for tower, name, rows in (
        (text, "contract", text.hidden),
        (text, "expand", text.wide),
        (image, "contract", image.hidden),
        (image, "expand", image.wide),
        (text, "outward", text.across_heads),
        (text, "inward", 3 * text.across_heads),
        (image, "outward", image.across_heads),
        (image, "inward", 3 * image.across_heads),
        (image, "vectors", 8),
        (text, "vectors", 8),
    ):
        width = tower.hidden if name == "expand" else tower.wide
        where[tower.index, name] = (start, rows, width)
        start += rows * (width // LANES)
    return where, start


def block_kernel(count, names, *refs):
    fields = [Fields(), Fields(), Fields()]
    for (index, name), ref in zip(names, refs):
        setattr(fields[index], name, ref)
    image = Tower(0, 2 * IMG_ROWS, IMG_ROWS, fields[0])
    text = Tower(1, 2 * TXT_ROWS, TXT_ROWS, fields[1])
    r = fields[2]
    places, _ = gradient_rows((image, text))
    deep = count // 4
    dp, mp = lax.axis_index("dp"), lax.axis_index("mp")
    flip, core_bit = mp // 2, lax.rem(mp, 2)
    core_mp = flip * 2 + 1 - core_bit
    across_mp = (1 - flip) * 2 + core_bit
    diag_mp = (1 - flip) * 2 + 1 - core_bit
    core, across, diag = (dp, core_mp), (dp, across_mp), (dp, diag_mp)
    own_mp = mp

    for tower in (text, image):
        tower.loads = {}
    for k, name in enumerate(LOADED):
        for tower in (text, image):
            source, target = getattr(tower, name + FAR), getattr(tower, name)
            copy = pltpu.make_async_copy(source, target, r.load_sems.at[2 * k + tower.index])
            copy.start()
            tower.loads[name] = copy
    r.blank[...] = jnp.zeros(r.blank.shape, FULL)
    blank_store = pltpu.make_async_copy(
        r.blank,
        image.token_grad.at[:, pl.ds(image.per, image.token_grad.shape[1] - image.per)],
        r.store_sems.at[7],
    )
    blank_store.start()
    barrier = pltpu.get_barrier_semaphore()
    friends = [core, across, diag] + [(lax.rem(dp + k, count), mp) for k in range(1, count)]
    for friend in friends:
        pl.semaphore_signal(barrier, inc=1, device_id=friend, device_id_type=MESH)

    scatter_sems = r.scatter_send, r.scatter_recv
    gather_sems = r.gather_send, r.gather_recv
    swap_sems = r.swap_send, r.swap_recv
    spread_sems = r.spread_send, r.spread_recv
    trade_sems = r.trade_send, r.trade_recv

    def remote(src, dst, group, k, peer):
        return pltpu.make_async_remote_copy(
            src_ref=src,
            dst_ref=dst,
            send_sem=group[0].at[k],
            recv_sem=group[1].at[k],
            device_id=peer,
            device_id_type=MESH,
        )

    class Scatter:
        def __init__(self, tower, phase, bank):
            self.tower = tower
            self.parts, self.near_buf, self.over_buf = (
                (tower.parts1, tower.near1, tower.over1)
                if bank
                else (tower.parts0, tower.near0, tower.over0)
            )
            k = (phase * 2 + tower.index) * 3
            self.far = remote(self.parts.at[tower.at(diag_mp)], self.near_buf.at[0], scatter_sems, k, core)
            self.near = remote(self.parts.at[tower.at(core_mp)], self.near_buf.at[1], scatter_sems, k + 1, core)
            self.over = remote(self.near_buf.at[0], self.over_buf, scatter_sems, k + 2, across)

        def send_over(self):
            self.far.wait()
            self.near_buf[0] = self.near_buf[0] + self.parts[self.tower.at(across_mp), :]
            self.over.start()

        def result(self):
            self.near.wait()
            self.over.wait()
            return self.parts[self.tower.at(own_mp), :] + self.near_buf[1] + self.over_buf[...]

    class Gather:
        def __init__(self, tower, phase):
            k = (phase * 2 + tower.index) * 3
            if phase == 2:
                source, mine, passed = (
                    tower.back,
                    tower.token_place(own_mp),
                    tower.token_place(across_mp),
                )
            else:
                mine = source = tower.carried.at[tower.at(own_mp)]
                passed = tower.carried.at[tower.at(across_mp)]
            self.one = remote(source, mine, gather_sems, k, across)
            self.two = remote(source, mine, gather_sems, k + 1, core)
            self.on = remote(passed, passed, gather_sems, k + 2, core)

        def start(self):
            self.one.start()
            self.two.start()

        def got_core(self):
            self.two.wait_recv()

        def got_across(self):
            self.one.wait_recv()
            self.on.start()

        def got_diag(self):
            self.on.wait_recv()

        def sent(self):
            self.one.wait_send()
            self.two.wait_send()
            self.on.wait_send()

    def length(example):
        return jnp.where(r.resolution[example] == 1, HIGH_LEN, LOW_LEN)

    def live(tower, owner, places_):
        if tower is text:
            return None
        first, second = length(2 * owner), length(2 * owner + 1) + tower.per
        return places_ < jnp.where(places_ < tower.per, first, second)

    def allowed(tower, owner):
        shape = (tower.rows, tower.rows)
        query = lax.broadcasted_iota(jnp.int32, shape, 0)
        key = lax.broadcasted_iota(jnp.int32, shape, 1)
        key_start = jnp.where(query < tower.per, 0, tower.per)
        if tower is text:
            end = query + 1
        else:
            first, second = length(2 * owner), length(2 * owner + 1) + tower.per
            end = jnp.where(query < tower.per, first, second)
        return jnp.logical_and(key >= key_start, key < end)

    def chosen_places(tower, owner):
        if tower is text:
            return r.ends[2 * owner], r.ends[2 * owner + 1] + tower.per
        return 0, tower.per

    def chosen_row(tower, example, read):
        first = example * tower.per
        if tower is image:
            return read(first, 16)[0:1]
        place = lax.broadcasted_iota(jnp.int32, (tower.per, 1), 0)
        rows = read(first, tower.per)
        return col_sum(jnp.where(place == r.ends[example], rows, 0.0))

    def softmax(tower, scores, mask):
        scores = jnp.where(mask, scores * HEAD ** (-0.5), MASKED)
        top = jnp.max(scores, axis=1, keepdims=True)
        weights = jnp.exp(scores - top)
        return weights * (1.0 / row_sum(weights))

    def owner_of(j):
        return lax.rem(flip + 1 - j // 2, 2) * 2 + lax.rem(core_bit + 1 - lax.rem(j, 2), 2)

    def prepare(tower):
        for name in ("tokens", "inward", "outward"):
            tower.loads[name].wait()
        heads = tower.across_heads
        if tower is text:
            for k in range(3):
                tower.joined[:, k * heads : (k + 1) * heads] = tower.inward[k]
        for k in range(tower.hidden // 128):
            tower.offset_row[:, k * 128 : (k + 1) * 128] = tower.offsets[k : k + 1, :]
        tower.bias_row[:, 0:heads] = tower.biases[0:1, :]
        tower.bias_row[:, heads : 2 * heads] = jnp.zeros((1, heads), FULL)
        tower.bias_row[:, 2 * heads : 3 * heads] = tower.biases[1:2, :]

    def rows_of(tower, owner):
        if tower is text:
            return tower.tokens[tower.at(owner), :].astype(FULL)
        pair = [tower.tokens[2 * owner + k].astype(FULL)[0 : tower.per] for k in range(2)]
        return jnp.concatenate(pair, axis=0)

    def into_heads(tower, normed):
        if tower is text:
            return mm(normed, tower.joined[...])
        return mm_nt(normed, tower.inward[...].reshape(3 * tower.across_heads, tower.wide))

    def out_of_heads(tower, grads):
        if tower is text:
            return mm_nt(grads, tower.joined[...])
        return mm(grads, tower.inward[...].reshape(3 * tower.across_heads, tower.wide))

    def attend(tower, owner):
        at, heads = tower.at(owner), tower.across_heads
        white, _ = whitened(rows_of(tower, owner))
        normed = (white * tower.norms[0:1, :] + tower.norms[1:2, :]).astype(LOW)
        tower.normed[at, :] = normed
        qkv = (into_heads(tower, normed) + tower.bias_row[...]).astype(LOW)
        tower.qkv[at, :] = qkv
        mask = allowed(tower, owner)
        mixed = []
        for h in range(heads // HEAD):
            query, key, value = (
                qkv[:, k * heads + h * HEAD : k * heads + (h + 1) * HEAD] for k in range(3)
            )
            weights = softmax(tower, mm_nt(query, key), mask)
            mixed.append(mm(weights.astype(LOW), value).astype(LOW))
        mixed = jnp.concatenate(mixed, axis=1)
        tower.mixed[at, :] = mixed
        tower.parts0[at, :] = mm(mixed, tower.outward[...])

    def attend_all(tower, scatter):
        def body(j, carry):
            attend(tower, owner_of(j))

            @pl.when(j == 0)
            def _():
                scatter.far.start()

            if tower is text:

                @pl.when(j == 1)
                def _():
                    scatter.send_over()

            @pl.when(j == 2)
            def _():
                scatter.near.start()

            return carry

        lax.fori_loop(0, 4, body, 0)
        tower.own_tokens[...] = rows_of(tower, own_mp).astype(LOW)

    def second_norm(tower, scatter):
        at = tower.at(own_mp)
        mine = tower.own_tokens[...].astype(FULL)
        resid = mine + scatter.result() + tower.shifts[0:1, :]
        tower.resid[...] = resid
        white, _ = whitened(resid)
        normed = (white * tower.norms[2:3, :] + tower.norms[3:4, :]).astype(LOW)
        tower.carried[at, :] = normed.astype(FULL)

    def feed(tower, owner):
        at = tower.at(owner)
        normed = tower.carried[at, :].astype(LOW)
        tower.normed_two[at, :] = normed
        hidden = mm(normed, tower.expand[...]) + tower.offset_row[...]
        gate = 1.0 / (1.0 + jnp.exp(-1.702 * hidden))
        active = (hidden * gate).astype(LOW)
        tower.active[at, :] = active
        tower.slope[at, :] = (gate * (1.0 + 1.702 * hidden * (1.0 - gate))).astype(LOW)
        tower.parts1[at, :] = mm(active, tower.contract[...])

    scatters = [[Scatter(t, phase, phase == 1) for t in (image, text)] for phase in range(4)]
    gathers = [[Gather(t, phase) for t in (image, text)] for phase in range(4)]

    every = r.every
    peers = (core, across, diag)

    def swap_all(buffer, tower, step):
        mine = buffer.at[own_mp]
        copies = [
            remote(mine, mine, swap_sems, (2 * step + tower.index) * 3 + k, peer)
            for k, peer in enumerate(peers)
        ]
        for copy in copies:
            copy.start()
        return copies

    def sum_of(buffer):
        return buffer[0] + buffer[1] + buffer[2] + buffer[3]

    def chosen_first(tower):
        def token_rows(first, rows):
            if tower is image:
                return tower.tokens[first // tower.per, 0:rows, :].astype(FULL)
            return tower.tokens[first : first + rows, :].astype(FULL)

        def part_rows(first, rows):
            return tower.parts0[first : first + rows, :]

        for e in range(8):
            tower.first[own_mp, e : e + 1, :] = chosen_row(tower, e, part_rows)
            tower.early[e : e + 1, :] = chosen_row(tower, e, token_rows) + tower.shifts[0:1, :]
        return swap_all(tower.first, tower, 0)

    def chosen_second(tower, copies):
        for copy in copies:
            copy.wait()
        resid = tower.early[...] + sum_of(tower.first)
        tower.early[...] = resid
        white, _ = whitened(resid)
        normed = (white * tower.norms[2:3, :] + tower.norms[3:4, :]).astype(LOW)
        hidden = mm(normed, tower.expand[...]) + tower.offset_row[...]
        active = (hidden * (1.0 / (1.0 + jnp.exp(-1.702 * hidden)))).astype(LOW)
        tower.second[own_mp] = mm(active, tower.contract[...])
        return swap_all(tower.second, tower, 1)

    def chosen_third(tower, copies):
        for copy in copies:
            copy.wait()
        final = tower.early[...] + sum_of(tower.second) + tower.shifts[1:2, :]
        for e in range(8):
            tower.top[e] = final[e : e + 1]
        for k in range(2):
            spot = 2 * tower.index + k
            every[own_mp, dp, spot : spot + 1, 0 : tower.wide] = tower.top[2 * own_mp + k]

    prepare(text)
    prepare(image)
    pl.semaphore_wait(barrier, len(friends))
    attend_all(text, scatters[0][1])
    attend_all(image, scatters[0][0])
    swaps = [chosen_first(tower) for tower in (image, text)]
    second_norm(text, scatters[0][1])
    for tower in (text, image):
        reload = pltpu.make_async_copy(
            tower.cotangent_far, tower.tokens, r.load_sems.at[2 * len(LOADED) + tower.index]
        )
        tower.loads["cotangent"] = reload
        reload.start()
        tower.loads["expand"].wait()
        tower.loads["contract"].wait()
    swaps = [chosen_second(tower, swaps[tower.index]) for tower in (image, text)]
    gathers[0][1].start()
    feed(text, own_mp)
    for k in range(2):
        mark = r.validity[2 * own_mp + k].astype(FULL)
        every[own_mp, dp, 2 + k : 3 + k, text.wide : text.wide + 128] = jnp.full((1, 128), mark, FULL)
    for tower in (image, text):
        chosen_third(tower, swaps[tower.index])
    mine = every.at[own_mp, dp]
    spread = [
        remote(mine, mine, spread_sems, k, (lax.rem(dp + k, count), mp)) for k in range(1, count)
    ]
    for copy in spread:
        copy.start()
    gathers[0][1].got_core()
    feed(text, core_mp)
    for copy in spread:
        copy.wait()
    one = remote(every.at[own_mp], every.at[own_mp], swap_sems, 12, across)
    two = remote(every.at[own_mp], every.at[own_mp], swap_sems, 13, core)
    on = remote(every.at[across_mp], every.at[across_mp], swap_sems, 14, core)
    one.start()
    two.start()
    scatters[0][0].send_over()
    gathers[0][1].got_across()
    feed(text, across_mp)
    one.wait_recv()
    on.start()
    gathers[0][1].got_diag()
    feed(text, diag_mp)
    two.wait_recv()
    on.wait_recv()
    for copy in (one, two, on):
        copy.wait_send()

    for place in range(count):
        for quarter in range(4):
            spot = (place * 4 + quarter) * 2
            block = every[quarter, place]
            image.every_row[spot : spot + 2, :] = block[0:2, :]
            text.every_row[spot : spot + 2, :] = block[2:4, 0 : text.wide]
            r.marks[spot : spot + 2, :] = block[2:4, text.wide : text.wide + 128]
    for tower in (text, image):
        tower.loads["embed"].wait()
    post = r.post_norms

    def head(tower, rows):
        lanes = slice(0, image.wide) if tower is image else slice(image.wide, image.wide + text.wide)
        white, scale = whitened(rows)
        low = (white * post[0:1, lanes] + post[1:2, lanes]).astype(LOW)
        raw = mm(low, tower.embed[...])
        inverse = lax.rsqrt(row_sum(raw * raw) + 1e-06)
        return lanes, white, scale, low, raw * inverse, inverse

    heads = [head(tower, tower.every_row[...]) for tower in (image, text)]
    unit_i, unit_t = heads[0][4], heads[1][4]
    marks = r.marks[...]
    examples = marks.shape[0]
    valid_col = marks[:, 0:1]
    valid_row = jnp.transpose(marks)[0:1, :]
    number = col_sum(valid_col)
    factor = jnp.exp(r.logit_scale[...])
    logits = factor * mm_nt(unit_i, unit_t, HIGHEST)
    by_row = jnp.where(valid_row > 0.5, logits, MASKED)
    by_col = jnp.where(valid_col > 0.5, logits, MASKED)
    row_top = jnp.max(by_row, axis=1, keepdims=True)
    row_lse = row_top + jnp.log(row_sum(jnp.exp(by_row - row_top)))
    col_top = jnp.max(by_col, axis=0, keepdims=True)
    col_lse = col_top + jnp.log(col_sum(jnp.exp(by_col - col_top)))
    diagonal = factor * row_sum(unit_i * unit_t)
    loss = col_sum(valid_col * (row_lse - 2.0 * diagonal)) + row_sum(valid_row * col_lse)
    r.loss[...] = loss / (2.0 * number)
    r.hits[...] = col_sum(valid_col * jnp.exp(diagonal - row_lse))
    row_id = lax.broadcasted_iota(jnp.int32, (examples, examples), 0)
    col_id = lax.broadcasted_iota(jnp.int32, (examples, examples), 1)
    same = jnp.where(row_id == col_id, 1.0, 0.0)
    pairs = (
        valid_col * (jnp.exp(by_row - row_lse) - same)
        + valid_row * (jnp.exp(by_col - col_lse) - same)
    ) / (2.0 * number)
    r.scale_grad[...] = col_sum(row_sum(pairs * logits))
    unit_grads = [
        factor * lax.dot(pairs, unit_t, precision=HIGHEST, preferred_element_type=FULL),
        factor * mm_tn(pairs, unit_i, HIGHEST),
    ]
    stores = []
    for tower, (lanes, white, scale, low, unit, inverse), grad in zip((image, text), heads, unit_grads):
        raw_grad = (inverse * (grad - unit * row_sum(unit * grad))).astype(LOW)
        spare = tower.parts1 if tower is image else tower.parts0
        home = spare.at[0 : tower.wide, 0 : tower.embed.shape[1]]
        home[...] = mm_tn(low, raw_grad)
        stores.append(pltpu.make_async_copy(home, tower.embed_grad, r.store_sems.at[tower.index]))
        stores[-1].start()
        low_grad = mm_nt(raw_grad, tower.embed[...])
        r.post_grad[0:1, lanes] = col_sum(low_grad * white)
        r.post_grad[1:2, lanes] = col_sum(low_grad)
        tower.every_row[...] = whitened_back(white, scale, post[0:1, lanes], low_grad)
        own = tower.every_row[pl.ds(pl.multiple_of(dp * 8, 8), 8), :]
        for k in range(8):
            tower.top[k] = own[k : k + 1, :]

    def grad_rows(tower, owner):
        place = lax.broadcasted_iota(jnp.int32, (tower.rows, 1), 0)
        values = rows_of(tower, owner)
        alive = live(tower, owner, place)
        if alive is not None:
            values = jnp.where(alive, values, 0.0)
        for k, at in enumerate(chosen_places(tower, owner)):
            values = values + jnp.where(place == at, tower.top[2 * owner + k], 0.0)
        return values

    def low_rows(tower):
        def body(owner, carry):
            tower.low_grad[tower.at(owner), :] = grad_rows(tower, owner).astype(LOW)
            return carry

        lax.fori_loop(0, 4, body, 0)

    def feed_back(tower, j, scatter):
        owner = owner_of(j)
        at = tower.at(owner)
        low = tower.low_grad[at, :]
        active_grad = mm_nt(low, tower.contract[...]).astype(LOW).astype(FULL)
        hidden_grad = active_grad * tower.slope[at, :].astype(FULL)
        tower.offset_grad[...] = tower.offset_grad[...] + col_sum(hidden_grad)
        hidden_low = hidden_grad.astype(LOW)
        tower.slope[at, :] = hidden_low
        tower.parts0[at, :] = mm_nt(hidden_low, tower.expand[...])

        @pl.when(j == 0)
        def _():
            scatter.far.start()

        @pl.when(j == 2)
        def _():
            scatter.near.start()

    def put_back(tower, values):
        tower.back[...] = values.reshape(2, tower.per, tower.wide)

    def get_back(tower):
        return tower.back[...].reshape(tower.rows, tower.wide)

    summed = r.summed

    def put(tower, name, values, first=0):
        start, rows, width = places[tower.index, name]
        for k in range(width // LANES):
            to = pl.ds(pl.multiple_of(start + k * rows + first, 8), values.shape[0])
            summed[to, :] = values[:, k * LANES : (k + 1) * LANES]

    def outer(tower, name, left, right):
        def body(j, carry):
            cut = pl.ds(pl.multiple_of(j * LANES, LANES), LANES)
            put(tower, name, mm_tn(left[:, cut], right[...]), j * LANES)
            return carry

        lax.fori_loop(0, left.shape[1] // LANES, body, 0)

    rings = [r.ring0, r.ring1, r.ring2, r.ring3, r.ring4, r.ring5]
    tick, ticks = dp_sum_machine(
        count, summed.shape[0] // SPAN, summed, rings, r.dp_send, r.dp_recv, r.dp_credit
    )
    out_copy = pltpu.make_async_copy(summed, r.summed_far, r.store_sems.at[4])
    clock = [0]

    def go(number):
        def body(t, carry):
            tick(t)
            done = t - 1 - 4 * deep

            @pl.when(done >= 0)
            def _():
                at = pl.ds(pl.multiple_of(done * SPAN, SPAN), SPAN)
                pltpu.make_async_copy(
                    summed.at[at], r.summed_far.at[at], r.store_sems.at[4]
                ).start()

            return carry

        lax.fori_loop(clock[0], clock[0] + number, body, 0)
        clock[0] += number

    def until(number):
        go(number - clock[0])

    for copy in stores:
        copy.wait()

    def begin_back(tower):
        tower.loads["cotangent"].wait()
        tower.offset_grad[...] = jnp.zeros(tower.offset_grad.shape, FULL)
        tower.bias_grad[...] = jnp.zeros(tower.bias_grad.shape, FULL)
        grads = grad_rows(tower, own_mp)
        put_back(tower, grads)
        tower.mixed_vectors[own_mp] = jnp.zeros((8, tower.wide), FULL)
        tower.mixed_vectors[own_mp, 5:6, :] = col_sum(grads)

    def feed_back_loop(tower, first, last, scatter):
        def body(j, carry):
            feed_back(tower, j, scatter)
            return carry

        lax.fori_loop(first, last, body, 0)

    begin_back(text)
    low_rows(text)
    outer(text, "contract", text.active, text.low_grad)
    until(1)
    gathers[0][1].sent()
    feed_back_loop(text, 0, 4, scatters[2][1])
    until(2)
    outer(text, "expand", text.normed_two, text.slope)
    begin_back(image)
    until(3)
    second_norm(image, scatters[0][0])
    gathers[0][0].start()
    scatters[2][1].send_over()
    feed(image, own_mp)
    until(5)
    low_rows(image)
    gathers[0][0].got_core()
    feed(image, core_mp)
    until(6)
    feed_back_loop(image, 2, 4, scatters[2][0])
    until(7)
    gathers[0][0].got_across()
    feed(image, across_mp)
    gathers[0][0].got_diag()
    feed(image, diag_mp)
    outer(image, "contract", image.active, image.low_grad)
    until(8)
    gathers[0][0].sent()
    feed_back_loop(image, 0, 2, scatters[2][0])
    scatters[2][0].send_over()
    until(10)

    def second_norm_back(tower, scatter, gather):
        normed_grad = scatter.result()
        white, scale = whitened(tower.resid[...])
        vectors = tower.mixed_vectors
        vectors[own_mp, 2:3, :] = col_sum(normed_grad * white)
        vectors[own_mp, 3:4, :] = col_sum(normed_grad)
        grads = get_back(tower) + whitened_back(white, scale, tower.norms[2:3, :], normed_grad)
        vectors[own_mp, 4:5, :] = col_sum(grads)
        put_back(tower, grads)
        tower.carried[tower.at(own_mp), :] = grads.astype(LOW).astype(FULL)
        gather.start()

    def attend_back(tower, owner):
        at, heads = tower.at(owner), tower.across_heads
        low = tower.carried[at, :].astype(LOW)
        tower.low_grad[at, :] = low
        mixed_grad = mm_nt(low, tower.outward[...]).astype(LOW)
        qkv = tower.qkv[at, :]
        mask = allowed(tower, owner)
        grads = [[], [], []]
        for h in range(heads // HEAD):
            query, key, value = (
                qkv[:, k * heads + h * HEAD : k * heads + (h + 1) * HEAD] for k in range(3)
            )
            weights = softmax(tower, mm_nt(query, key), mask)
            grad = mixed_grad[:, h * HEAD : (h + 1) * HEAD]
            weight_grad = mm_nt(grad, value)
            grads[2].append(mm_tn(weights.astype(LOW), grad))
            score_grad = weights * (weight_grad - row_sum(weight_grad * weights))
            score_grad = score_grad.astype(LOW)
            grads[0].append(mm(score_grad, key) * HEAD ** (-0.5))
            grads[1].append(mm_tn(score_grad, query) * HEAD ** (-0.5))
        joined = jnp.concatenate([part for kind in grads for part in kind], axis=1)
        tower.bias_grad[...] = tower.bias_grad[...] + col_sum(joined)
        low = joined.astype(LOW)
        tower.qkv[at, :] = low
        tower.parts0[at, :] = out_of_heads(tower, low)

    def outer_attention(tower):
        heads = tower.across_heads
        put(tower, "outward", mm_tn(tower.mixed[...], tower.low_grad[...]))
        for k in range(3):
            grads = tower.qkv[:, k * heads : (k + 1) * heads]
            if tower is image:
                put(tower, "inward", mm_tn(grads, tower.normed[...]), k * heads)
            else:
                part = mm_tn(tower.normed[...], grads)
                start, rows, _ = places[tower.index, "inward"]
                high = tower.wide // 2
                for side in range(2):
                    summed[start + k * high : start + (k + 1) * high, side * heads : (side + 1) * heads] = (
                        part[side * high : (side + 1) * high]
                    )

    second_norm_back(text, scatters[2][1], gathers[1][1])
    attend_back(text, own_mp)
    until(11)
    outer(image, "expand", image.normed_two, image.slope)
    until(13)
    second_norm_back(image, scatters[2][0], gathers[1][0])
    gathers[1][1].got_core()
    attend_back(text, core_mp)
    scatters[3][1].near.start()
    until(14)
    attend_back(image, own_mp)
    until(15)
    gathers[1][0].got_core()
    attend_back(image, core_mp)
    scatters[3][0].near.start()
    until(16)
    gathers[1][1].got_across()
    attend_back(text, across_mp)
    until(17)
    gathers[1][1].got_diag()
    attend_back(text, diag_mp)
    scatters[3][1].far.start()
    until(18)
    gathers[1][1].sent()
    scatters[3][1].send_over()
    gathers[1][0].got_across()
    attend_back(image, across_mp)
    until(19)
    gathers[1][0].got_diag()
    attend_back(image, diag_mp)
    scatters[3][0].far.start()
    until(21)
    gathers[1][0].sent()
    scatters[3][0].send_over()
    for scatter in scatters[1]:
        scatter.far.start()
        scatter.near.start()
    outer_attention(text)
    until(22)
    outer_attention(image)
    until(23)

    def first_norm_back(tower, scatter, gather):
        normed_grad = scatter.result()
        white, scale = whitened(tower.own_tokens[...].astype(FULL))
        vectors = tower.mixed_vectors
        vectors[own_mp, 0:1, :] = col_sum(normed_grad * white)
        vectors[own_mp, 1:2, :] = col_sum(normed_grad)
        more = whitened_back(white, scale, tower.norms[0:1, :], normed_grad)
        put_back(tower, get_back(tower) + more)
        gather.start()
        store = pltpu.make_async_copy(
            tower.back, tower.token_place(own_mp), r.store_sems.at[2 + tower.index]
        )
        store.start()
        return store

    token_stores = [first_norm_back(text, scatters[3][1], gathers[2][1])]
    until(26)
    token_stores.append(first_norm_back(image, scatters[3][0], gathers[2][0]))
    for scatter in scatters[1]:
        scatter.send_over()
    trades = []
    for tower in (image, text):
        vectors = tower.mixed_vectors
        for k, peer in enumerate((core, across, diag)):
            mine = vectors.at[own_mp]
            trades.append(remote(mine, mine, trade_sems, 3 * tower.index + k, peer))
            trades[-1].start()
    until(38)

    def result_rows(tower, scatter, gather):
        values = tower.resid[...] + scatter.result() + tower.shifts[1:2, :]
        place = lax.broadcasted_iota(jnp.int32, (tower.rows, 1), 0)
        alive = live(tower, own_mp, place)
        if alive is not None:
            values = jnp.where(alive, values, 0.0)
        tower.carried[tower.at(own_mp), :] = values.astype(LOW).astype(FULL)
        gather.start()

    result_rows(text, scatters[1][1], gathers[3][1])
    result_rows(image, scatters[1][0], gathers[3][0])
    until(40)
    for gather in gathers[2]:
        gather.got_core()
        gather.got_across()
    until(42)
    for trade in trades:
        trade.wait()
    vec_start = places[0, "vectors"][0]
    left = summed.shape[0] - vec_start
    summed[vec_start:, :] = jnp.zeros((left, LANES), FULL)
    for tower in (image, text):
        vectors = tower.mixed_vectors
        sums = vectors[0] + vectors[1] + vectors[2] + vectors[3]
        vectors[own_mp] = sums
        heads = tower.across_heads
        vectors[own_mp, 6:7, :] = tower.offset_grad[...]
        vectors[own_mp, 7:8, 0:heads] = tower.bias_grad[:, 0:heads]
        vectors[own_mp, 7:8, heads : 2 * heads] = tower.bias_grad[:, 2 * heads : 3 * heads]
        put(tower, "vectors", vectors[own_mp])
    until(49)
    gathers[3][1].got_core()
    gathers[3][1].got_across()
    gathers[3][0].got_core()
    gathers[3][0].got_across()
    until(51)
    result_stores = []
    for tower in (text, image):
        gathers[3][tower.index].got_diag()
        for owner in range(4):
            at = tower.at(owner)
            values = tower.carried[at, :]
            if tower is text:
                tower.tokens[at, :] = values.astype(LOW)
            else:
                for k in range(2):
                    part = values[k * tower.per : (k + 1) * tower.per]
                    blank = jnp.zeros((tower.tokens.shape[1] - tower.per, tower.wide), FULL)
                    tower.tokens[2 * owner + k] = jnp.concatenate([part, blank], axis=0).astype(LOW)
        result_stores.append(
            pltpu.make_async_copy(tower.tokens, tower.result, r.store_sems.at[5 + tower.index])
        )
        result_stores[-1].start()
    until(ticks)
    for gather in gathers[2]:
        gather.got_diag()
    for gather in gathers[2] + gathers[3]:
        gather.sent()
    for copy in token_stores + result_stores + [blank_store]:
        copy.wait()
    out_copy.wait()


LOADED = ("tokens", "inward", "outward", "expand", "contract", "embed")
FAR = "_far"


def block_call(count, towers, post_norms, logit_scale, scalars, collective_id):
    names, args, in_specs = [], [], []
    outs, out_names, out_specs = [], [], []
    scratch, scratch_names = [], []
    vmem, smem, anywhere = pltpu.VMEM, pltpu.SMEM, pl.ANY

    def give(index, space, **named):
        for name, value in named.items():
            names.append((index, name))
            args.append(value)
            in_specs.append(pl.BlockSpec(memory_space=space))

    def take(index, space, kind=FULL, **named):
        for name, shape in named.items():
            out_names.append((index, name))
            outs.append(jax.ShapeDtypeStruct(shape, kind))
            out_specs.append(pl.BlockSpec(memory_space=space))

    def hold(index, **named):
        for name, what in named.items():
            scratch_names.append((index, name))
            scratch.append(what)

    examples = 8 * count
    sizes = []
    for index, tower in enumerate(towers):
        give(index, anywhere, cotangent_far=tower["cotangent"])
        for name in LOADED:
            give(index, anywhere, **{name + FAR: tower[name]})
            hold(index, **{name: vmem(tower[name].shape, LOW)})
        for name in ("norms", "biases", "shifts", "offsets"):
            give(index, vmem, **{name: tower[name]})
        rows, wide, spaces = 8 * IMG_ROWS, tower["tokens"].shape[-1], tower["tokens"].shape
        if index:
            rows, spaces = 8 * TXT_ROWS, (8, TXT_ROWS, wide)
        heads, hidden, quarter = tower["biases"].shape[1], tower["offsets"].size, rows // 4
        size = Fields()
        size.index, size.wide, size.across_heads, size.hidden = index, wide, heads, hidden
        sizes.append(size)
        take(index, anywhere, token_grad=spaces, embed_grad=tower["embed"].shape)
        take(index, anywhere, LOW, result=tower["tokens"].shape)
        hold(
            index,
            joined=vmem((wide, 3 * heads), LOW),
            normed=vmem((rows, wide), LOW),
            qkv=vmem((rows, 3 * heads), LOW),
            mixed=vmem((rows, heads), LOW),
            normed_two=vmem((rows, wide), LOW),
            active=vmem((rows, hidden), LOW),
            slope=vmem((rows, hidden), LOW),
            bias_row=vmem((1, 3 * heads), FULL),
            offset_row=vmem((1, hidden), FULL),
            resid=vmem((quarter, wide), FULL),
            carried=vmem((rows, wide), FULL),
            back=vmem((2, quarter // 2, wide), FULL),
            own_tokens=vmem((quarter, wide), LOW),
            low_grad=vmem((rows, wide), LOW),
            parts0=vmem((rows, wide), FULL),
            near0=vmem((2, quarter, wide), FULL),
            over0=vmem((quarter, wide), FULL),
            parts1=vmem((rows, wide), FULL),
            near1=vmem((2, quarter, wide), FULL),
            over1=vmem((quarter, wide), FULL),
            top=vmem((8, 1, wide), FULL),
            every_row=vmem((examples, wide), FULL),
            early=vmem((8, wide), FULL),
            first=vmem((4, 8, wide), FULL),
            second=vmem((4, 8, wide), FULL),
            offset_grad=vmem((1, hidden), FULL),
            bias_grad=vmem((1, 3 * heads), FULL),
            mixed_vectors=vmem((4, 8, wide), FULL),
        )
    _, held = gradient_rows(sizes)
    held += -held % SPAN
    give(2, vmem, post_norms=post_norms, logit_scale=logit_scale)
    give(2, smem, **scalars)
    take(2, anywhere, summed_far=(held, LANES))
    take(2, vmem, loss=(1, 1), hits=(1, 1), scale_grad=(1, 1), post_grad=post_norms.shape)
    wide = sizes[0].wide
    dma = pltpu.SemaphoreType.DMA
    rings = dp_rings()
    hold(
        2,
        summed=vmem((held, LANES), FULL),
        marks=vmem((examples, 128), FULL),
        every=vmem((4, count, 4, wide), FULL),
        load_sems=dma((2 * len(LOADED) + 2,)),
        store_sems=dma((8,)),
        blank=vmem((8, towers[0]["tokens"].shape[1] - IMG_ROWS, wide), FULL),
        scatter_send=dma((24,)),
        scatter_recv=dma((24,)),
        gather_send=dma((24,)),
        gather_recv=dma((24,)),
        swap_send=dma((15,)),
        swap_recv=dma((15,)),
        spread_send=dma((count,)),
        spread_recv=dma((count,)),
        trade_send=dma((6,)),
        trade_recv=dma((6,)),
        ring0=rings[0],
        ring1=rings[1],
        ring2=rings[2],
        ring3=rings[3],
        ring4=rings[4],
        ring5=rings[5],
        dp_send=rings[6],
        dp_recv=rings[7],
        dp_credit=rings[8],
    )
    results = pl.pallas_call(
        functools.partial(block_kernel, count, names + out_names + scratch_names),
        out_shape=outs,
        in_specs=in_specs,
        out_specs=out_specs,
        scratch_shapes=scratch,
        compiler_params=pltpu.CompilerParams(
            collective_id=collective_id, has_side_effects=True, vmem_limit_bytes=64 << 20
        ),
        name="block",
    )(*args)
    out = [Fields(), Fields(), Fields()]
    for (index, name), value in zip(out_names, results):
        setattr(out[index], name, value)
    return out, sizes


def finish_kernel(where, names, *refs):
    r = Fields()
    for name, ref in zip(names, refs):
        setattr(r, name, ref)
    copies = []

    def move(source, target):
        copies.append(pltpu.make_async_copy(source, target, r.sems.at[len(copies)]))
        copies[-1].start()

    def load(source, target):
        move(source, target)
        return copies[-1]

    def load_weight(index, name):
        start, rows, width = where[index, name]
        at = pl.ds(start, rows * (width // LANES))
        return load(r.summed.at[at], r.held.at[at])

    kinds, wide, heads = r.inward_t.shape
    high = wide // 2
    start, _, _ = where[0, "vectors"]
    vectors = load(r.summed.at[start : start + 40], r.vectors)
    rows_loaded = load(r.token_grad_t, r.text_rows)
    low_loaded = load(r.result_t, r.text_low)
    weights = [
        (index, name, load_weight(index, name), target)
        for index, name, target in (
            (0, "contract", r.contract_i),
            (0, "expand", r.expand_i),
            (0, "inward", r.inward_i),
            (0, "outward", r.outward_i),
            (1, "contract", r.contract_t),
            (1, "expand", r.expand_t),
            (1, "inward", None),
            (1, "outward", r.outward_t),
        )
    ]
    others = [
        (load(source, held), held, target)
        for source, held, target in (
            (r.token_grad_i, r.held_tokens, r.tokens_i),
            (r.embed_grad_i, r.held_embed_i, r.embed_i),
            (r.embed_grad_t, r.held_embed_t, r.embed_t),
            (r.result_i, r.held_result, r.image_result),
        )
    ]
    first = len(copies)
    for index, name, loaded, target in weights:
        loaded.wait()
        start, rows, width = where[index, name]
        if target is not None:
            for k in range(width // LANES):
                source = r.held.at[start + k * rows : start + (k + 1) * rows]
                move(source, target.at[:, k * LANES : (k + 1) * LANES])
            continue
        for k in range(kinds):
            for side in range(2):
                source = r.held.at[
                    start + k * high : start + (k + 1) * high, side * heads : (side + 1) * heads
                ]
                move(source, r.inward_t.at[k, side * high : (side + 1) * high])
    for loaded, held, target in others:
        loaded.wait()
        move(held, target)
    for loaded in (vectors, rows_loaded, low_loaded):
        loaded.wait()
    context, examples, _ = r.tokens_t.shape
    for e in range(examples):
        r.tokens_t[:, e, :] = r.text_rows[e][0:context]
        r.text_turned[:, e, :] = r.text_low[e * TXT_ROWS : (e + 1) * TXT_ROWS].astype(FULL)[0:context]
    r.text_result[...] = r.text_turned[...].astype(LOW)
    at = 0
    for norms, shifts, offsets, biases in (
        (r.norms_i, r.shifts_i, r.offsets_i, r.biases_i),
        (r.norms_t, r.shifts_t, r.offsets_t, r.biases_t),
    ):
        count = norms.shape[1] // LANES
        rows = jnp.concatenate([r.vectors[at + 8 * k : at + 8 * k + 8, :] for k in range(count)], axis=1)
        at += 8 * count
        norms[...] = rows[0:4]
        shifts[...] = rows[4:6]
        offsets[...] = jnp.concatenate(
            [rows[6:7, k * 128 : (k + 1) * 128] for k in range(offsets.shape[0])], axis=0
        )
        heads = biases.shape[1]
        biases[...] = jnp.concatenate([rows[7:8, 0:heads], rows[7:8, heads : 2 * heads]], axis=0)
    for copy in copies[first:]:
        copy.wait()


def finish_call(out, where, shapes, context, biases_i, biases_t):
    names, outs, out_specs = [], [], []
    given = dict(
        summed=out[2].summed_far,
        token_grad_i=out[0].token_grad,
        token_grad_t=out[1].token_grad,
        result_i=out[0].result,
        result_t=out[1].result,
        embed_grad_i=out[0].embed_grad,
        embed_grad_t=out[1].embed_grad,
    )

    def take(space, kind=FULL, **named):
        for name, shape in named.items():
            names.append(name)
            outs.append(jax.ShapeDtypeStruct(shape, kind))
            out_specs.append(pl.BlockSpec(memory_space=space))

    for name, shape in shapes.items():
        take(pl.ANY, **{name: shape})
    examples, patch, wide_i = out[0].token_grad.shape
    wide_t = out[1].token_grad.shape[2]
    take(pl.ANY, LOW, image_result=(examples, patch, wide_i))
    take(pltpu.VMEM, LOW, text_result=(context, examples, wide_t))
    take(pltpu.VMEM, tokens_t=(context, examples, wide_t))
    for name, shape in dict(norms=4, shifts=2).items():
        take(pltpu.VMEM, **{name + "_i": (shape, wide_i), name + "_t": (shape, wide_t)})
    take(pltpu.VMEM, offsets_i=(shapes["expand_i"][1] // 128, 128))
    take(pltpu.VMEM, offsets_t=(shapes["expand_t"][1] // 128, 128))
    take(pltpu.VMEM, biases_i=biases_i, biases_t=biases_t)
    scratch = dict(
        vectors=pltpu.VMEM((40, LANES), FULL),
        text_rows=pltpu.VMEM(out[1].token_grad.shape, FULL),
        text_low=pltpu.VMEM(out[1].result.shape, LOW),
        text_turned=pltpu.VMEM((context, examples, wide_t), FULL),
        held=pltpu.VMEM(out[2].summed_far.shape, FULL),
        held_tokens=pltpu.VMEM(out[0].token_grad.shape, FULL),
        held_embed_i=pltpu.VMEM(out[0].embed_grad.shape, FULL),
        held_embed_t=pltpu.VMEM(out[1].embed_grad.shape, FULL),
        held_result=pltpu.VMEM(out[0].result.shape, LOW),
        sems=pltpu.SemaphoreType.DMA((64,)),
    )
    results = pl.pallas_call(
        functools.partial(finish_kernel, where, list(given) + names + list(scratch)),
        out_shape=outs,
        in_specs=[pl.BlockSpec(memory_space=pl.ANY)] * len(given),
        out_specs=out_specs,
        scratch_shapes=list(scratch.values()),
        compiler_params=pltpu.CompilerParams(vmem_limit_bytes=62 << 20),
        name="finish",
    )(*given.values())
    fields = Fields()
    for name, value in zip(names, results):
        setattr(fields, name, value)
    return fields


def shards(
    count,
    image_tokens,
    image_norms,
    image_inward,
    image_biases,
    image_outward,
    image_shifts,
    image_expand,
    image_offsets,
    image_contract,
    image_embed,
    text_tokens,
    text_norms,
    text_inward,
    text_biases,
    text_outward,
    text_shifts,
    text_expand,
    text_offsets,
    text_contract,
    text_embed,
    post_norms,
    logit_scale,
    image_cotangent,
    text_cotangent,
    resolution,
    validity,
    text_ends,
):
    examples, patch, image_width = image_tokens.shape
    context, text_width = text_tokens.shape[1:]

    def fit(values):
        grow = ((0, 0), (0, TXT_ROWS - context), (0, 0))
        return jnp.pad(values, grow).reshape(-1, values.shape[2])

    image = dict(
        tokens=image_tokens,
        inward=jnp.swapaxes(image_inward, 1, 2),
        outward=image_outward,
        expand=image_expand,
        contract=image_contract,
        embed=image_embed,
        cotangent=image_cotangent,
        norms=image_norms,
        biases=image_biases,
        shifts=image_shifts,
        offsets=image_offsets.reshape(-1, 128),
    )
    text = dict(
        tokens=fit(text_tokens),
        inward=text_inward,
        outward=text_outward,
        expand=text_expand,
        contract=text_contract,
        embed=text_embed,
        cotangent=fit(text_cotangent),
        norms=text_norms,
        biases=text_biases,
        shifts=text_shifts,
        offsets=text_offsets.reshape(-1, 128),
    )
    scalars = dict(resolution=resolution, validity=validity, ends=text_ends)
    out, sizes = block_call(
        count, (image, text), post_norms, logit_scale.reshape(1, 1), scalars, 0
    )
    where, _ = gradient_rows(sizes)
    shapes = dict(
        contract_i=image_contract.shape,
        expand_i=image_expand.shape,
        outward_i=image_outward.shape,
        inward_i=(image_inward.shape[0] * image_inward.shape[2], image_width),
        embed_i=image_embed.shape,
        tokens_i=image_tokens.shape,
        contract_t=text_contract.shape,
        expand_t=text_expand.shape,
        outward_t=text_outward.shape,
        inward_t=text_inward.shape,
        embed_t=text_embed.shape,
    )
    end = finish_call(out, where, shapes, context, image_biases.shape, text_biases.shape)
    inward_i = end.inward_i.reshape(image_inward.shape[0], -1, image_width)
    return (
        end.image_result,
        jnp.swapaxes(end.text_result, 0, 1),
        out[2].loss.reshape(1),
        out[2].hits.reshape(1),
        end.tokens_i,
        jnp.swapaxes(end.tokens_t, 0, 1),
        end.norms_i,
        jnp.swapaxes(inward_i, 1, 2),
        end.biases_i,
        end.outward_i,
        end.shifts_i,
        end.expand_i,
        end.offsets_i.reshape(-1),
        end.contract_i,
        end.embed_i,
        end.norms_t,
        end.inward_t,
        end.biases_t,
        end.outward_t,
        end.shifts_t,
        end.expand_t,
        end.offsets_t.reshape(-1),
        end.contract_t,
        end.embed_t,
        out[2].post_grad,
        out[2].scale_grad.reshape(1),
    )


def solution(mesh):
    placed = (
        P("dp", None, None),
        P(),
        P(None, None, "mp"),
        P(None, "mp"),
        P("mp", None),
        P(),
        P(None, "mp"),
        P("mp"),
        P("mp", None),
        P(),
        P("dp", None, None),
        P(),
        P(None, None, "mp"),
        P(None, "mp"),
        P("mp", None),
        P(),
        P(None, "mp"),
        P("mp"),
        P("mp", None),
        P(),
        P(),
        P(),
        P("dp", None, None),
        P("dp", None, None),
        P("dp"),
        P("dp"),
        P("dp"),
    )
    return jax.shard_map(
        functools.partial(shards, mesh.shape["dp"]),
        mesh=mesh,
        in_specs=placed,
        out_specs=(
            P("dp", None, None),
            P("dp", None, None),
            P(),
            P(),
            P("dp", None, None),
            P("dp", None, None),
            P(),
            P(None, None, "mp"),
            P(None, "mp"),
            P("mp", None),
            P(),
            P(None, "mp"),
            P("mp"),
            P("mp", None),
            P(),
            P(),
            P(None, None, "mp"),
            P(None, "mp"),
            P("mp", None),
            P(),
            P(None, "mp"),
            P("mp"),
            P("mp", None),
            P(),
            P(),
            P(),
        ),
        check_vma=False,
    )
```
